256 devices in a mesh: dp: 16 (over y, x), group: 16 (over z, core).
Axes of the slice: x: 4, y: 4, z: 8, core: 2. Of those that a mesh axis runs over, the one named last changes fastest.
Arguments:
- layer_input: bfloat16 [65536, 1280], P(('dp', 'group')), may hold values from -6 to 6
- grad_packed: bfloat16 [65536, 1280], P(('dp', 'group')), may hold values from -6 to 6
- source_row: int32 [16, 4096], P('dp'), may hold values from 0 to 4095, each once within a row
- window_id: int32 [16, 4096], P('dp'), may hold values from 0 to 4095, as said below
- w_qkv: bfloat16 [3, 1280, 1280], P(None, None, 'group'), may hold values from -1 to 1
- gain: float32 [1280], replicated, may hold values from 0.25 to 1.75
Outputs:
- grad_input: bfloat16 [65536, 1280], P(('dp', 'group'))
- grad_weight: float32 [3, 1280, 1280], P(None, None, 'group')
- grad_gain: float32 [1280], replicated
The draws below stay inside these ranges and needn't reach their ends.
Inputs may be any that keep to these rules, and one draw needn't show every extreme that they name: `source_row`: each batch's row is named once. `window_id`: window numbers never decrease along a batch's rows; each window is a run of consecutive rows inside one aligned block of 64 rows; the last window of every batch is numbered 4096 - 1.
All inputs are finite; a program needn't handle non-finite values.
Results may differ from the reference program's by a relative error of at most 0.018.
Values may be sent and summed in bfloat16 or wider, within the bound.
No kernel may reach another device: no remote copies, remote signals or barrier semaphores. Data moves between devices by JAX's collectives and lax.ppermute only.
A program may use at most 128 MiB of HBM per device.

```python
import jax
import jax.numpy as jnp
from jax import lax

D = 1280
HEAD = 80
WIN = 64
GROUP_ROWS = 4096
ROWS = 65536
N_DP = 16


def draw_window_id(key, part):
    key = jax.random.fold_in(key, 7)
    marks = jax.random.randint(key, (N_DP, GROUP_ROWS // WIN, WIN), 0, 4)
    position = jnp.arange(WIN, dtype=jnp.int32)[None, None, :]
    breaks = jnp.where(position > 0, (marks == 0).astype(jnp.int32), 0)
    within = jnp.cumsum(breaks, axis=2).astype(jnp.int32)
    total = jnp.sum(breaks, axis=2, keepdims=True).astype(jnp.int32)
    block_index = jnp.arange(GROUP_ROWS // WIN, dtype=jnp.int32)[None, :, None]
    labels = block_index * WIN + (WIN - 1) - (total - within)
    return labels.reshape(N_DP, GROUP_ROWS).astype(jnp.int32)


def draw_layer_input(key, part):
    key = jax.random.fold_in(key, 11)
    noise_key = jax.random.fold_in(key, 0)
    noise = jax.random.normal(noise_key, (ROWS, D), jnp.float32)
    values = noise
    return jnp.clip(values, -6.0, 6.0).astype(jnp.bfloat16)


def draw_w_qkv(key, part):
    key = jax.random.fold_in(key, 13)
    noise_key = jax.random.fold_in(key, 0)
    base = jnp.clip(jax.random.normal(noise_key, (3, D, D), jnp.float32), -6.0, 6.0) * D ** (-0.5)
    return base.astype(jnp.bfloat16)


def levels(key, dims, shards, smallest, top_value):
    level, own = 1.0, jax.random.fold_in(key, 6)
    for axis_at, shards_of in shards:
        draws = jnp.exp(jax.random.uniform(jax.random.fold_in(own, axis_at), (shards_of,), jnp.float32, smallest / len(shards), top_value / len(shards)))
        level = level * jnp.repeat(draws, dims[axis_at] // shards_of).reshape([-1 if axis == axis_at else 1 for axis in range(len(dims))])
    return level


def normal_values(own_key, dims, width, bound, pieces=(), held_as=jnp.bfloat16):
    factor_of = levels(own_key, dims, pieces, -0.22, 0.18) if pieces else 1.0
    values = jax.random.normal(own_key, dims, jnp.float32) * width * factor_of
    return jnp.minimum(jnp.maximum(values, -bound), bound).astype(held_as)


def setup_inputs(seed: int = 0) -> dict:
    streams_of = jax.random.split(jax.random.key(seed), 7)
    return {
        "layer_input": draw_layer_input(jax.random.fold_in(streams_of[6], 71), 0),
        "grad_packed": normal_values(streams_of[1], (ROWS, D), 1.0, 6.0, ((0, 256),)),
        "source_row": jax.vmap(lambda own: jax.random.permutation(own, GROUP_ROWS))(jax.random.split(streams_of[2], N_DP)).reshape((N_DP, GROUP_ROWS)).astype(jnp.int32),
        "window_id": draw_window_id(jax.random.fold_in(streams_of[6], 71), 0),
        "w_qkv": draw_w_qkv(jax.random.fold_in(streams_of[6], 71), 0),
        "gain": jnp.clip(1.0 + 0.15 * jax.random.normal(streams_of[5], (D,), jnp.float32), 0.25, 1.75),
    }


epsilon = 1e-06

def normalize(rows_in, gain):
    values = rows_in.astype(jnp.float32)
    inverse = lax.rsqrt(lax.optimization_barrier(jnp.mean(values * values, axis=-1, keepdims=True)) + epsilon)
    scaled = values * inverse
    normed = (scaled * gain).astype(jnp.bfloat16)
    return (scaled, inverse, normed)

def to_low(values):
    rounded = values.astype(jnp.bfloat16)
    rounded = lax.optimization_barrier(rounded)
    return rounded.astype(jnp.float32)

def attention_grad(stacked, grad_out, windows):
    total_rows = stacked.shape[1]
    blocks = total_rows // WIN
    local_heads = stacked.shape[2] // HEAD
    shaped = stacked.astype(jnp.float32).reshape(3, blocks, WIN, local_heads, HEAD)
    query, keys, values = (shaped[0], shaped[1], shaped[2])
    upstream = grad_out.astype(jnp.float32).reshape(blocks, WIN, local_heads, HEAD)
    labels = windows.reshape(blocks, WIN)
    same_window = labels[:, :, None] == labels[:, None, :]
    scaling = HEAD ** (-0.5)
    scores = jnp.einsum('bqhe,bkhe->bhqk', query, keys) * scaling
    scores = jnp.where(same_window[:, None], scores, -1e+30)
    probs = jax.nn.softmax(scores, axis=-1)
    grad_probs = jnp.einsum('bqhe,bkhe->bhqk', upstream, values)
    row_dot = lax.optimization_barrier(jnp.sum(probs * grad_probs, axis=-1, keepdims=True))
    grad_scores = to_low(probs * (grad_probs - row_dot))
    probs_low = to_low(probs)
    grad_values = jnp.einsum('bhqk,bqhe->bkhe', probs_low, upstream)
    grad_query = jnp.einsum('bhqk,bkhe->bqhe', grad_scores, keys) * scaling
    grad_keys = jnp.einsum('bhqk,bqhe->bkhe', grad_scores, query) * scaling
    joined = jnp.stack([grad_query, grad_keys, grad_values])
    return joined.reshape(3, total_rows, local_heads * HEAD).astype(jnp.bfloat16)

def reference(layer_input, grad_packed, source_row, window_id, w_qkv, gain):
    weights = w_qkv.astype(jnp.float32)

    def batch_step(sums_so_far, batch_items):
        rows_in, packed, sources, windows = batch_items
        scaled, inverse, normed = normalize(rows_in, gain)
        normed_wide = normed.astype(jnp.float32)
        projected = jnp.einsum('rd,jde->jre', normed_wide, weights).astype(jnp.bfloat16)
        grad_out = jnp.take(packed, sources, axis=0)
        grad_qkv = attention_grad(projected, grad_out, windows)
        grad_wide = grad_qkv.astype(jnp.float32)
        weight_part = jnp.einsum('rd,jre->jde', normed_wide, grad_wide)
        grad_normed = jnp.einsum('jre,jde->rd', grad_wide, weights)
        grad_scaled = grad_normed * gain
        mixed = lax.optimization_barrier(jnp.mean(grad_scaled * scaled, axis=-1, keepdims=True))
        grad_rows = (inverse * (grad_scaled - scaled * mixed)).astype(jnp.bfloat16)
        gain_part = lax.optimization_barrier(jnp.sum(grad_normed * scaled, axis=0))
        return ((sums_so_far[0] + weight_part, sums_so_far[1] + gain_part), grad_rows)
    start_sums = (jnp.zeros((3, D, D), jnp.float32), jnp.zeros((D,), jnp.float32))
    batched = (layer_input.reshape(N_DP, GROUP_ROWS, D), grad_packed.reshape(N_DP, GROUP_ROWS, D), source_row, window_id)
    (grad_weight, grad_gain), grad_rows = lax.scan(batch_step, start_sums, batched)
    return (grad_rows.reshape(ROWS, D), grad_weight, grad_gain)
```

```python
import functools

import jax
import jax.numpy as jnp
from jax import lax
from jax.experimental import pallas as pl
from jax.experimental.pallas import tpu as pltpu
from jax.sharding import Mesh, PartitionSpec as P

HEAD = 80
HEADS = 16
SUPER = 128
CHUNK = 256
SLOTS = 4
RING = 4
LINES = 160
PADDED = 256
XOR_ORDER = (0, 2, 1, 3)
epsilon = 1e-06
bf16 = jnp.bfloat16
f32 = jnp.float32
NT = (((1,), (1,)), ((), ()))
TN = (((0,), (0,)), ((), ()))
NN = (((1,), (0,)), ((), ()))
BIG = 56 * 1024 * 1024


def dot(a, b, dims):
    return lax.dot_general(a, b, dims, preferred_element_type=f32)


def lanes(shape):
    return lax.broadcasted_iota(jnp.int32, shape, len(shape) - 1)


def roll(x, shift):
    shift = shift % x.shape[-1]
    return x if shift == 0 else pltpu.roll(x, shift, x.ndim - 1)


def pack(rows):
    top = jnp.where(lanes((128, 128)) < 64, rows[:128], roll(rows[128:], 64))
    group = lanes((32, 128)) // 16
    low = roll(rows[:32], -64)
    for k in range(1, 8):
        low = jnp.where(group == k, roll(rows[32 * k : 32 * k + 32], 16 * k - 64), low)
    return top, low


def unpack(top, low, place):
    at = lanes((128, 128))
    upper = roll(top, place)
    lower = roll(top, place - 64)
    tail = [roll(low, place + 64 - 16 * k) for k in range(8)]
    first = jnp.concatenate(tail[:4], axis=0)
    second = jnp.concatenate(tail[4:], axis=0)
    wide = (at >= place) & (at < place + 64)
    rest = (at >= place + 64) & (at < place + HEAD)
    one = jnp.where(wide, upper, jnp.where(rest, first, 0.0))
    two = jnp.where(wide, lower, jnp.where(rest, second, 0.0))
    return one, two


def pack_kernel(rows_ref, out_ref):
    for g in range(HEADS):
        start = (HEAD * g) // 128 * 128
        shift = HEAD * g - start
        size = 128 if shift + HEAD <= 128 else 256
        window = rows_ref[:, start : start + size].astype(f32)
        window = roll(window, -shift)[:, :128]
        top, low = pack(window)
        out_ref[g, :128, :] = top.astype(bf16)
        out_ref[g, 128:, :] = low.astype(bf16)


def permute_kernel(place_ref, source_ref, in_ref, out_ref, table, picked):
    slot = place_ref[1]
    for src in range(HEADS):
        one, two = unpack(
            in_ref[src, :128, :].astype(f32), in_ref[src, 128:, :].astype(f32), 0
        )
        table[CHUNK * src : CHUNK * src + 128, :] = one
        table[CHUNK * src + 128 : CHUNK * src + 256, :] = two
    for q in range(RING):
        for o, off in enumerate(XOR_ORDER):
            base = q * SLOTS * CHUNK + (slot ^ off) * CHUNK

            def step(i, carry):
                at = i * 16
                for u in range(16):
                    row = source_ref[base + at + u]
                    picked[pl.ds(at + u, 1), :] = table[pl.ds(row, 1), :]
                return carry

            lax.fori_loop(0, CHUNK // 16, step, 0)
            top, low = pack(picked[...])
            out_ref[q, o, :128, :] = top.astype(bf16)
            out_ref[q, o, 128:, :] = low.astype(bf16)


def norm_kernel(rows_ref, gain_ref, out_ref):
    values = rows_ref[...].astype(f32)
    inverse = lax.rsqrt(jnp.mean(values * values, axis=-1, keepdims=True) + epsilon)
    out_ref[...] = (values * inverse * gain_ref[...]).astype(bf16)


def head_kernel(
    place_ref, normed_ref, w_ref, up_ref, window_ref, grad_ref, weight_ref, gain_ref,
    first, second, key_at, query_at, upstream,
):
    head = pl.program_id(0)
    ring, slot = place_ref[0], place_ref[1]
    scaling = HEAD ** (-0.5)
    w = w_ref[0]
    for c in range(SLOTS):
        rows = slice(CHUNK * c, CHUNK * c + CHUNK)
        all_three = dot(normed_ref[rows, :], w, NT)
        low = all_three.astype(bf16)
        first[rows, :] = low[:, :128]
        second[rows, :] = low[:, 128:]
        rounded = low.astype(f32)
        at = lanes((CHUNK, PADDED))
        moved = jnp.where(at < HEAD, roll(rounded, -HEAD), 0.0)
        key_at[rows, :] = moved[:, :128].astype(bf16)
        query_at[rows, :] = jnp.where(
            (at >= HEAD) & (at < 2 * HEAD), roll(rounded, HEAD), 0.0
        ).astype(bf16)
        one, two = unpack(
            up_ref[0, c, :128, :].astype(f32), up_ref[0, c, 128:, :].astype(f32), 32
        )
        upstream[CHUNK * c : CHUNK * c + 128, :] = one.astype(bf16)
        upstream[CHUNK * c + 128 : CHUNK * c + 256, :] = two.astype(bf16)
    for b in range(SLOTS * CHUNK // SUPER):
        rows = slice(SUPER * b, SUPER * b + SUPER)
        line = ring * 8 + (slot ^ XOR_ORDER[b // 2]) * 2 + b % 2
        labels = jnp.broadcast_to(window_ref[pl.ds(line, 1), :], (SUPER, SUPER))
        same = labels == labels.T
        keys = key_at[rows, :]
        up = upstream[rows, :]
        scores = dot(first[rows, :], keys, NT) * scaling
        scores = jnp.where(same, scores, -1e30)
        top = jnp.max(scores, axis=-1, keepdims=True)
        powers = jnp.exp(scores - top)
        probs = powers / jnp.sum(powers, axis=-1, keepdims=True)
        grad_probs = dot(up, second[rows, :], NT)
        row_dot = jnp.sum(probs * grad_probs, axis=-1, keepdims=True)
        grad_scores = (probs * (grad_probs - row_dot)).astype(bf16)
        grad_query = dot(grad_scores, keys, NN)
        grad_key = dot(grad_scores, query_at[rows, :], TN)
        grad_value = dot(probs.astype(bf16), up, TN)
        grad_ref[0, rows, :128] = ((grad_query + grad_key[:, :128]) * scaling).astype(bf16)
        grad_ref[0, rows, 128:] = (grad_key[:, 128:] * scaling + grad_value).astype(bf16)
    grads = grad_ref[0]
    for n in range(5):
        cols = slice(256 * n, 256 * n + 256)
        part = dot(grads, normed_ref[:, cols], TN)
        weight_ref[:, 0, :, cols] = part.astype(bf16).reshape(16, 16, 256)
        gained = jnp.sum(part * w[:, cols].astype(f32), axis=0, keepdims=True)

        @pl.when(head == 0)
        def _():
            gain_ref[:, cols] = gained

        @pl.when(head > 0)
        def _():
            gain_ref[:, cols] += gained


def back_kernel(grad_ref, w_ref, keep_ref, send_ref):
    for c in range(SLOTS):
        rows = slice(CHUNK * c, CHUNK * c + CHUNK)
        total = dot(grad_ref[0, rows, :], w_ref[0], NN)
        for h in range(1, RING):
            total += dot(grad_ref[h, rows, :], w_ref[h], NN)
        if c < 2:
            keep_ref[rows, :] = total
        else:
            send_ref[CHUNK * (c - 2) : CHUNK * (c - 1), :] = total.astype(bf16)


def final_kernel(rows_ref, gain_ref, keep_ref, core_ref, pair_ref, out_ref):
    values = rows_ref[...].astype(f32)
    inverse = lax.rsqrt(jnp.mean(values * values, axis=-1, keepdims=True) + epsilon)
    scaled = values * inverse
    normed_grad = keep_ref[...] + core_ref[...].astype(f32) + pair_ref[...].astype(f32)
    grad_scaled = normed_grad * gain_ref[...]
    mixed = jnp.mean(grad_scaled * scaled, axis=-1, keepdims=True)
    out_ref[...] = (inverse * (grad_scaled - scaled * mixed)).astype(bf16)


def vmem():
    return pl.BlockSpec(memory_space=pltpu.VMEM)


def smem():
    return pl.BlockSpec(memory_space=pltpu.SMEM)


def params():
    return pltpu.CompilerParams(vmem_limit_bytes=BIG)


def pack_call(rows):
    return pl.pallas_call(
        pack_kernel,
        out_shape=jax.ShapeDtypeStruct((HEADS, LINES, 128), bf16),
        in_specs=[vmem()],
        out_specs=vmem(),
        compiler_params=params(),
    )(rows)


def permute_call(place, source, received):
    return pl.pallas_call(
        permute_kernel,
        out_shape=jax.ShapeDtypeStruct((RING, SLOTS, LINES, 128), bf16),
        in_specs=[smem(), smem(), vmem()],
        out_specs=vmem(),
        scratch_shapes=[pltpu.VMEM((HEADS * CHUNK, 128), f32), pltpu.VMEM((CHUNK, 128), f32)],
        compiler_params=params(),
    )(place, source, received)


def norm_call(rows, gain):
    return pl.pallas_call(
        norm_kernel,
        out_shape=jax.ShapeDtypeStruct(rows.shape, bf16),
        in_specs=[vmem(), vmem()],
        out_specs=vmem(),
        compiler_params=params(),
    )(rows, gain)


def head_call(place, normed, weights, upstream, windows):
    rows, width = normed.shape
    return pl.pallas_call(
        head_kernel,
        grid=(RING,),
        out_shape=(
            jax.ShapeDtypeStruct((RING, rows, PADDED), bf16),
            jax.ShapeDtypeStruct((16, RING, 16, width), bf16),
            jax.ShapeDtypeStruct((1, width), f32),
        ),
        in_specs=[
            smem(),
            pl.BlockSpec((rows, width), lambda h: (0, 0)),
            pl.BlockSpec((1, PADDED, width), lambda h: (h, 0, 0)),
            pl.BlockSpec((1, SLOTS, LINES, 128), lambda h: (h, 0, 0, 0)),
            pl.BlockSpec((32, 128), lambda h: (0, 0)),
        ],
        out_specs=(
            pl.BlockSpec((1, rows, PADDED), lambda h: (h, 0, 0)),
            pl.BlockSpec((16, 1, 16, width), lambda h: (0, h, 0, 0)),
            pl.BlockSpec((1, width), lambda h: (0, 0)),
        ),
        scratch_shapes=[
            pltpu.VMEM((rows, 128), bf16),
            pltpu.VMEM((rows, 128), bf16),
            pltpu.VMEM((rows, 128), bf16),
            pltpu.VMEM((rows, PADDED), bf16),
            pltpu.VMEM((rows, 128), bf16),
        ],
        compiler_params=params(),
    )(place, normed, weights, upstream, windows)


def back_call(grads, weights):
    width = weights.shape[-1]
    return pl.pallas_call(
        back_kernel,
        out_shape=(
            jax.ShapeDtypeStruct((2 * CHUNK, width), f32),
            jax.ShapeDtypeStruct((2 * CHUNK, width), bf16),
        ),
        in_specs=[vmem(), vmem()],
        out_specs=(vmem(), vmem()),
        compiler_params=params(),
    )(grads, weights)


def final_call(rows, gain, keep, from_core, from_pair):
    return pl.pallas_call(
        final_kernel,
        out_shape=jax.ShapeDtypeStruct(rows.shape, bf16),
        in_specs=[vmem()] * 5,
        out_specs=vmem(),
        compiler_params=params(),
    )(rows, gain, keep, from_core, from_pair)


def swap(x, axis):
    return lax.ppermute(x, axis, [(0, 1), (1, 0)])


def on_device(layer_input, grad_packed, source_row, window_id, w_qkv, gain):
    width = layer_input.shape[1]
    dp = lax.axis_index("y") * 4 + lax.axis_index("x")
    ring = lax.axis_index("zq")
    slot = lax.axis_index("zp") * 2 + lax.axis_index("core")
    place = jnp.stack([ring, slot]).astype(jnp.int32)
    gain_row = gain.reshape(1, width)

    flipped = jnp.swapaxes(w_qkv, 1, 2).reshape(3 * HEAD, width)
    flipped = jnp.pad(flipped, ((0, PADDED - 3 * HEAD), (0, 0)))
    share = lax.dynamic_slice(flipped, (16 * dp, 0), (16, width))
    weights = lax.all_gather(share, ("zq", "y", "x"), axis=0, tiled=True)
    weights = weights.reshape(RING, PADDED, width)

    packed = pack_call(grad_packed)
    by_head = lax.all_to_all(packed, ("zq", "zp", "core"), split_axis=0, concat_axis=0)
    permuted = permute_call(place, source_row.reshape(-1), by_head)
    upstream = lax.all_to_all(permuted, "zq", split_axis=0, concat_axis=0)

    own = norm_call(layer_input, gain_row)
    half = jnp.concatenate([own, swap(own, "zp")], axis=0)
    normed = jnp.concatenate([half, swap(half, "core")], axis=0)

    windows = window_id.reshape(32, 128).astype(f32)
    grads, weight_part, gain_part = head_call(place, normed, weights, upstream, windows)

    arrived = lax.all_to_all(weight_part, ("y", "x"), split_axis=0, concat_axis=0)
    summed = jnp.sum(arrived.astype(f32), axis=0).astype(bf16)
    gain_part = gain_part + swap(gain_part, "core")
    gain_part = gain_part + swap(gain_part, "zp")
    beside = jnp.pad(gain_part.reshape(10, 128), ((0, 6), (0, 0))).astype(bf16)
    beside = jnp.broadcast_to(beside[None], (RING, 16, 128))
    message = jnp.concatenate([summed, beside], axis=2)
    arrived = lax.all_to_all(message, "zq", split_axis=0, concat_axis=0)
    summed = jnp.sum(arrived.astype(f32), axis=0).astype(bf16)
    copies = jnp.broadcast_to(summed[None], (16,) + summed.shape)
    whole = lax.all_to_all(copies, ("y", "x"), split_axis=0, concat_axis=0)
    gradient = whole[:, :, :width].reshape(PADDED, width)[: 3 * HEAD].astype(f32)
    grad_weight = jnp.swapaxes(gradient.reshape(3, HEAD, width), 1, 2)
    grad_gain = jnp.sum(whole[:, :10, width:].astype(f32), axis=0).reshape(width) / gain

    keep, send = back_call(grads, weights)
    from_core = swap(send, "core")
    pair = (keep[CHUNK:] + from_core[CHUNK:].astype(f32)).astype(bf16)
    from_pair = swap(pair, "zp")
    grad_input = final_call(layer_input, gain_row, keep[:CHUNK], from_core[:CHUNK], from_pair)
    return (grad_input, grad_weight, grad_gain)


def solution(mesh):
    fine = Mesh(mesh.devices.reshape(4, 4, 4, 2, 2), ("y", "x", "zq", "zp", "core"))
    dp, group = ("y", "x"), ("zq", "zp", "core")
    rows = P(dp + group, None)
    return jax.shard_map(
        on_device,
        mesh=fine,
        in_specs=(rows, rows, P(dp, None), P(dp, None), P(None, None, group), P()),
        out_specs=(rows, P(None, None, group), P()),
        check_vma=False,
    )
```

```python
import functools

import jax
import jax.numpy as jnp
from jax import lax
from jax.experimental import pallas as pl
from jax.experimental.pallas import tpu as pltpu
from jax.sharding import Mesh, PartitionSpec as P

HEAD = 80
HEADS = 16
SUPER = 128
CHUNK = 256
SLOTS = 4
RING = 4
LINES = 160
PADDED = 256
XOR_ORDER = (0, 2, 1, 3)
epsilon = 1e-06
bf16 = jnp.bfloat16
f32 = jnp.float32
NT = (((1,), (1,)), ((), ()))
TN = (((0,), (0,)), ((), ()))
NN = (((1,), (0,)), ((), ()))
BIG = 28 * 1024 * 1024


def dot(a, b, dims):
    return lax.dot_general(a, b, dims, preferred_element_type=f32)


def lanes(shape):
    return lax.broadcasted_iota(jnp.int32, shape, len(shape) - 1)


def roll(x, shift):
    shift = shift % x.shape[-1]
    return x if shift == 0 else pltpu.roll(x, shift, x.ndim - 1)


def pack(rows):
    top = jnp.where(lanes((128, 128)) < 64, rows[:128], roll(rows[128:], 64))
    group = lanes((32, 128)) // 16
    low = roll(rows[:32], -64)
    for k in range(1, 8):
        low = jnp.where(group == k, roll(rows[32 * k : 32 * k + 32], 16 * k - 64), low)
    return top, low


def unpack(top, low, place):
    at = lanes((128, 128))
    upper = roll(top, place)
    lower = roll(top, place - 64)
    tail = [roll(low, place + 64 - 16 * k) for k in range(8)]
    first = jnp.concatenate(tail[:4], axis=0)
    second = jnp.concatenate(tail[4:], axis=0)
    wide = (at >= place) & (at < place + 64)
    rest = (at >= place + 64) & (at < place + HEAD)
    one = jnp.where(wide, upper, jnp.where(rest, first, 0.0))
    two = jnp.where(wide, lower, jnp.where(rest, second, 0.0))
    return one, two


def pack_kernel(rows_ref, out_ref):
    for g in range(HEADS):
        start = (HEAD * g) // 128 * 128
        shift = HEAD * g - start
        size = 128 if shift + HEAD <= 128 else 256
        window = rows_ref[:, start : start + size].astype(f32)
        window = roll(window, -shift)[:, :128]
        top, low = pack(window)
        out_ref[g, :128, :] = top.astype(bf16)
        out_ref[g, 128:, :] = low.astype(bf16)


def permute_kernel(place_ref, source_ref, in_ref, out_ref, table, picked):
    slot = place_ref[1]
    for src in range(HEADS):
        one, two = unpack(
            in_ref[src, :128, :].astype(f32), in_ref[src, 128:, :].astype(f32), 0
        )
        table[CHUNK * src : CHUNK * src + 128, :] = one
        table[CHUNK * src + 128 : CHUNK * src + 256, :] = two
    for q in range(RING):
        for o, off in enumerate(XOR_ORDER):
            base = q * SLOTS * CHUNK + (slot ^ off) * CHUNK

            def step(i, carry):
                at = i * 16
                for u in range(16):
                    row = source_ref[base + at + u]
                    picked[pl.ds(at + u, 1), :] = table[pl.ds(row, 1), :]
                return carry

            lax.fori_loop(0, CHUNK // 16, step, 0)
            top, low = pack(picked[...])
            out_ref[q, o, :128, :] = top.astype(bf16)
            out_ref[q, o, 128:, :] = low.astype(bf16)


def norm_kernel(rows_ref, gain_ref, out_ref):
    values = rows_ref[...].astype(f32)
    inverse = lax.rsqrt(jnp.mean(values * values, axis=-1, keepdims=True) + epsilon)
    out_ref[...] = (values * inverse * gain_ref[...]).astype(bf16)


def head_kernel(
    place_ref, normed_ref, w_ref, up_ref, window_ref, grad_ref, weight_ref, gain_ref,
    first, second, key_at, query_at, upstream,
):
    head = pl.program_id(0)
    ring, slot = place_ref[0], place_ref[1]
    scaling = HEAD ** (-0.5)
    w = w_ref[:, 0].reshape(PADDED, w_ref.shape[-1])
    total_rows = SLOTS * CHUNK
    low = dot(normed_ref[...], w, NT).astype(bf16)
    first[...] = low[:, :128]
    second[...] = low[:, 128:]
    rounded = low.astype(f32)
    at = lanes((total_rows, PADDED))
    key_at[...] = jnp.where(at < HEAD, roll(rounded, -HEAD), 0.0)[:, :128].astype(bf16)
    query_at[...] = jnp.where(
        (at >= HEAD) & (at < 2 * HEAD), roll(rounded, HEAD), 0.0
    ).astype(bf16)
    for c in range(SLOTS):
        one, two = unpack(
            up_ref[0, c, :128, :].astype(f32), up_ref[0, c, 128:, :].astype(f32), 32
        )
        upstream[CHUNK * c : CHUNK * c + 128, :] = one.astype(bf16)
        upstream[CHUNK * c + 128 : CHUNK * c + 256, :] = two.astype(bf16)
    blocks = [slice(SUPER * b, SUPER * b + SUPER) for b in range(total_rows // SUPER)]
    scores = [dot(first[r, :], key_at[r, :], NT) for r in blocks]
    grad_probs = [dot(upstream[r, :], second[r, :], NT) for r in blocks]
    probs, grad_scores = [], []
    for b in range(len(blocks)):
        line = ring * 8 + (slot ^ XOR_ORDER[b // 2]) * 2 + b % 2
        labels = jnp.broadcast_to(window_ref[pl.ds(line, 1), :], (SUPER, SUPER))
        masked = jnp.where(labels == labels.T, scores[b] * scaling, -1e30)
        powers = jnp.exp(masked - jnp.max(masked, axis=-1, keepdims=True))
        prob = powers / jnp.sum(powers, axis=-1, keepdims=True)
        row_dot = jnp.sum(prob * grad_probs[b], axis=-1, keepdims=True)
        grad_scores.append((prob * (grad_probs[b] - row_dot)).astype(bf16))
        probs.append(prob.astype(bf16))
    for b, r in enumerate(blocks):
        grad_query = dot(grad_scores[b], key_at[r, :], NN)
        grad_key = dot(grad_scores[b], query_at[r, :], TN)
        grad_value = dot(probs[b], upstream[r, :], TN)
        grad_ref[r, :128] = ((grad_query + grad_key[:, :128]) * scaling).astype(bf16)
        grad_ref[r, 128:] = (grad_key[:, 128:] * scaling + grad_value).astype(bf16)
    part = dot(grad_ref[...], normed_ref[...], TN)
    weight_ref[:, 0] = part.astype(bf16).reshape(16, 16, part.shape[1])
    gained = jnp.sum(part * w.astype(f32), axis=0, keepdims=True)

    @pl.when(head == 0)
    def _():
        gain_ref[...] = gained

    @pl.when(head > 0)
    def _():
        gain_ref[...] += gained


def back_kernel(grad_ref, w_ref, keep_ref, send_ref):
    parts = [w_ref[:, h].reshape(PADDED, w_ref.shape[-1]) for h in range(RING)]
    total = dot(grad_ref[...], jnp.concatenate(parts, axis=0), NN)
    keep_ref[...] = total[: 2 * CHUNK]
    send_ref[...] = total[2 * CHUNK :].astype(bf16)


def final_kernel(rows_ref, gain_ref, keep_ref, core_ref, pair_ref, out_ref):
    values = rows_ref[...].astype(f32)
    inverse = lax.rsqrt(jnp.mean(values * values, axis=-1, keepdims=True) + epsilon)
    scaled = values * inverse
    normed_grad = keep_ref[...] + core_ref[...].astype(f32) + pair_ref[...].astype(f32)
    grad_scaled = normed_grad * gain_ref[...]
    mixed = jnp.mean(grad_scaled * scaled, axis=-1, keepdims=True)
    out_ref[...] = (inverse * (grad_scaled - scaled * mixed)).astype(bf16)


def vmem():
    return pl.BlockSpec(memory_space=pltpu.VMEM)


def smem():
    return pl.BlockSpec(memory_space=pltpu.SMEM)


def params():
    return pltpu.CompilerParams(vmem_limit_bytes=BIG)


def pack_call(rows):
    return pl.pallas_call(
        pack_kernel,
        out_shape=jax.ShapeDtypeStruct((HEADS, LINES, 128), bf16),
        in_specs=[vmem()],
        out_specs=vmem(),
        compiler_params=params(),
    )(rows)


def permute_call(place, source, received):
    return pl.pallas_call(
        permute_kernel,
        out_shape=jax.ShapeDtypeStruct((RING, SLOTS, LINES, 128), bf16),
        in_specs=[smem(), smem(), vmem()],
        out_specs=vmem(),
        scratch_shapes=[pltpu.VMEM((HEADS * CHUNK, 128), f32), pltpu.VMEM((CHUNK, 128), f32)],
        compiler_params=params(),
    )(place, source, received)


def norm_call(rows, gain):
    return pl.pallas_call(
        norm_kernel,
        out_shape=jax.ShapeDtypeStruct(rows.shape, bf16),
        in_specs=[vmem(), vmem()],
        out_specs=vmem(),
        compiler_params=params(),
    )(rows, gain)


def head_call(place, normed, weights, upstream, windows):
    rows, width = normed.shape
    return pl.pallas_call(
        head_kernel,
        grid=(RING,),
        out_shape=(
            jax.ShapeDtypeStruct((rows, RING * PADDED), bf16),
            jax.ShapeDtypeStruct((16, RING, 16, width), bf16),
            jax.ShapeDtypeStruct((1, width), f32),
        ),
        in_specs=[
            smem(),
            pl.BlockSpec((rows, width), lambda h: (0, 0)),
            pl.BlockSpec((16, 1, 16, width), lambda h: (0, h, 0, 0)),
            pl.BlockSpec((1, SLOTS, LINES, 128), lambda h: (h, 0, 0, 0)),
            pl.BlockSpec((32, 128), lambda h: (0, 0)),
        ],
        out_specs=(
            pl.BlockSpec((rows, PADDED), lambda h: (0, h)),
            pl.BlockSpec((16, 1, 16, width), lambda h: (0, h, 0, 0)),
            pl.BlockSpec((1, width), lambda h: (0, 0)),
        ),
        scratch_shapes=[
            pltpu.VMEM((rows, 128), bf16),
            pltpu.VMEM((rows, 128), bf16),
            pltpu.VMEM((rows, 128), bf16),
            pltpu.VMEM((rows, PADDED), bf16),
            pltpu.VMEM((rows, 128), bf16),
        ],
        compiler_params=params(),
    )(place, normed, weights, upstream, windows)


def back_call(grads, weights):
    rows, width = grads.shape[0], weights.shape[-1]
    piece = 256
    return pl.pallas_call(
        back_kernel,
        grid=(width // piece,),
        out_shape=(
            jax.ShapeDtypeStruct((2 * CHUNK, width), f32),
            jax.ShapeDtypeStruct((2 * CHUNK, width), bf16),
        ),
        in_specs=[
            pl.BlockSpec((rows, RING * PADDED), lambda n: (0, 0)),
            pl.BlockSpec((16, RING, 16, piece), lambda n: (0, 0, 0, n)),
        ],
        out_specs=(
            pl.BlockSpec((2 * CHUNK, piece), lambda n: (0, n)),
            pl.BlockSpec((2 * CHUNK, piece), lambda n: (0, n)),
        ),
        compiler_params=params(),
    )(grads, weights)


def final_call(rows, gain, keep, from_core, from_pair):
    return pl.pallas_call(
        final_kernel,
        out_shape=jax.ShapeDtypeStruct(rows.shape, bf16),
        in_specs=[vmem()] * 5,
        out_specs=vmem(),
        compiler_params=params(),
    )(rows, gain, keep, from_core, from_pair)


def swap(x, axis):
    return lax.ppermute(x, axis, [(0, 1), (1, 0)])


def on_device(layer_input, grad_packed, source_row, window_id, w_qkv, gain):
    width = layer_input.shape[1]
    dp = lax.axis_index("y") * 4 + lax.axis_index("x")
    ring = lax.axis_index("zq")
    slot = lax.axis_index("zp") * 2 + lax.axis_index("core")
    place = jnp.stack([ring, slot]).astype(jnp.int32)
    gain_row = gain.reshape(1, width)

    flipped = jnp.swapaxes(w_qkv, 1, 2).reshape(3 * HEAD, width)
    flipped = jnp.pad(flipped, ((0, PADDED - 3 * HEAD), (0, 0)))
    share = lax.dynamic_slice(flipped, (16 * dp, 0), (16, width))
    others = [lax.ppermute(share, "zq", [(i, (i + k) % RING) for i in range(RING)]) for k in (3, 2, 1)]
    circle = jnp.concatenate([share] + others + [share] + others, axis=0)
    ordered = lax.dynamic_slice(circle, (16 * ((RING - ring) % RING), 0), (16 * RING, width))
    weights = lax.all_gather(ordered, ("y", "x"), axis=0, tiled=True)
    weights = weights.reshape(16, RING, 16, width)

    packed = pack_call(grad_packed)
    packed, rows_in = lax.optimization_barrier((packed, layer_input))
    by_head = lax.all_to_all(packed, ("zq", "zp", "core"), split_axis=0, concat_axis=0)
    permuted = permute_call(place, source_row.reshape(-1), by_head)
    upstream = lax.all_to_all(permuted, "zq", split_axis=0, concat_axis=0)

    own = norm_call(rows_in, gain_row)
    half = jnp.concatenate([own, swap(own, "zp")], axis=0)
    normed = jnp.concatenate([half, swap(half, "core")], axis=0)

    windows = window_id.reshape(32, 128).astype(f32)
    grads, weight_part, gain_part = head_call(place, normed, weights, upstream, windows)

    arrived = lax.all_to_all(weight_part, ("y", "x"), split_axis=0, concat_axis=0)
    summed = jnp.sum(arrived.astype(f32), axis=0).astype(bf16)
    gain_part = gain_part + swap(gain_part, "core")
    gain_part = gain_part + swap(gain_part, "zp")
    beside = jnp.pad(gain_part.reshape(10, 128), ((0, 6), (0, 0))).astype(bf16)
    beside = jnp.broadcast_to(beside[None], (RING, 16, 128))
    keep, send = back_call(grads, weights)
    from_core = swap(send, "core")
    pair = (keep[CHUNK:] + from_core[CHUNK:].astype(f32)).astype(bf16)
    from_pair = swap(pair, "zp")
    grad_input = final_call(layer_input, gain_row, keep[:CHUNK], from_core[:CHUNK], from_pair)
    message = jnp.concatenate([summed, beside], axis=2)
    message, grad_input = lax.optimization_barrier((message, grad_input))
    arrived = lax.all_to_all(message, "zq", split_axis=0, concat_axis=0)
    summed = jnp.sum(arrived.astype(f32), axis=0).astype(bf16)
    copies = jnp.broadcast_to(summed[None], (16,) + summed.shape)
    whole = lax.all_to_all(copies, ("y", "x"), split_axis=0, concat_axis=0)
    gradient = whole[:, :, :width].reshape(PADDED, width)[: 3 * HEAD].astype(f32)
    grad_weight = jnp.swapaxes(gradient.reshape(3, HEAD, width), 1, 2)
    grad_gain = jnp.sum(whole[:, :10, width:].astype(f32), axis=0).reshape(width) / gain

    return (grad_input, grad_weight, grad_gain)


def solution(mesh):
    fine = Mesh(mesh.devices.reshape(4, 4, 4, 2, 2), ("y", "x", "zq", "zp", "core"))
    dp, group = ("y", "x"), ("zq", "zp", "core")
    rows = P(dp + group, None)
    return jax.shard_map(
        on_device,
        mesh=fine,
        in_specs=(rows, rows, P(dp, None), P(dp, None), P(None, None, group), P()),
        out_specs=(rows, P(None, None, group), P()),
        check_vma=False,
    )
```

```python
import functools

import jax
import jax.numpy as jnp
from jax import lax
from jax.experimental import pallas as pl
from jax.experimental.pallas import tpu as pltpu
from jax.sharding import Mesh, PartitionSpec as P

HEAD = 80
HEADS = 16
SUPER = 128
CHUNK = 256
SLOTS = 4
RING = 4
LINES = 160
PADDED = 256
XOR_ORDER = (0, 2, 1, 3)
epsilon = 1e-06
bf16 = jnp.bfloat16
f32 = jnp.float32
NT = (((1,), (1,)), ((), ()))
TN = (((0,), (0,)), ((), ()))
NN = (((1,), (0,)), ((), ()))
BIG = 28 * 1024 * 1024


def dot(a, b, dims):
    return lax.dot_general(a, b, dims, preferred_element_type=f32)


def lanes(shape):
    return lax.broadcasted_iota(jnp.int32, shape, len(shape) - 1)


def roll(x, shift):
    shift = shift % x.shape[-1]
    return x if shift == 0 else pltpu.roll(x, shift, x.ndim - 1)


def pack(rows):
    top = jnp.where(lanes((128, 128)) < 64, rows[:128], roll(rows[128:], 64))
    group = lanes((32, 128)) // 16
    low = roll(rows[:32], -64)
    for k in range(1, 8):
        low = jnp.where(group == k, roll(rows[32 * k : 32 * k + 32], 16 * k - 64), low)
    return top, low


def unpack(top, low, place):
    at = lanes((128, 128))
    upper = roll(top, place)
    lower = roll(top, place - 64)
    tail = [roll(low, place + 64 - 16 * k) for k in range(8)]
    first = jnp.concatenate(tail[:4], axis=0)
    second = jnp.concatenate(tail[4:], axis=0)
    wide = (at >= place) & (at < place + 64)
    rest = (at >= place + 64) & (at < place + HEAD)
    one = jnp.where(wide, upper, jnp.where(rest, first, 0.0))
    two = jnp.where(wide, lower, jnp.where(rest, second, 0.0))
    return one, two


def pack_kernel(rows_ref, out_ref):
    for g in range(HEADS):
        start = (HEAD * g) // 128 * 128
        shift = HEAD * g - start
        size = 128 if shift + HEAD <= 128 else 256
        window = rows_ref[:, start : start + size].astype(f32)
        window = roll(window, -shift)[:, :128]
        top, low = pack(window)
        out_ref[g, :128, :] = top.astype(bf16)
        out_ref[g, 128:, :] = low.astype(bf16)


def permute_kernel(place_ref, source_ref, in_ref, out_ref, table, picked):
    slot = place_ref[1]
    for src in range(HEADS):
        one, two = unpack(
            in_ref[src, :128, :].astype(f32), in_ref[src, 128:, :].astype(f32), 0
        )
        table[CHUNK * src : CHUNK * src + 128, :] = one
        table[CHUNK * src + 128 : CHUNK * src + 256, :] = two
    for q in range(RING):
        for o, off in enumerate(XOR_ORDER):
            base = q * SLOTS * CHUNK + (slot ^ off) * CHUNK

            def step(i, carry):
                at = i * 16
                for u in range(16):
                    row = source_ref[base + at + u]
                    picked[pl.ds(at + u, 1), :] = table[pl.ds(row, 1), :]
                return carry

            lax.fori_loop(0, CHUNK // 16, step, 0)
            top, low = pack(picked[...])
            out_ref[q, o, :128, :] = top.astype(bf16)
            out_ref[q, o, 128:, :] = low.astype(bf16)


def norm_kernel(rows_ref, gain_ref, out_ref):
    values = rows_ref[...].astype(f32)
    inverse = lax.rsqrt(jnp.mean(values * values, axis=-1, keepdims=True) + epsilon)
    out_ref[...] = (values * inverse * gain_ref[...]).astype(bf16)


def shifted(shape, move):
    row = lax.broadcasted_iota(jnp.int32, shape, 0)
    return jnp.where(move(row, lanes(shape)), 1.0, 0.0).astype(bf16)


def head_kernel(
    place_ref, normed_ref, turned_ref, w_ref, up_ref, window_ref, grad_ref, weight_ref,
    first, second, key_at, query_at, upstream, same,
):
    ring, slot = place_ref[0], place_ref[1]
    scaling = HEAD ** (-0.5)
    total_rows = SLOTS * CHUNK
    width = w_ref.shape[-1]
    blocks = [slice(SUPER * b, SUPER * b + SUPER) for b in range(total_rows // SUPER)]
    to_key = shifted((PADDED, 128), lambda r, c: (c < HEAD) & (r == c + HEAD))
    to_query = shifted(
        (128, PADDED), lambda r, c: (c >= HEAD) & (c < 2 * HEAD) & (r == c - HEAD)
    )
    to_wide = shifted(
        (128, 128), lambda r, c: (c >= 32) & (c < 96) & (r % 64 == c - 32)
    )
    to_rest = shifted(
        (128, 128), lambda r, c: (c >= 96) & (c < 112) & (r % 16 == c - 96)
    )
    row = lax.broadcasted_iota(jnp.int32, (CHUNK, 128), 0)
    keep_wide = row // 128 == lanes((CHUNK, 128)) // 64
    keep_rest = row // 32 == lanes((CHUNK, 128)) // 16

    def project(h):
        w = w_ref[:, h].reshape(PADDED, width)
        low = dot(normed_ref[...], w, NT).astype(bf16)
        first[h] = low[:, :128]
        second[h] = low[:, 128:]
        rounded = low.astype(f32)
        at = lanes((total_rows, PADDED))
        key_at[h] = jnp.where(at < HEAD, roll(rounded, -HEAD), 0.0)[:, :128].astype(bf16)
        query_at[h] = jnp.where(
            (at >= HEAD) & (at < 2 * HEAD), roll(rounded, HEAD), 0.0
        ).astype(bf16)

    def spread(h):
        for c in range(SLOTS):
            top, low = up_ref[h, c, :128, :], up_ref[h, c, 128:, :]
            wide = jnp.where(keep_wide, jnp.concatenate([top] * 2, axis=0), 0.0)
            rest = jnp.where(keep_rest, jnp.concatenate([low] * 8, axis=0), 0.0)
            both = dot(wide.astype(bf16), to_wide, NN) + dot(rest.astype(bf16), to_rest, NN)
            upstream[h, CHUNK * c : CHUNK * c + CHUNK, :] = both.astype(bf16)

    def attend(h):
        cols = slice(PADDED * h, PADDED * h + 128)
        more = slice(PADDED * h + 128, PADDED * h + PADDED)
        scores = [dot(first[h, r, :], key_at[h, r, :], NT) for r in blocks]
        grad_probs = [dot(upstream[h, r, :], second[h, r, :], NT) for r in blocks]
        probs, grad_scores = [], []
        for b, r in enumerate(blocks):
            masked = scores[b] * scaling + same[r, :]
            powers = jnp.exp(masked - jnp.max(masked, axis=-1, keepdims=True))
            prob = powers * (1.0 / jnp.sum(powers, axis=-1, keepdims=True))
            row_dot = jnp.sum(prob * grad_probs[b], axis=-1, keepdims=True)
            grad_scores.append((prob * (grad_probs[b] - row_dot)).astype(bf16))
            probs.append(prob.astype(bf16))
        for b, r in enumerate(blocks):
            grad_query = dot(grad_scores[b], key_at[h, r, :], NN)
            grad_key = dot(grad_scores[b], query_at[h, r, :], TN)
            grad_value = dot(probs[b], upstream[h, r, :], TN)
            grad_ref[r, cols] = ((grad_query + grad_key[:, :128]) * scaling).astype(bf16)
            grad_ref[r, more] = (grad_key[:, 128:] * scaling + grad_value).astype(bf16)

    def weigh(h):
        grads = grad_ref[:, PADDED * h : PADDED * h + PADDED]
        part = dot(turned_ref[...], grads, NN).astype(bf16)
        weight_ref[:, h] = part.reshape(16, width // 16, PADDED)

    for b, r in enumerate(blocks):
        line = ring * 8 + (slot ^ XOR_ORDER[b // 2]) * 2 + b % 2
        labels = jnp.broadcast_to(window_ref[pl.ds(line, 1), :], (SUPER, SUPER))
        same[r, :] = jnp.where(labels == labels.T, 0.0, -1e30)
    project(0)
    spread(0)
    for h in range(RING):
        if h + 1 < RING:
            project(h + 1)
            spread(h + 1)
        attend(h)
        weigh(h)


def back_kernel(grad_ref, w_ref, normed_ref, keep_ref, send_ref, gain_ref):
    parts = [w_ref[:, h].reshape(PADDED, w_ref.shape[-1]) for h in range(RING)]
    total = dot(grad_ref[...], jnp.concatenate(parts, axis=0), NN)
    keep_ref[...] = total[: 2 * CHUNK]
    send_ref[...] = total[2 * CHUNK :].astype(bf16)
    gain_ref[...] = jnp.sum(total * normed_ref[...].astype(f32), axis=0, keepdims=True)


def final_kernel(rows_ref, gain_ref, keep_ref, core_ref, pair_ref, out_ref):
    values = rows_ref[...].astype(f32)
    inverse = lax.rsqrt(jnp.mean(values * values, axis=-1, keepdims=True) + epsilon)
    scaled = values * inverse
    normed_grad = keep_ref[...] + core_ref[...].astype(f32) + pair_ref[...].astype(f32)
    grad_scaled = normed_grad * gain_ref[...]
    mixed = jnp.mean(grad_scaled * scaled, axis=-1, keepdims=True)
    out_ref[...] = (inverse * (grad_scaled - scaled * mixed)).astype(bf16)


def vmem():
    return pl.BlockSpec(memory_space=pltpu.VMEM)


def smem():
    return pl.BlockSpec(memory_space=pltpu.SMEM)


def params():
    return pltpu.CompilerParams(vmem_limit_bytes=BIG)


def pack_call(rows):
    return pl.pallas_call(
        pack_kernel,
        out_shape=jax.ShapeDtypeStruct((HEADS, LINES, 128), bf16),
        in_specs=[vmem()],
        out_specs=vmem(),
        compiler_params=params(),
    )(rows)


def permute_call(place, source, received):
    return pl.pallas_call(
        permute_kernel,
        out_shape=jax.ShapeDtypeStruct((RING, SLOTS, LINES, 128), bf16),
        in_specs=[smem(), smem(), vmem()],
        out_specs=vmem(),
        scratch_shapes=[pltpu.VMEM((HEADS * CHUNK, 128), f32), pltpu.VMEM((CHUNK, 128), f32)],
        compiler_params=params(),
    )(place, source, received)


def norm_call(rows, gain):
    return pl.pallas_call(
        norm_kernel,
        out_shape=jax.ShapeDtypeStruct(rows.shape, bf16),
        in_specs=[vmem(), vmem()],
        out_specs=vmem(),
        compiler_params=params(),
    )(rows, gain)


def head_call(place, normed, turned, weights, upstream, windows):
    rows, width = normed.shape
    return pl.pallas_call(
        head_kernel,
        out_shape=(
            jax.ShapeDtypeStruct((rows, RING * PADDED), bf16),
            jax.ShapeDtypeStruct((16, RING, width // 16, PADDED), bf16),
        ),
        in_specs=[smem()] + [vmem()] * 5,
        out_specs=(vmem(), vmem()),
        scratch_shapes=[
            pltpu.VMEM((RING, rows, 128), bf16),
            pltpu.VMEM((RING, rows, 128), bf16),
            pltpu.VMEM((RING, rows, 128), bf16),
            pltpu.VMEM((RING, rows, PADDED), bf16),
            pltpu.VMEM((RING, rows, 128), bf16),
            pltpu.VMEM((rows, SUPER), f32),
        ],
        compiler_params=params(),
    )(place, normed, turned, weights, upstream, windows)


def back_call(grads, weights, normed):
    rows, width = grads.shape[0], weights.shape[-1]
    piece = 256
    return pl.pallas_call(
        back_kernel,
        grid=(width // piece,),
        out_shape=(
            jax.ShapeDtypeStruct((2 * CHUNK, width), f32),
            jax.ShapeDtypeStruct((2 * CHUNK, width), bf16),
            jax.ShapeDtypeStruct((1, width), f32),
        ),
        in_specs=[
            pl.BlockSpec((rows, RING * PADDED), lambda n: (0, 0)),
            pl.BlockSpec((16, RING, 16, piece), lambda n: (0, 0, 0, n)),
            pl.BlockSpec((rows, piece), lambda n: (0, n)),
        ],
        out_specs=(
            pl.BlockSpec((2 * CHUNK, piece), lambda n: (0, n)),
            pl.BlockSpec((2 * CHUNK, piece), lambda n: (0, n)),
            pl.BlockSpec((1, piece), lambda n: (0, n)),
        ),
        compiler_params=params(),
    )(grads, weights, normed)


def final_call(rows, gain, keep, from_core, from_pair):
    return pl.pallas_call(
        final_kernel,
        out_shape=jax.ShapeDtypeStruct(rows.shape, bf16),
        in_specs=[vmem()] * 5,
        out_specs=vmem(),
        compiler_params=params(),
    )(rows, gain, keep, from_core, from_pair)


def swap(x, axis):
    return lax.ppermute(x, axis, [(0, 1), (1, 0)])


def on_device(layer_input, grad_packed, source_row, window_id, w_qkv, gain):
    width = layer_input.shape[1]
    dp = lax.axis_index("y") * 4 + lax.axis_index("x")
    ring = lax.axis_index("zq")
    slot = lax.axis_index("zp") * 2 + lax.axis_index("core")
    place = jnp.stack([ring, slot]).astype(jnp.int32)
    gain_row = gain.reshape(1, width)

    packed = pack_call(grad_packed)
    flipped = jnp.swapaxes(w_qkv, 1, 2).reshape(3 * HEAD, width)
    flipped = jnp.pad(flipped, ((0, PADDED - 3 * HEAD), (0, 0)))
    share = lax.dynamic_slice(flipped, (16 * dp, 0), (16, width))
    packed, share = lax.optimization_barrier((packed, share))
    others = [lax.ppermute(share, "zq", [(i, (i + k) % RING) for i in range(RING)]) for k in (3, 2, 1)]
    circle = jnp.concatenate([share] + others + [share] + others, axis=0)
    ordered = lax.dynamic_slice(circle, (16 * ((RING - ring) % RING), 0), (16 * RING, width))
    weights = lax.all_gather(ordered, ("y", "x"), axis=0, tiled=True)
    weights = weights.reshape(16, RING, 16, width)

    by_head = lax.all_to_all(packed, ("zq", "zp", "core"), split_axis=0, concat_axis=0)
    own = norm_call(layer_input, gain_row)
    by_head, own = lax.optimization_barrier((by_head, own))
    permuted = permute_call(place, source_row.reshape(-1), by_head)
    upstream = lax.all_to_all(permuted, "zq", split_axis=0, concat_axis=0)

    half = jnp.concatenate([own, swap(own, "zp")], axis=0)
    normed = jnp.concatenate([half, swap(half, "core")], axis=0)
    windows = window_id.reshape(32, 128).astype(f32)
    grads, weight_part = head_call(place, normed, normed.T, weights, upstream, windows)

    arrived = lax.all_to_all(weight_part, ("y", "x"), split_axis=0, concat_axis=0)
    summed = jnp.sum(arrived.astype(f32), axis=0).astype(bf16)
    keep, send, gain_part = back_call(grads, weights, normed)
    from_core = swap(send, "core")
    pair = (keep[CHUNK:] + from_core[CHUNK:].astype(f32)).astype(bf16)
    gain_part = gain_part + swap(gain_part, "core")
    gain_part = gain_part + swap(gain_part, "zp")
    beside = gain_part.reshape(width // 16, 16).astype(bf16)
    beside = jnp.broadcast_to(beside[None], (RING, width // 16, 16))
    message = jnp.concatenate([summed[..., : 3 * HEAD], beside], axis=2)
    message, pair = lax.optimization_barrier((message, pair))
    from_pair = swap(pair, "zp")
    arrived = lax.all_to_all(message, "zq", split_axis=0, concat_axis=0)
    summed = jnp.sum(arrived.astype(f32), axis=0).astype(bf16)
    copies = jnp.broadcast_to(summed[None], (16,) + summed.shape)
    copies, from_pair = lax.optimization_barrier((copies, from_pair))
    whole = lax.all_to_all(copies, ("y", "x"), split_axis=0, concat_axis=0)
    gradient = whole.reshape(width, PADDED).astype(f32)
    grad_weight = jnp.stack([gradient[:, HEAD * j : HEAD * j + HEAD] for j in range(3)])
    grad_gain = jnp.sum(whole[:, :, 3 * HEAD :].astype(f32), axis=0).reshape(width) / gain
    grad_input = final_call(layer_input, gain_row, keep[:CHUNK], from_core[:CHUNK], from_pair)
    return (grad_input, grad_weight, grad_gain)


def solution(mesh):
    fine = Mesh(mesh.devices.reshape(4, 4, 4, 2, 2), ("y", "x", "zq", "zp", "core"))
    dp, group = ("y", "x"), ("zq", "zp", "core")
    rows = P(dp + group, None)
    return jax.shard_map(
        on_device,
        mesh=fine,
        in_specs=(rows, rows, P(dp, None), P(dp, None), P(None, None, group), P()),
        out_specs=(rows, P(None, None, group), P()),
        check_vma=False,
    )
```

```python
import functools

import jax
import jax.numpy as jnp
from jax import lax
from jax.experimental import pallas as pl
from jax.experimental.pallas import tpu as pltpu
from jax.sharding import Mesh, PartitionSpec as P

HEAD = 80
HEADS = 16
SUPER = 128
CHUNK = 256
SLOTS = 4
RING = 4
LINES = 160
PADDED = 256
XOR_ORDER = (0, 2, 1, 3)
epsilon = 1e-06
bf16 = jnp.bfloat16
f32 = jnp.float32
NT = (((1,), (1,)), ((), ()))
TN = (((0,), (0,)), ((), ()))
NN = (((1,), (0,)), ((), ()))
BIG = 34 * 1024 * 1024
SMALL = 20 * 1024 * 1024


def dot(a, b, dims):
    return lax.dot_general(a, b, dims, preferred_element_type=f32)


def lanes(shape):
    return lax.broadcasted_iota(jnp.int32, shape, len(shape) - 1)


def roll(x, shift):
    shift = shift % x.shape[-1]
    return x if shift == 0 else pltpu.roll(x, shift, x.ndim - 1)


def pack(rows):
    top = jnp.where(lanes((128, 128)) < 64, rows[:128], roll(rows[128:], 64))
    group = lanes((32, 128)) // 16
    low = roll(rows[:32], -64)
    for k in range(1, 8):
        low = jnp.where(group == k, roll(rows[32 * k : 32 * k + 32], 16 * k - 64), low)
    return top, low


def unpack(top, low, place):
    at = lanes((128, 128))
    upper = roll(top, place)
    lower = roll(top, place - 64)
    tail = [roll(low, place + 64 - 16 * k) for k in range(8)]
    first = jnp.concatenate(tail[:4], axis=0)
    second = jnp.concatenate(tail[4:], axis=0)
    wide = (at >= place) & (at < place + 64)
    rest = (at >= place + 64) & (at < place + HEAD)
    one = jnp.where(wide, upper, jnp.where(rest, first, 0.0))
    two = jnp.where(wide, lower, jnp.where(rest, second, 0.0))
    return one, two


def pack_kernel(rows_ref, out_ref):
    for g in range(HEADS):
        start = (HEAD * g) // 128 * 128
        shift = HEAD * g - start
        size = 128 if shift + HEAD <= 128 else 256
        window = rows_ref[:, start : start + size].astype(f32)
        window = roll(window, -shift)[:, :128]
        top, low = pack(window)
        out_ref[g, :128, :] = top.astype(bf16)
        out_ref[g, 128:, :] = low.astype(bf16)


def permute_kernel(place_ref, source_ref, in_ref, out_ref, table, picked):
    slot = place_ref[1]
    for src in range(HEADS):
        one, two = unpack(
            in_ref[src, :128, :].astype(f32), in_ref[src, 128:, :].astype(f32), 0
        )
        table[CHUNK * src : CHUNK * src + 128, :] = one
        table[CHUNK * src + 128 : CHUNK * src + 256, :] = two
    for q in range(RING):
        for o, off in enumerate(XOR_ORDER):
            base = q * SLOTS * CHUNK + (slot ^ off) * CHUNK

            def step(i, carry):
                at = i * 16
                for u in range(16):
                    row = source_ref[base + at + u]
                    picked[pl.ds(at + u, 1), :] = table[pl.ds(row, 1), :]
                return carry

            lax.fori_loop(0, CHUNK // 16, step, 0)
            top, low = pack(picked[...])
            out_ref[q, o, :128, :] = top.astype(bf16)
            out_ref[q, o, 128:, :] = low.astype(bf16)


def norm_kernel(rows_ref, gain_ref, out_ref):
    values = rows_ref[...].astype(f32)
    inverse = lax.rsqrt(jnp.mean(values * values, axis=-1, keepdims=True) + epsilon)
    out_ref[...] = (values * inverse * gain_ref[...]).astype(bf16)


def shifted(shape, move):
    row = lax.broadcasted_iota(jnp.int32, shape, 0)
    return jnp.where(move(row, lanes(shape)), 1.0, 0.0).astype(bf16)


def head_kernel(
    place_ref, normed_ref, turned_hbm, w_hbm, up_ref, window_ref, grad_hbm, weight_hbm,
    first, second, key_at, query_at, upstream, same,
    turned_ref, w_ref, grad_ref, weight_ref, in_sems, out_sems,
):
    ring, slot = place_ref[0], place_ref[1]
    scaling = HEAD ** (-0.5)
    total_rows = SLOTS * CHUNK
    width = normed_ref.shape[-1]
    blocks = [slice(SUPER * b, SUPER * b + SUPER) for b in range(total_rows // SUPER)]
    w_copies = [
        pltpu.make_async_copy(w_hbm.at[:, h], w_ref.at[h], in_sems.at[h]) for h in range(RING)
    ]
    turned_copy = pltpu.make_async_copy(turned_hbm, turned_ref, in_sems.at[RING])
    w_copies[0].start()
    for h in range(1, RING):
        w_copies[h].start()
    turned_copy.start()
    grad_copies = [
        pltpu.make_async_copy(grad_ref.at[h], grad_hbm.at[h], out_sems.at[h])
        for h in range(RING)
    ]
    weight_copies = [
        pltpu.make_async_copy(weight_ref.at[h], weight_hbm.at[:, h], out_sems.at[RING + h])
        for h in range(RING)
    ]
    to_wide = shifted(
        (128, 128), lambda r, c: (c >= 32) & (c < 96) & (r % 64 == c - 32)
    )
    to_rest = shifted(
        (128, 128), lambda r, c: (c >= 96) & (c < 112) & (r % 16 == c - 96)
    )
    row = lax.broadcasted_iota(jnp.int32, (CHUNK, 128), 0)
    keep_wide = row // 128 == lanes((CHUNK, 128)) // 64
    keep_rest = row // 32 == lanes((CHUNK, 128)) // 16

    def project(h):
        w = w_ref[h].reshape(PADDED, width)
        low = dot(normed_ref[...], w, NT).astype(bf16)
        first[h] = low[:, :128]
        second[h] = low[:, 128:]
        rounded = low.astype(f32)
        at = lanes((total_rows, PADDED))
        key_at[h] = jnp.where(at < HEAD, roll(rounded, -HEAD), 0.0)[:, :128].astype(bf16)
        query_at[h] = jnp.where(
            (at >= HEAD) & (at < 2 * HEAD), roll(rounded, HEAD), 0.0
        ).astype(bf16)

    def spread(h):
        for c in range(SLOTS):
            top, low = up_ref[h, c, :128, :], up_ref[h, c, 128:, :]
            wide = jnp.where(keep_wide, jnp.concatenate([top] * 2, axis=0), 0.0)
            rest = jnp.where(keep_rest, jnp.concatenate([low] * 8, axis=0), 0.0)
            both = dot(wide.astype(bf16), to_wide, NN) + dot(rest.astype(bf16), to_rest, NN)
            upstream[h, CHUNK * c : CHUNK * c + CHUNK, :] = both.astype(bf16)

    def attend(h):
        scores = [dot(first[h, r, :], key_at[h, r, :], NT) for r in blocks]
        grad_probs = [dot(upstream[h, r, :], second[h, r, :], NT) for r in blocks]
        probs, grad_scores = [], []
        for b, r in enumerate(blocks):
            masked = scores[b] * scaling + same[r, :]
            powers = jnp.exp(masked - jnp.max(masked, axis=-1, keepdims=True))
            prob = powers * (1.0 / jnp.sum(powers, axis=-1, keepdims=True))
            row_dot = jnp.sum(prob * grad_probs[b], axis=-1, keepdims=True)
            grad_scores.append((prob * (grad_probs[b] - row_dot)).astype(bf16))
            probs.append(prob.astype(bf16))
        for b, r in enumerate(blocks):
            grad_query = dot(grad_scores[b], key_at[h, r, :], NN)
            grad_key = dot(grad_scores[b], query_at[h, r, :], TN)
            grad_value = dot(probs[b], upstream[h, r, :], TN)
            grad_ref[h, r, :128] = ((grad_query + grad_key[:, :128]) * scaling).astype(bf16)
            grad_ref[h, r, 128:] = (grad_key[:, 128:] * scaling + grad_value).astype(bf16)

    def weigh(h):
        part = dot(turned_ref[...], grad_ref[h], NN).astype(bf16)
        weight_ref[h] = part.reshape(16, width // 16, PADDED)

    for b, r in enumerate(blocks):
        line = ring * 8 + (slot ^ XOR_ORDER[b // 2]) * 2 + b % 2
        labels = jnp.broadcast_to(window_ref[pl.ds(line, 1), :], (SUPER, SUPER))
        same[r, :] = jnp.where(labels == labels.T, 0.0, -1e30)
    spread(0)
    w_copies[0].wait()
    project(0)
    for copy in w_copies[1:] + [turned_copy]:
        copy.wait()
    for h in range(RING):
        if h + 1 < RING:
            project(h + 1)
            spread(h + 1)
        attend(h)
        weigh(h)
    for copy in weight_copies + grad_copies:
        copy.start()
    for copy in weight_copies + grad_copies:
        copy.wait()


def back_kernel(grad_ref, w_ref, normed_ref, keep_ref, send_ref, gain_ref):
    parts = [w_ref[:, h].reshape(PADDED, w_ref.shape[-1]) for h in range(RING)]
    grads = jnp.concatenate([grad_ref[h] for h in range(RING)], axis=1)
    total = dot(grads, jnp.concatenate(parts, axis=0), NN)
    keep_ref[...] = total[: 2 * CHUNK]
    send_ref[...] = total[2 * CHUNK :].astype(bf16)
    gain_ref[...] = jnp.sum(total * normed_ref[...].astype(f32), axis=0, keepdims=True)


def final_kernel(rows_ref, gain_ref, keep_ref, core_ref, pair_ref, out_ref):
    values = rows_ref[...].astype(f32)
    inverse = lax.rsqrt(jnp.mean(values * values, axis=-1, keepdims=True) + epsilon)
    scaled = values * inverse
    normed_grad = keep_ref[...] + core_ref[...].astype(f32) + pair_ref[...].astype(f32)
    grad_scaled = normed_grad * gain_ref[...]
    mixed = jnp.mean(grad_scaled * scaled, axis=-1, keepdims=True)
    out_ref[...] = (inverse * (grad_scaled - scaled * mixed)).astype(bf16)


def vmem():
    return pl.BlockSpec(memory_space=pltpu.VMEM)


def smem():
    return pl.BlockSpec(memory_space=pltpu.SMEM)


def params(limit=SMALL):
    return pltpu.CompilerParams(vmem_limit_bytes=limit)


def pack_call(rows):
    return pl.pallas_call(
        pack_kernel,
        out_shape=jax.ShapeDtypeStruct((HEADS, LINES, 128), bf16),
        in_specs=[vmem()],
        out_specs=vmem(),
        compiler_params=params(),
    )(rows)


def permute_call(place, source, received):
    return pl.pallas_call(
        permute_kernel,
        out_shape=jax.ShapeDtypeStruct((RING, SLOTS, LINES, 128), bf16),
        in_specs=[smem(), smem(), vmem()],
        out_specs=vmem(),
        scratch_shapes=[pltpu.VMEM((HEADS * CHUNK, 128), f32), pltpu.VMEM((CHUNK, 128), f32)],
        compiler_params=params(),
    )(place, source, received)


def norm_call(rows, gain):
    return pl.pallas_call(
        norm_kernel,
        out_shape=jax.ShapeDtypeStruct(rows.shape, bf16),
        in_specs=[vmem(), vmem()],
        out_specs=vmem(),
        compiler_params=params(),
    )(rows, gain)


def head_call(place, normed, turned, weights, upstream, windows):
    rows, width = normed.shape
    return pl.pallas_call(
        head_kernel,
        out_shape=(
            jax.ShapeDtypeStruct((RING, rows, PADDED), bf16),
            jax.ShapeDtypeStruct((16, RING, width // 16, PADDED), bf16),
        ),
        in_specs=[smem(), vmem()] + [pl.BlockSpec(memory_space=pl.ANY)] * 2 + [vmem()] * 2,
        out_specs=(pl.BlockSpec(memory_space=pl.ANY),) * 2,
        scratch_shapes=[
            pltpu.VMEM((RING, rows, 128), bf16),
            pltpu.VMEM((RING, rows, 128), bf16),
            pltpu.VMEM((RING, rows, 128), bf16),
            pltpu.VMEM((RING, rows, PADDED), bf16),
            pltpu.VMEM((RING, rows, 128), bf16),
            pltpu.VMEM((rows, SUPER), f32),
            pltpu.VMEM((width, rows), bf16),
            pltpu.VMEM((RING, 16, 16, width), bf16),
            pltpu.VMEM((RING, rows, PADDED), bf16),
            pltpu.VMEM((RING, 16, width // 16, PADDED), bf16),
            pltpu.SemaphoreType.DMA((RING + 1,)),
            pltpu.SemaphoreType.DMA((2 * RING,)),
        ],
        compiler_params=params(BIG),
    )(place, normed, turned, weights, upstream, windows)


def back_call(grads, weights, normed):
    rows, width = grads.shape[1], weights.shape[-1]
    piece = 256
    return pl.pallas_call(
        back_kernel,
        grid=(width // piece,),
        out_shape=(
            jax.ShapeDtypeStruct((2 * CHUNK, width), f32),
            jax.ShapeDtypeStruct((2 * CHUNK, width), bf16),
            jax.ShapeDtypeStruct((1, width), f32),
        ),
        in_specs=[
            pl.BlockSpec((RING, rows, PADDED), lambda n: (0, 0, 0)),
            pl.BlockSpec((16, RING, 16, piece), lambda n: (0, 0, 0, n)),
            pl.BlockSpec((rows, piece), lambda n: (0, n)),
        ],
        out_specs=(
            pl.BlockSpec((2 * CHUNK, piece), lambda n: (0, n)),
            pl.BlockSpec((2 * CHUNK, piece), lambda n: (0, n)),
            pl.BlockSpec((1, piece), lambda n: (0, n)),
        ),
        compiler_params=params(),
    )(grads, weights, normed)


def final_call(rows, gain, keep, from_core, from_pair):
    return pl.pallas_call(
        final_kernel,
        out_shape=jax.ShapeDtypeStruct(rows.shape, bf16),
        in_specs=[vmem()] * 5,
        out_specs=vmem(),
        compiler_params=params(),
    )(rows, gain, keep, from_core, from_pair)


def swap(x, axis):
    return lax.ppermute(x, axis, [(0, 1), (1, 0)])


def on_device(layer_input, grad_packed, source_row, window_id, w_qkv, gain):
    width = layer_input.shape[1]
    dp = lax.axis_index("y") * 4 + lax.axis_index("x")
    ring = lax.axis_index("zq")
    slot = lax.axis_index("zp") * 2 + lax.axis_index("core")
    place = jnp.stack([ring, slot]).astype(jnp.int32)
    gain_row = gain.reshape(1, width)

    packed = pack_call(grad_packed)
    flipped = jnp.swapaxes(w_qkv, 1, 2).reshape(3 * HEAD, width)
    flipped = jnp.pad(flipped, ((0, PADDED - 3 * HEAD), (0, 0)))
    share = lax.dynamic_slice(flipped, (16 * dp, 0), (16, width))
    others = [lax.ppermute(share, "zq", [(i, (i + k) % RING) for i in range(RING)]) for k in (3, 2, 1)]
    own = norm_call(layer_input, gain_row)
    others, packed, own = lax.optimization_barrier((others, packed, own))
    circle = jnp.concatenate([share] + others + [share] + others, axis=0)
    ordered = lax.dynamic_slice(circle, (16 * ((RING - ring) % RING), 0), (16 * RING, width))
    weights = lax.all_gather(ordered, ("y", "x"), axis=0, tiled=True)
    weights = weights.reshape(16, RING, 16, width)

    by_head = lax.all_to_all(packed, ("zq", "zp", "core"), split_axis=0, concat_axis=0)
    permuted = permute_call(place, source_row.reshape(-1), by_head)
    upstream = lax.all_to_all(permuted, "zq", split_axis=0, concat_axis=0)

    half = jnp.concatenate([own, swap(own, "zp")], axis=0)
    normed = jnp.concatenate([half, swap(half, "core")], axis=0)
    windows = window_id.reshape(32, 128).astype(f32)
    grads, weight_part = head_call(place, normed, normed.T, weights, upstream, windows)

    arrived = lax.all_to_all(weight_part, ("y", "x"), split_axis=0, concat_axis=0)
    summed = jnp.sum(arrived.astype(f32), axis=0).astype(bf16)
    keep, send, gain_part = back_call(grads, weights, normed)
    from_core = swap(send, "core")
    pair = (keep[CHUNK:] + from_core[CHUNK:].astype(f32)).astype(bf16)
    gain_part = gain_part + swap(gain_part, "core")
    gain_part = gain_part + swap(gain_part, "zp")
    beside = gain_part.reshape(width // 16, 16).astype(bf16)
    beside = jnp.broadcast_to(beside[None], (RING, width // 16, 16))
    message = jnp.concatenate([summed[..., : 3 * HEAD], beside], axis=2)
    message, pair = lax.optimization_barrier((message, pair))
    arrived = lax.all_to_all(message, "zq", split_axis=0, concat_axis=0)
    summed = jnp.sum(arrived.astype(f32), axis=0).astype(bf16)
    copies = jnp.broadcast_to(summed[None], (16,) + summed.shape)
    copies, pair = lax.optimization_barrier((copies, pair))
    from_pair = swap(pair, "zp")
    whole = lax.all_to_all(copies, ("y", "x"), split_axis=0, concat_axis=0)
    gradient = whole.reshape(width, PADDED).astype(f32)
    grad_weight = jnp.stack([gradient[:, HEAD * j : HEAD * j + HEAD] for j in range(3)])
    grad_gain = jnp.sum(whole[:, :, 3 * HEAD :].astype(f32), axis=0).reshape(width) / gain
    grad_input = final_call(layer_input, gain_row, keep[:CHUNK], from_core[:CHUNK], from_pair)
    return (grad_input, grad_weight, grad_gain)


def solution(mesh):
    fine = Mesh(mesh.devices.reshape(4, 4, 4, 2, 2), ("y", "x", "zq", "zp", "core"))
    dp, group = ("y", "x"), ("zq", "zp", "core")
    rows = P(dp + group, None)
    return jax.shard_map(
        on_device,
        mesh=fine,
        in_specs=(rows, rows, P(dp, None), P(dp, None), P(None, None, group), P()),
        out_specs=(rows, P(None, None, group), P()),
        check_vma=False,
    )
```

```python
import functools

import jax
import jax.numpy as jnp
from jax import lax
from jax.experimental import pallas as pl
from jax.experimental.pallas import tpu as pltpu
from jax.sharding import Mesh, PartitionSpec as P

HEAD = 80
HEADS = 16
SUPER = 128
CHUNK = 256
SLOTS = 4
RING = 4
LINES = 160
PADDED = 256
XOR_ORDER = (0, 2, 1, 3)
epsilon = 1e-06
bf16 = jnp.bfloat16
f32 = jnp.float32
NT = (((1,), (1,)), ((), ()))
TN = (((0,), (0,)), ((), ()))
NN = (((1,), (0,)), ((), ()))
BIG = 58 * 1024 * 1024
SMALL = 20 * 1024 * 1024


def dot(a, b, dims):
    return lax.dot_general(a, b, dims, preferred_element_type=f32)


def lanes(shape):
    return lax.broadcasted_iota(jnp.int32, shape, len(shape) - 1)


def roll(x, shift):
    shift = shift % x.shape[-1]
    return x if shift == 0 else pltpu.roll(x, shift, x.ndim - 1)


def pack(rows):
    top = jnp.where(lanes((128, 128)) < 64, rows[:128], roll(rows[128:], 64))
    group = lanes((32, 128)) // 16
    low = roll(rows[:32], -64)
    for k in range(1, 8):
        low = jnp.where(group == k, roll(rows[32 * k : 32 * k + 32], 16 * k - 64), low)
    return top, low


def unpack(top, low, place):
    at = lanes((128, 128))
    upper = roll(top, place)
    lower = roll(top, place - 64)
    tail = [roll(low, place + 64 - 16 * k) for k in range(8)]
    first = jnp.concatenate(tail[:4], axis=0)
    second = jnp.concatenate(tail[4:], axis=0)
    wide = (at >= place) & (at < place + 64)
    rest = (at >= place + 64) & (at < place + HEAD)
    one = jnp.where(wide, upper, jnp.where(rest, first, 0.0))
    two = jnp.where(wide, lower, jnp.where(rest, second, 0.0))
    return one, two


def pack_kernel(rows_ref, out_ref):
    for g in range(HEADS):
        start = (HEAD * g) // 128 * 128
        shift = HEAD * g - start
        size = 128 if shift + HEAD <= 128 else 256
        window = rows_ref[:, start : start + size].astype(f32)
        window = roll(window, -shift)[:, :128]
        top, low = pack(window)
        out_ref[g, :128, :] = top.astype(bf16)
        out_ref[g, 128:, :] = low.astype(bf16)


def permute_kernel(place_ref, source_ref, in_ref, out_ref, table, picked):
    slot = place_ref[1]
    for src in range(HEADS):
        one, two = unpack(
            in_ref[src, :128, :].astype(f32), in_ref[src, 128:, :].astype(f32), 0
        )
        table[CHUNK * src : CHUNK * src + 128, :] = one
        table[CHUNK * src + 128 : CHUNK * src + 256, :] = two
    for q in range(RING):
        for o, off in enumerate(XOR_ORDER):
            base = q * SLOTS * CHUNK + (slot ^ off) * CHUNK

            def step(i, carry):
                at = i * 64
                for u in range(64):
                    row = source_ref[base + at + u]
                    picked[pl.ds(at + u, 1), :] = table[pl.ds(row, 1), :]
                return carry

            lax.fori_loop(0, CHUNK // 64, step, 0)
            top, low = pack(picked[...])
            out_ref[q, o, :128, :] = top.astype(bf16)
            out_ref[q, o, 128:, :] = low.astype(bf16)


def norm_kernel(rows_ref, gain_ref, out_ref):
    values = rows_ref[...].astype(f32)
    inverse = lax.rsqrt(jnp.mean(values * values, axis=-1, keepdims=True) + epsilon)
    out_ref[...] = (values * inverse * gain_ref[...]).astype(bf16)


def shifted(shape, move):
    row = lax.broadcasted_iota(jnp.int32, shape, 0)
    return jnp.where(move(row, lanes(shape)), 1.0, 0.0).astype(bf16)


def head_kernel(
    place_ref, normed_hbm, turned_hbm, w_hbm, up_ref, window_ref, grad_hbm, weight_hbm,
    first, second, key_at, query_at, upstream, same,
    normed_ref, turned_ref, w_ref, grad_ref, weight_ref, in_sems, out_sems,
):
    ring, slot = place_ref[0], place_ref[1]
    scaling = HEAD ** (-0.5)
    total_rows = SLOTS * CHUNK
    width = normed_ref.shape[-1]
    blocks = [slice(SUPER * b, SUPER * b + SUPER) for b in range(total_rows // SUPER)]
    w_copies = [
        pltpu.make_async_copy(w_hbm.at[:, h], w_ref.at[h], in_sems.at[h]) for h in range(RING)
    ]
    turned_copy = pltpu.make_async_copy(turned_hbm, turned_ref, in_sems.at[RING])
    normed_copy = pltpu.make_async_copy(normed_hbm, normed_ref, in_sems.at[RING + 1])
    w_copies[0].start()
    normed_copy.start()
    for h in range(1, RING):
        w_copies[h].start()
    turned_copy.start()
    grad_copies = [
        pltpu.make_async_copy(grad_ref.at[h], grad_hbm.at[h], out_sems.at[h])
        for h in range(RING)
    ]
    weight_copies = [
        pltpu.make_async_copy(weight_ref.at[h], weight_hbm.at[:, h], out_sems.at[RING + h])
        for h in range(RING)
    ]
    to_wide = shifted(
        (128, 128), lambda r, c: (c >= 32) & (c < 96) & (r % 64 == c - 32)
    )
    to_rest = shifted(
        (128, 128), lambda r, c: (c >= 96) & (c < 112) & (r % 16 == c - 96)
    )
    row = lax.broadcasted_iota(jnp.int32, (CHUNK, 128), 0)
    keep_wide = row // 128 == lanes((CHUNK, 128)) // 64
    keep_rest = row // 32 == lanes((CHUNK, 128)) // 16

    def project(h):
        w = w_ref[h].reshape(PADDED, width)
        low = dot(normed_ref[...], w, NT).astype(bf16)
        first[h] = low[:, :128]
        second[h] = low[:, 128:]
        rounded = low.astype(f32)
        at = lanes((total_rows, PADDED))
        key_at[h] = jnp.where(at < HEAD, roll(rounded, -HEAD), 0.0)[:, :128].astype(bf16)
        query_at[h] = jnp.where(
            (at >= HEAD) & (at < 2 * HEAD), roll(rounded, HEAD), 0.0
        ).astype(bf16)

    def spread(h):
        for c in range(SLOTS):
            top, low = up_ref[h, c, :128, :], up_ref[h, c, 128:, :]
            wide = jnp.where(keep_wide, jnp.concatenate([top] * 2, axis=0), 0.0)
            rest = jnp.where(keep_rest, jnp.concatenate([low] * 8, axis=0), 0.0)
            both = dot(wide.astype(bf16), to_wide, NN) + dot(rest.astype(bf16), to_rest, NN)
            upstream[h, CHUNK * c : CHUNK * c + CHUNK, :] = both.astype(bf16)

    def attend(h):
        scores = [dot(first[h, r, :], key_at[h, r, :], NT) for r in blocks]
        grad_probs = [dot(upstream[h, r, :], second[h, r, :], NT) for r in blocks]
        probs, grad_scores = [], []
        for b, r in enumerate(blocks):
            masked = scores[b] * scaling + same[r, :]
            powers = jnp.exp(masked - jnp.max(masked, axis=-1, keepdims=True))
            prob = powers * (1.0 / jnp.sum(powers, axis=-1, keepdims=True))
            row_dot = jnp.sum(prob * grad_probs[b], axis=-1, keepdims=True)
            grad_scores.append((prob * (grad_probs[b] - row_dot)).astype(bf16))
            probs.append(prob.astype(bf16))
        for b, r in enumerate(blocks):
            grad_query = dot(grad_scores[b], key_at[h, r, :], NN)
            grad_key = dot(grad_scores[b], query_at[h, r, :], TN)
            grad_value = dot(probs[b], upstream[h, r, :], TN)
            grad_ref[h, r, :128] = ((grad_query + grad_key[:, :128]) * scaling).astype(bf16)
            grad_ref[h, r, 128:] = (grad_key[:, 128:] * scaling + grad_value).astype(bf16)

    def weigh(h):
        part = dot(turned_ref[...], grad_ref[h], NN).astype(bf16)
        weight_ref[h] = part.reshape(16, width // 16, PADDED)

    for b, r in enumerate(blocks):
        line = ring * 8 + (slot ^ XOR_ORDER[b // 2]) * 2 + b % 2
        labels = jnp.broadcast_to(window_ref[pl.ds(line, 1), :], (SUPER, SUPER))
        same[r, :] = jnp.where(labels == labels.T, 0.0, -1e30)
    spread(0)
    w_copies[0].wait()
    normed_copy.wait()
    project(0)
    for copy in w_copies[1:] + [turned_copy]:
        copy.wait()
    for h in range(RING):
        if h + 1 < RING:
            project(h + 1)
            spread(h + 1)
        attend(h)
        weigh(h)
    for copy in weight_copies + grad_copies:
        copy.start()
    for copy in weight_copies + grad_copies:
        copy.wait()


def back_kernel(grad_ref, w_ref, normed_ref, keep_ref, send_ref, gain_ref):
    parts = [w_ref[:, h].reshape(PADDED, w_ref.shape[-1]) for h in range(RING)]
    grads = jnp.concatenate([grad_ref[h] for h in range(RING)], axis=1)
    total = dot(grads, jnp.concatenate(parts, axis=0), NN)
    keep_ref[...] = total[: 2 * CHUNK]
    send_ref[...] = total[2 * CHUNK :].astype(bf16)
    gain_ref[...] = jnp.sum(total * normed_ref[...].astype(f32), axis=0, keepdims=True)


def final_kernel(
    rows_ref, gain_ref, keep_ref, core_ref, pair_ref, whole_ref, out_ref, weight_ref
):
    whole = whole_ref[...].reshape(weight_ref.shape[1], PADDED).astype(f32)
    for j in range(3):
        weight_ref[j] = roll(whole, -HEAD * j)[:, :HEAD]
    values = rows_ref[...].astype(f32)
    inverse = lax.rsqrt(jnp.mean(values * values, axis=-1, keepdims=True) + epsilon)
    scaled = values * inverse
    normed_grad = keep_ref[...] + core_ref[...].astype(f32) + pair_ref[...].astype(f32)
    grad_scaled = normed_grad * gain_ref[...]
    mixed = jnp.mean(grad_scaled * scaled, axis=-1, keepdims=True)
    out_ref[...] = (inverse * (grad_scaled - scaled * mixed)).astype(bf16)


def vmem():
    return pl.BlockSpec(memory_space=pltpu.VMEM)


def smem():
    return pl.BlockSpec(memory_space=pltpu.SMEM)


def params(limit=SMALL):
    return pltpu.CompilerParams(vmem_limit_bytes=limit)


def pack_call(rows):
    return pl.pallas_call(
        pack_kernel,
        out_shape=jax.ShapeDtypeStruct((HEADS, LINES, 128), bf16),
        in_specs=[vmem()],
        out_specs=vmem(),
        compiler_params=params(),
    )(rows)


def permute_call(place, source, received):
    return pl.pallas_call(
        permute_kernel,
        out_shape=jax.ShapeDtypeStruct((RING, SLOTS, LINES, 128), bf16),
        in_specs=[smem(), smem(), vmem()],
        out_specs=vmem(),
        scratch_shapes=[pltpu.VMEM((HEADS * CHUNK, 128), f32), pltpu.VMEM((CHUNK, 128), f32)],
        compiler_params=params(),
    )(place, source, received)


def norm_call(rows, gain):
    return pl.pallas_call(
        norm_kernel,
        out_shape=jax.ShapeDtypeStruct(rows.shape, bf16),
        in_specs=[vmem(), vmem()],
        out_specs=vmem(),
        compiler_params=params(),
    )(rows, gain)


def head_call(place, normed, turned, weights, upstream, windows):
    rows, width = normed.shape
    return pl.pallas_call(
        head_kernel,
        out_shape=(
            jax.ShapeDtypeStruct((RING, rows, PADDED), bf16),
            jax.ShapeDtypeStruct((16, RING, width // 16, PADDED), bf16),
        ),
        in_specs=[smem()] + [pl.BlockSpec(memory_space=pl.ANY)] * 3 + [vmem()] * 2,
        out_specs=(pl.BlockSpec(memory_space=pl.ANY),) * 2,
        scratch_shapes=[
            pltpu.VMEM((RING, rows, 128), bf16),
            pltpu.VMEM((RING, rows, 128), bf16),
            pltpu.VMEM((RING, rows, 128), bf16),
            pltpu.VMEM((RING, rows, PADDED), bf16),
            pltpu.VMEM((RING, rows, 128), bf16),
            pltpu.VMEM((rows, SUPER), f32),
            pltpu.VMEM((rows, width), bf16),
            pltpu.VMEM((width, rows), bf16),
            pltpu.VMEM((RING, 16, 16, width), bf16),
            pltpu.VMEM((RING, rows, PADDED), bf16),
            pltpu.VMEM((RING, 16, width // 16, PADDED), bf16),
            pltpu.SemaphoreType.DMA((RING + 2,)),
            pltpu.SemaphoreType.DMA((2 * RING,)),
        ],
        compiler_params=params(BIG),
    )(place, normed, turned, weights, upstream, windows)


def back_call(grads, weights, normed):
    rows, width = grads.shape[1], weights.shape[-1]
    piece = 256
    return pl.pallas_call(
        back_kernel,
        grid=(width // piece,),
        out_shape=(
            jax.ShapeDtypeStruct((2 * CHUNK, width), f32),
            jax.ShapeDtypeStruct((2 * CHUNK, width), bf16),
            jax.ShapeDtypeStruct((1, width), f32),
        ),
        in_specs=[
            pl.BlockSpec((RING, rows, PADDED), lambda n: (0, 0, 0)),
            pl.BlockSpec((16, RING, 16, piece), lambda n: (0, 0, 0, n)),
            pl.BlockSpec((rows, piece), lambda n: (0, n)),
        ],
        out_specs=(
            pl.BlockSpec((2 * CHUNK, piece), lambda n: (0, n)),
            pl.BlockSpec((2 * CHUNK, piece), lambda n: (0, n)),
            pl.BlockSpec((1, piece), lambda n: (0, n)),
        ),
        compiler_params=params(),
    )(grads, weights, normed)


def final_call(rows, gain, keep, from_core, from_pair, whole):
    part = pl.BlockSpec(rows.shape, lambda i: (0, 0))
    width = rows.shape[1]
    return pl.pallas_call(
        final_kernel,
        grid=(1,),
        out_shape=(
            jax.ShapeDtypeStruct(rows.shape, bf16),
            jax.ShapeDtypeStruct((3, width, HEAD), f32),
        ),
        in_specs=[
            part,
            pl.BlockSpec((1, width), lambda i: (0, 0)),
            part,
            part,
            part,
            pl.BlockSpec(whole.shape, lambda i: (0, 0, 0)),
        ],
        out_specs=(part, pl.BlockSpec((3, width, HEAD), lambda i: (0, 0, 0))),
        compiler_params=params(),
    )(rows, gain, keep, from_core, from_pair, whole)


def swap(x, axis):
    return lax.ppermute(x, axis, [(0, 1), (1, 0)])


def on_device(layer_input, grad_packed, source_row, window_id, w_qkv, gain):
    width = layer_input.shape[1]
    dp = lax.axis_index("y") * 4 + lax.axis_index("x")
    ring = lax.axis_index("zq")
    slot = lax.axis_index("zp") * 2 + lax.axis_index("core")
    place = jnp.stack([ring, slot]).astype(jnp.int32)
    gain_row = gain.reshape(1, width)

    packed = pack_call(grad_packed)
    flipped = jnp.swapaxes(w_qkv, 1, 2).reshape(3 * HEAD, width)
    flipped = jnp.pad(flipped, ((0, PADDED - 3 * HEAD), (0, 0)))
    share = lax.dynamic_slice(flipped, (16 * dp, 0), (16, width))
    others = [lax.ppermute(share, "zq", [(i, (i + k) % RING) for i in range(RING)]) for k in (3, 2, 1)]
    own = norm_call(layer_input, gain_row)
    others, packed, own = lax.optimization_barrier((others, packed, own))
    circle = jnp.concatenate([share] + others + [share] + others, axis=0)
    ordered = lax.dynamic_slice(circle, (16 * ((RING - ring) % RING), 0), (16 * RING, width))
    weights = lax.all_gather(ordered, ("y", "x"), axis=0, tiled=True)
    weights = weights.reshape(16, RING, 16, width)

    by_head = lax.all_to_all(packed, ("zq", "zp", "core"), split_axis=0, concat_axis=0)
    permuted = permute_call(place, source_row.reshape(-1), by_head)
    upstream = lax.all_to_all(permuted, "zq", split_axis=0, concat_axis=0)

    half = jnp.concatenate([own, swap(own, "zp")], axis=0)
    normed = jnp.concatenate([half, swap(half, "core")], axis=0)
    windows = window_id.reshape(32, 128).astype(f32)
    grads, weight_part = head_call(place, normed, normed.T, weights, upstream, windows)

    arrived = lax.all_to_all(weight_part, ("y", "x"), split_axis=0, concat_axis=0)
    summed = jnp.sum(arrived.astype(f32), axis=0).astype(bf16)
    keep, send, gain_part = back_call(grads, weights, normed)
    from_core = swap(send, "core")
    pair = (keep[CHUNK:] + from_core[CHUNK:].astype(f32)).astype(bf16)
    gain_part = gain_part + swap(gain_part, "core")
    gain_part = gain_part + swap(gain_part, "zp")
    beside = gain_part.reshape(width // 16, 16).astype(bf16)
    beside = jnp.broadcast_to(beside[None], (RING, width // 16, 16))
    message = jnp.concatenate([summed[..., : 3 * HEAD], beside], axis=2)
    message, pair = lax.optimization_barrier((message, pair))
    arrived = lax.all_to_all(message, "zq", split_axis=0, concat_axis=0)
    summed = jnp.sum(arrived.astype(f32), axis=0).astype(bf16)
    copies = jnp.broadcast_to(summed[None], (16,) + summed.shape)
    copies, pair = lax.optimization_barrier((copies, pair))
    from_pair = swap(pair, "zp")
    whole = lax.all_to_all(copies, ("y", "x"), split_axis=0, concat_axis=0)
    grad_gain = jnp.sum(whole[:, :, 3 * HEAD :].astype(f32), axis=0).reshape(width) / gain
    grad_input, grad_weight = final_call(
        layer_input, gain_row, keep, from_core, from_pair, whole
    )
    return (grad_input, grad_weight, grad_gain)


def solution(mesh):
    fine = Mesh(mesh.devices.reshape(4, 4, 4, 2, 2), ("y", "x", "zq", "zp", "core"))
    dp, group = ("y", "x"), ("zq", "zp", "core")
    rows = P(dp + group, None)
    return jax.shard_map(
        on_device,
        mesh=fine,
        in_specs=(rows, rows, P(dp, None), P(dp, None), P(None, None, group), P()),
        out_specs=(rows, P(None, None, group), P()),
        check_vma=False,
    )
```

```python
import functools

import jax
import jax.numpy as jnp
from jax import lax
from jax.experimental import pallas as pl
from jax.experimental.pallas import tpu as pltpu
from jax.sharding import Mesh, PartitionSpec as P

HEAD = 80
HEADS = 16
SUPER = 128
CHUNK = 256
SLOTS = 4
RING = 4
LINES = 160
PADDED = 256
XOR_ORDER = (0, 2, 1, 3)
epsilon = 1e-06
bf16 = jnp.bfloat16
f32 = jnp.float32
NT = (((1,), (1,)), ((), ()))
TN = (((0,), (0,)), ((), ()))
NN = (((1,), (0,)), ((), ()))
BIG = 58 * 1024 * 1024
SMALL = 20 * 1024 * 1024


def dot(a, b, dims):
    return lax.dot_general(a, b, dims, preferred_element_type=f32)


def lanes(shape):
    return lax.broadcasted_iota(jnp.int32, shape, len(shape) - 1)


def roll(x, shift):
    shift = shift % x.shape[-1]
    return x if shift == 0 else pltpu.roll(x, shift, x.ndim - 1)


def pack(rows):
    top = jnp.where(lanes((128, 128)) < 64, rows[:128], roll(rows[128:], 64))
    group = lanes((32, 128)) // 16
    low = roll(rows[:32], -64)
    for k in range(1, 8):
        low = jnp.where(group == k, roll(rows[32 * k : 32 * k + 32], 16 * k - 64), low)
    return top, low


def unpack(top, low, place):
    at = lanes((128, 128))
    upper = roll(top, place)
    lower = roll(top, place - 64)
    tail = [roll(low, place + 64 - 16 * k) for k in range(8)]
    first = jnp.concatenate(tail[:4], axis=0)
    second = jnp.concatenate(tail[4:], axis=0)
    wide = (at >= place) & (at < place + 64)
    rest = (at >= place + 64) & (at < place + HEAD)
    one = jnp.where(wide, upper, jnp.where(rest, first, 0.0))
    two = jnp.where(wide, lower, jnp.where(rest, second, 0.0))
    return one, two


def pack_kernel(rows_ref, out_ref):
    for g in range(HEADS):
        start = (HEAD * g) // 128 * 128
        shift = HEAD * g - start
        size = 128 if shift + HEAD <= 128 else 256
        window = rows_ref[:, start : start + size].astype(f32)
        window = roll(window, -shift)[:, :128]
        top, low = pack(window)
        out_ref[g, :128, :] = top.astype(bf16)
        out_ref[g, 128:, :] = low.astype(bf16)


def permute_kernel(place_ref, source_ref, in_ref, out_ref, table, picked):
    slot = place_ref[1]
    for src in range(HEADS):
        one, two = unpack(
            in_ref[src, :128, :].astype(f32), in_ref[src, 128:, :].astype(f32), 0
        )
        table[CHUNK * src : CHUNK * src + 128, :] = one
        table[CHUNK * src + 128 : CHUNK * src + 256, :] = two
    for q in range(RING):
        for o, off in enumerate(XOR_ORDER):
            base = q * SLOTS * CHUNK + (slot ^ off) * CHUNK

            def step(i, carry):
                at = i * 64
                for u in range(64):
                    row = source_ref[base + at + u]
                    picked[pl.ds(at + u, 1), :] = table[pl.ds(row, 1), :]
                return carry

            lax.fori_loop(0, CHUNK // 64, step, 0)
            top, low = pack(picked[...])
            out_ref[q, o, :128, :] = top.astype(bf16)
            out_ref[q, o, 128:, :] = low.astype(bf16)


def norm_kernel(rows_ref, gain_ref, out_ref):
    values = rows_ref[...].astype(f32)
    inverse = lax.rsqrt(jnp.mean(values * values, axis=-1, keepdims=True) + epsilon)
    out_ref[...] = (values * inverse * gain_ref[...]).astype(bf16)


def shifted(shape, move):
    row = lax.broadcasted_iota(jnp.int32, shape, 0)
    return jnp.where(move(row, lanes(shape)), 1.0, 0.0).astype(bf16)


def head_kernel(
    place_ref, normed_hbm, turned_hbm, w_hbm, up_ref, window_ref, grad_hbm, weight_hbm,
    first, second, key_at, query_at, upstream, same,
    normed_ref, turned_ref, w_ref, grad_ref, weight_ref, in_sems, out_sems,
):
    ring, slot = place_ref[0], place_ref[1]
    scaling = HEAD ** (-0.5)
    total_rows = SLOTS * CHUNK
    width = normed_ref.shape[-1]
    blocks = [slice(SUPER * b, SUPER * b + SUPER) for b in range(total_rows // SUPER)]
    w_copies = [
        pltpu.make_async_copy(w_hbm.at[:, h], w_ref.at[h], in_sems.at[h]) for h in range(RING)
    ]
    turned_copy = pltpu.make_async_copy(turned_hbm, turned_ref, in_sems.at[RING])
    normed_copy = pltpu.make_async_copy(normed_hbm, normed_ref, in_sems.at[RING + 1])
    w_copies[0].start()
    normed_copy.start()
    for h in range(1, RING):
        w_copies[h].start()
    turned_copy.start()
    grad_copies = [
        pltpu.make_async_copy(grad_ref.at[h], grad_hbm.at[h], out_sems.at[h])
        for h in range(RING)
    ]
    weight_copies = [
        pltpu.make_async_copy(weight_ref.at[h], weight_hbm.at[:, h], out_sems.at[RING + h])
        for h in range(RING)
    ]
    to_wide = shifted(
        (128, 128), lambda r, c: (c >= 32) & (c < 96) & (r % 64 == c - 32)
    )
    to_rest = shifted(
        (128, 128), lambda r, c: (c >= 96) & (c < 112) & (r % 16 == c - 96)
    )
    row = lax.broadcasted_iota(jnp.int32, (CHUNK, 128), 0)
    keep_wide = row // 128 == lanes((CHUNK, 128)) // 64
    keep_rest = row // 32 == lanes((CHUNK, 128)) // 16

    def project(h):
        w = w_ref[h].reshape(PADDED, width)
        low = dot(normed_ref[...], w, NT).astype(bf16)
        first[h] = low[:, :128]
        second[h] = low[:, 128:]
        rounded = low.astype(f32)
        at = lanes((total_rows, PADDED))
        key_at[h] = jnp.where(at < HEAD, roll(rounded, -HEAD), 0.0)[:, :128].astype(bf16)
        query_at[h] = jnp.where(
            (at >= HEAD) & (at < 2 * HEAD), roll(rounded, HEAD), 0.0
        ).astype(bf16)

    def spread(h):
        for c in range(SLOTS):
            top, low = up_ref[h, c, :128, :], up_ref[h, c, 128:, :]
            wide = jnp.where(keep_wide, jnp.concatenate([top] * 2, axis=0), 0.0)
            rest = jnp.where(keep_rest, jnp.concatenate([low] * 8, axis=0), 0.0)
            both = dot(wide.astype(bf16), to_wide, NN) + dot(rest.astype(bf16), to_rest, NN)
            upstream[h, CHUNK * c : CHUNK * c + CHUNK, :] = both.astype(bf16)

    def attend(h):
        scores = [dot(first[h, r, :], key_at[h, r, :], NT) for r in blocks]
        grad_probs = [dot(upstream[h, r, :], second[h, r, :], NT) for r in blocks]
        probs, grad_scores = [], []
        for b, r in enumerate(blocks):
            masked = scores[b] * scaling + same[r, :]
            powers = jnp.exp(masked - jnp.max(masked, axis=-1, keepdims=True))
            prob = powers * (1.0 / jnp.sum(powers, axis=-1, keepdims=True))
            row_dot = jnp.sum(prob * grad_probs[b], axis=-1, keepdims=True)
            grad_scores.append((prob * (grad_probs[b] - row_dot)).astype(bf16))
            probs.append(prob.astype(bf16))
        for b, r in enumerate(blocks):
            grad_query = dot(grad_scores[b], key_at[h, r, :], NN)
            grad_key = dot(grad_scores[b], query_at[h, r, :], TN)
            grad_value = dot(probs[b], upstream[h, r, :], TN)
            grad_ref[h, r, :128] = ((grad_query + grad_key[:, :128]) * scaling).astype(bf16)
            grad_ref[h, r, 128:] = (grad_key[:, 128:] * scaling + grad_value).astype(bf16)

    def weigh(h):
        part = dot(turned_ref[...], grad_ref[h], NN).astype(bf16)
        weight_ref[h] = part.reshape(16, width // 16, PADDED)

    for b, r in enumerate(blocks):
        line = ring * 8 + (slot ^ XOR_ORDER[b // 2]) * 2 + b % 2
        labels = jnp.broadcast_to(window_ref[pl.ds(line, 1), :], (SUPER, SUPER))
        same[r, :] = jnp.where(labels == labels.T, 0.0, -1e30)
    spread(0)
    w_copies[0].wait()
    normed_copy.wait()
    project(0)
    for copy in w_copies[1:] + [turned_copy]:
        copy.wait()
    for h in range(RING):
        if h + 1 < RING:
            project(h + 1)
            spread(h + 1)
        attend(h)
        weigh(h)
    for copy in weight_copies + grad_copies:
        copy.start()
    for copy in weight_copies + grad_copies:
        copy.wait()


def back_kernel(grad_ref, w_ref, normed_ref, out_ref, gain_ref):
    parts = [w_ref[:, h].reshape(PADDED, w_ref.shape[-1]) for h in range(RING)]
    grads = jnp.concatenate([grad_ref[h] for h in range(RING)], axis=1)
    total = dot(grads, jnp.concatenate(parts, axis=0), NN)
    out_ref[...] = total.astype(out_ref.dtype)
    gain_ref[...] = jnp.sum(total * normed_ref[...].astype(f32), axis=0, keepdims=True)


def turn_kernel(whole_ref, out_ref):
    whole = whole_ref[...].reshape(out_ref.shape[1], PADDED).astype(f32)
    out_ref[...] = whole.T[: 3 * HEAD]


def final_kernel(rows_ref, gain_ref, keep_ref, core_ref, pair_ref, out_ref):
    values = rows_ref[...].astype(f32)
    inverse = lax.rsqrt(jnp.mean(values * values, axis=-1, keepdims=True) + epsilon)
    scaled = values * inverse
    normed_grad = keep_ref[...] + core_ref[...].astype(f32) + pair_ref[...].astype(f32)
    grad_scaled = normed_grad * gain_ref[...]
    mixed = jnp.mean(grad_scaled * scaled, axis=-1, keepdims=True)
    out_ref[...] = (inverse * (grad_scaled - scaled * mixed)).astype(bf16)


def vmem():
    return pl.BlockSpec(memory_space=pltpu.VMEM)


def smem():
    return pl.BlockSpec(memory_space=pltpu.SMEM)


def params(limit=SMALL):
    return pltpu.CompilerParams(vmem_limit_bytes=limit)


def pack_call(rows):
    return pl.pallas_call(
        pack_kernel,
        out_shape=jax.ShapeDtypeStruct((HEADS, LINES, 128), bf16),
        in_specs=[vmem()],
        out_specs=vmem(),
        compiler_params=params(),
    )(rows)


def permute_call(place, source, received):
    return pl.pallas_call(
        permute_kernel,
        out_shape=jax.ShapeDtypeStruct((RING, SLOTS, LINES, 128), bf16),
        in_specs=[smem(), smem(), vmem()],
        out_specs=vmem(),
        scratch_shapes=[pltpu.VMEM((HEADS * CHUNK, 128), f32), pltpu.VMEM((CHUNK, 128), f32)],
        compiler_params=params(),
    )(place, source, received)


def norm_call(rows, gain):
    return pl.pallas_call(
        norm_kernel,
        out_shape=jax.ShapeDtypeStruct(rows.shape, bf16),
        in_specs=[vmem(), vmem()],
        out_specs=vmem(),
        compiler_params=params(),
    )(rows, gain)


def head_call(place, normed, turned, weights, upstream, windows):
    rows, width = normed.shape
    return pl.pallas_call(
        head_kernel,
        out_shape=(
            jax.ShapeDtypeStruct((RING, rows, PADDED), bf16),
            jax.ShapeDtypeStruct((16, RING, width // 16, PADDED), bf16),
        ),
        in_specs=[smem()] + [pl.BlockSpec(memory_space=pl.ANY)] * 3 + [vmem()] * 2,
        out_specs=(pl.BlockSpec(memory_space=pl.ANY),) * 2,
        scratch_shapes=[
            pltpu.VMEM((RING, rows, 128), bf16),
            pltpu.VMEM((RING, rows, 128), bf16),
            pltpu.VMEM((RING, rows, 128), bf16),
            pltpu.VMEM((RING, rows, PADDED), bf16),
            pltpu.VMEM((RING, rows, 128), bf16),
            pltpu.VMEM((rows, SUPER), f32),
            pltpu.VMEM((rows, width), bf16),
            pltpu.VMEM((width, rows), bf16),
            pltpu.VMEM((RING, 16, 16, width), bf16),
            pltpu.VMEM((RING, rows, PADDED), bf16),
            pltpu.VMEM((RING, 16, width // 16, PADDED), bf16),
            pltpu.SemaphoreType.DMA((RING + 2,)),
            pltpu.SemaphoreType.DMA((2 * RING,)),
        ],
        compiler_params=params(BIG),
    )(place, normed, turned, weights, upstream, windows)


def back_call(grads, weights, normed, half, dtype):
    rows, width = 2 * CHUNK, weights.shape[-1]
    piece = 256
    return pl.pallas_call(
        back_kernel,
        grid=(width // piece,),
        out_shape=(
            jax.ShapeDtypeStruct((rows, width), dtype),
            jax.ShapeDtypeStruct((1, width), f32),
        ),
        in_specs=[
            pl.BlockSpec((RING, rows, PADDED), lambda n: (0, half, 0)),
            pl.BlockSpec((16, RING, 16, piece), lambda n: (0, 0, 0, n)),
            pl.BlockSpec((rows, piece), lambda n: (half, n)),
        ],
        out_specs=(
            pl.BlockSpec((rows, piece), lambda n: (0, n)),
            pl.BlockSpec((1, piece), lambda n: (0, n)),
        ),
        compiler_params=params(BIG),
    )(grads, weights, normed)


def final_call(rows, gain, keep, from_core, from_pair):
    part = pl.BlockSpec(rows.shape, lambda i: (0, 0))
    return pl.pallas_call(
        final_kernel,
        grid=(1,),
        out_shape=jax.ShapeDtypeStruct(rows.shape, bf16),
        in_specs=[part, pl.BlockSpec(gain.shape, lambda i: (0, 0)), part, part, part],
        out_specs=part,
        compiler_params=params(BIG),
    )(rows, gain, keep, from_core, from_pair)


def turn_call(whole):
    width = whole.shape[0] * whole.shape[1]
    return pl.pallas_call(
        turn_kernel,
        out_shape=jax.ShapeDtypeStruct((3 * HEAD, width), f32),
        in_specs=[vmem()],
        out_specs=vmem(),
        compiler_params=params(BIG),
    )(whole)


def swap(x, axis):
    return lax.ppermute(x, axis, [(0, 1), (1, 0)])


def on_device(layer_input, grad_packed, source_row, window_id, w_qkv, gain):
    width = layer_input.shape[1]
    dp = lax.axis_index("y") * 4 + lax.axis_index("x")
    ring = lax.axis_index("zq")
    slot = lax.axis_index("zp") * 2 + lax.axis_index("core")
    place = jnp.stack([ring, slot]).astype(jnp.int32)
    gain_row = gain.reshape(1, width)

    packed = pack_call(grad_packed)
    flipped = jnp.swapaxes(w_qkv, 1, 2).reshape(3 * HEAD, width)
    flipped = jnp.pad(flipped, ((0, PADDED - 3 * HEAD), (0, 0)))
    share = lax.dynamic_slice(flipped, (16 * dp, 0), (16, width))
    others = [lax.ppermute(share, "zq", [(i, (i + k) % RING) for i in range(RING)]) for k in (3, 2, 1)]
    own = norm_call(layer_input, gain_row)
    others, packed, own = lax.optimization_barrier((others, packed, own))
    circle = jnp.concatenate([share] + others + [share] + others, axis=0)
    ordered = lax.dynamic_slice(circle, (16 * ((RING - ring) % RING), 0), (16 * RING, width))
    weights = lax.all_gather(ordered, ("y", "x"), axis=0, tiled=True)
    weights = weights.reshape(16, RING, 16, width)

    by_head = lax.all_to_all(packed, ("zq", "zp", "core"), split_axis=0, concat_axis=0)
    permuted = permute_call(place, source_row.reshape(-1), by_head)
    upstream = lax.all_to_all(permuted, "zq", split_axis=0, concat_axis=0)

    half = jnp.concatenate([own, swap(own, "zp")], axis=0)
    normed = jnp.concatenate([half, swap(half, "core")], axis=0)
    windows = window_id.reshape(32, 128).astype(f32)
    grads, weight_part = head_call(place, normed, normed.T, weights, upstream, windows)

    arrived = lax.all_to_all(weight_part, ("y", "x"), split_axis=0, concat_axis=0)
    summed = jnp.sum(arrived.astype(f32), axis=0).astype(bf16)
    send, gain_send = back_call(grads, weights, normed, 1, bf16)
    keep, gain_keep = back_call(grads, weights, normed, 0, f32)
    gain_part = gain_send + gain_keep
    from_core = swap(send, "core")
    pair = (keep[CHUNK:] + from_core[CHUNK:].astype(f32)).astype(bf16)
    gain_part = gain_part + swap(gain_part, "core")
    gain_part = gain_part + swap(gain_part, "zp")
    beside = gain_part.reshape(width // 16, 16).astype(bf16)
    beside = jnp.broadcast_to(beside[None], (RING, width // 16, 16))
    message = jnp.concatenate([summed[..., : 3 * HEAD], beside], axis=2)
    from_pair = swap(pair, "zp")
    message, from_pair = lax.optimization_barrier((message, from_pair))
    arrived = lax.all_to_all(message, "zq", split_axis=0, concat_axis=0)
    summed = jnp.sum(arrived.astype(f32), axis=0).astype(bf16)
    copies = jnp.broadcast_to(summed[None], (16,) + summed.shape)
    whole = lax.all_to_all(copies, ("y", "x"), split_axis=0, concat_axis=0)
    grad_gain = jnp.sum(whole[:, :, 3 * HEAD :].astype(f32), axis=0).reshape(width) / gain
    grad_weight = jnp.swapaxes(turn_call(whole).reshape(3, HEAD, width), 1, 2)
    grad_input = final_call(layer_input, gain_row, keep, from_core, from_pair)
    return (grad_input, grad_weight, grad_gain)


def solution(mesh):
    fine = Mesh(mesh.devices.reshape(4, 4, 4, 2, 2), ("y", "x", "zq", "zp", "core"))
    dp, group = ("y", "x"), ("zq", "zp", "core")
    rows = P(dp + group, None)
    return jax.shard_map(
        on_device,
        mesh=fine,
        in_specs=(rows, rows, P(dp, None), P(dp, None), P(None, None, group), P()),
        out_specs=(rows, P(None, None, group), P()),
        check_vma=False,
    )
```

```python
import functools

import jax
import jax.numpy as jnp
from jax import lax
from jax.experimental import pallas as pl
from jax.experimental.pallas import tpu as pltpu
from jax.sharding import Mesh, PartitionSpec as P

HEAD = 80
HEADS = 16
SUPER = 128
CHUNK = 256
SLOTS = 4
RING = 4
LINES = 160
PADDED = 256
XOR_ORDER = (0, 2, 1, 3)
epsilon = 1e-06
bf16 = jnp.bfloat16
f32 = jnp.float32
NT = (((1,), (1,)), ((), ()))
TN = (((0,), (0,)), ((), ()))
NN = (((1,), (0,)), ((), ()))
BIG = 58 * 1024 * 1024
SMALL = 20 * 1024 * 1024


def dot(a, b, dims):
    return lax.dot_general(a, b, dims, preferred_element_type=f32)


def lanes(shape):
    return lax.broadcasted_iota(jnp.int32, shape, len(shape) - 1)


def roll(x, shift):
    shift = shift % x.shape[-1]
    return x if shift == 0 else pltpu.roll(x, shift, x.ndim - 1)


def pack(rows):
    top = jnp.where(lanes((128, 128)) < 64, rows[:128], roll(rows[128:], 64))
    group = lanes((32, 128)) // 16
    low = roll(rows[:32], -64)
    for k in range(1, 8):
        low = jnp.where(group == k, roll(rows[32 * k : 32 * k + 32], 16 * k - 64), low)
    return top, low


def unpack(top, low, place):
    at = lanes((128, 128))
    upper = roll(top, place)
    lower = roll(top, place - 64)
    tail = [roll(low, place + 64 - 16 * k) for k in range(8)]
    first = jnp.concatenate(tail[:4], axis=0)
    second = jnp.concatenate(tail[4:], axis=0)
    wide = (at >= place) & (at < place + 64)
    rest = (at >= place + 64) & (at < place + HEAD)
    one = jnp.where(wide, upper, jnp.where(rest, first, 0.0))
    two = jnp.where(wide, lower, jnp.where(rest, second, 0.0))
    return one, two


def pack_kernel(rows_ref, out_ref):
    for g in range(HEADS):
        start = (HEAD * g) // 128 * 128
        shift = HEAD * g - start
        size = 128 if shift + HEAD <= 128 else 256
        window = rows_ref[:, start : start + size].astype(f32)
        window = roll(window, -shift)[:, :128]
        top, low = pack(window)
        out_ref[g, :128, :] = top.astype(bf16)
        out_ref[g, 128:, :] = low.astype(bf16)


def permute_kernel(place_ref, source_ref, in_ref, out_ref, table, picked):
    slot = place_ref[1]
    for src in range(HEADS):
        one, two = unpack(
            in_ref[src, :128, :].astype(f32), in_ref[src, 128:, :].astype(f32), 0
        )
        table[CHUNK * src : CHUNK * src + 128, :] = one
        table[CHUNK * src + 128 : CHUNK * src + 256, :] = two
    for q in range(RING):
        for o, off in enumerate(XOR_ORDER):
            base = q * SLOTS * CHUNK + (slot ^ off) * CHUNK

            def step(i, carry):
                at = i * 64
                for u in range(64):
                    row = source_ref[base + at + u]
                    picked[pl.ds(at + u, 1), :] = table[pl.ds(row, 1), :]
                return carry

            lax.fori_loop(0, CHUNK // 64, step, 0)
            top, low = pack(picked[...])
            out_ref[q, o, :128, :] = top.astype(bf16)
            out_ref[q, o, 128:, :] = low.astype(bf16)


def norm_kernel(rows_ref, gain_ref, out_ref):
    values = rows_ref[...].astype(f32)
    inverse = lax.rsqrt(jnp.mean(values * values, axis=-1, keepdims=True) + epsilon)
    out_ref[...] = (values * inverse * gain_ref[...]).astype(bf16)


def shifted(shape, move):
    row = lax.broadcasted_iota(jnp.int32, shape, 0)
    return jnp.where(move(row, lanes(shape)), 1.0, 0.0).astype(bf16)


def gather_kernel(half_ref, core_ref, out_ref, turned_ref):
    for c, part in enumerate((half_ref, core_ref)):
        rows = slice(2 * CHUNK * c, 2 * CHUNK * c + 2 * CHUNK)
        out_ref[rows, :] = part[...]
        turned_ref[:, rows] = part[...].T


def blocks_of(total_rows):
    return [slice(SUPER * b, SUPER * b + SUPER) for b in range(total_rows // SUPER)]


def forward_kernel(
    place_ref, normed_hbm, w_hbm, window_ref, second_hbm, key_hbm, query_hbm, probs_hbm,
    second, key_at, query_at, probs, first, same, normed_ref, w_ref, in_sems, out_sems,
):
    ring, slot = place_ref[0], place_ref[1]
    scaling = HEAD ** (-0.5)
    total_rows, width = normed_ref.shape
    blocks = blocks_of(total_rows)
    copies = [pltpu.make_async_copy(normed_hbm, normed_ref, in_sems.at[RING])] + [
        pltpu.make_async_copy(w_hbm.at[:, h], w_ref.at[h], in_sems.at[h]) for h in range(RING)
    ]
    for copy in copies:
        copy.start()
    for b, r in enumerate(blocks):
        line = ring * 8 + (slot ^ XOR_ORDER[b // 2]) * 2 + b % 2
        labels = jnp.broadcast_to(window_ref[pl.ds(line, 1), :], (SUPER, SUPER))
        same[r, :] = jnp.where(labels == labels.T, 0.0, -1e30)
    for copy in copies:
        copy.wait()

    def project(h):
        w = w_ref[h].reshape(PADDED, width)
        low = dot(normed_ref[...], w, NT).astype(bf16)
        first[h] = low[:, :128]
        second[h] = low[:, 128:]
        rounded = low.astype(f32)
        at = lanes((total_rows, PADDED))
        key_at[h] = jnp.where(at < HEAD, roll(rounded, -HEAD), 0.0)[:, :128].astype(bf16)
        query_at[h] = jnp.where(
            (at >= HEAD) & (at < 2 * HEAD), roll(rounded, HEAD), 0.0
        ).astype(bf16)

    def soften(h):
        scores = [dot(first[h, r, :], key_at[h, r, :], NT) for r in blocks]
        for b, r in enumerate(blocks):
            masked = scores[b] * scaling + same[r, :]
            powers = jnp.exp(masked - jnp.max(masked, axis=-1, keepdims=True))
            probs[h, r, :] = powers * (1.0 / jnp.sum(powers, axis=-1, keepdims=True))

    project(0)
    for h in range(RING):
        if h + 1 < RING:
            project(h + 1)
        soften(h)
    copies = [
        pltpu.make_async_copy(src, dst, out_sems.at[i])
        for i, (src, dst) in enumerate(
            ((second, second_hbm), (key_at, key_hbm), (query_at, query_hbm), (probs, probs_hbm))
        )
    ]
    for copy in copies:
        copy.start()
    for copy in copies:
        copy.wait()


def head_kernel(
    turned_hbm, up_ref, second_hbm, key_hbm, query_hbm, probs_hbm, grad_hbm, weight_hbm,
    second, key_at, query_at, probs, upstream, turned_ref, grad_ref, weight_ref,
    in_sems, out_sems,
):
    scaling = HEAD ** (-0.5)
    width, total_rows = turned_ref.shape
    blocks = blocks_of(total_rows)
    copies = [
        pltpu.make_async_copy(src, dst, in_sems.at[i])
        for i, (src, dst) in enumerate(
            (
                (second_hbm, second), (probs_hbm, probs), (key_hbm, key_at),
                (query_hbm, query_at), (turned_hbm, turned_ref),
            )
        )
    ]
    for copy in copies:
        copy.start()
    to_wide = shifted(
        (128, 128), lambda r, c: (c >= 32) & (c < 96) & (r % 64 == c - 32)
    )
    to_rest = shifted(
        (128, 128), lambda r, c: (c >= 96) & (c < 112) & (r % 16 == c - 96)
    )
    row = lax.broadcasted_iota(jnp.int32, (CHUNK, 128), 0)
    keep_wide = row // 128 == lanes((CHUNK, 128)) // 64
    keep_rest = row // 32 == lanes((CHUNK, 128)) // 16

    def spread(h):
        for c in range(SLOTS):
            top, low = up_ref[h, c, :128, :], up_ref[h, c, 128:, :]
            wide = jnp.where(keep_wide, jnp.concatenate([top] * 2, axis=0), 0.0)
            rest = jnp.where(keep_rest, jnp.concatenate([low] * 8, axis=0), 0.0)
            both = dot(wide.astype(bf16), to_wide, NN) + dot(rest.astype(bf16), to_rest, NN)
            upstream[h, CHUNK * c : CHUNK * c + CHUNK, :] = both.astype(bf16)

    def attend(h):
        grad_probs = [dot(upstream[h, r, :], second[h, r, :], NT) for r in blocks]
        grad_scores, probs_low = [], []
        for b, r in enumerate(blocks):
            prob = probs[h, r, :]
            row_dot = jnp.sum(prob * grad_probs[b], axis=-1, keepdims=True)
            grad_scores.append((prob * (grad_probs[b] - row_dot)).astype(bf16))
            probs_low.append(prob.astype(bf16))
        for b, r in enumerate(blocks):
            grad_query = dot(grad_scores[b], key_at[h, r, :], NN)
            grad_key = dot(grad_scores[b], query_at[h, r, :], TN)
            grad_value = dot(probs_low[b], upstream[h, r, :], TN)
            grad_ref[h, r, :128] = ((grad_query + grad_key[:, :128]) * scaling).astype(bf16)
            grad_ref[h, r, 128:] = (grad_key[:, 128:] * scaling + grad_value).astype(bf16)

    def weigh(h):
        part = dot(turned_ref[...], grad_ref[h], NN).astype(bf16)
        weight_ref[h] = part.reshape(16, width // 16, PADDED)

    for h in range(RING):
        spread(h)
    for copy in copies:
        copy.wait()
    attend(0)
    for h in range(RING):
        if h + 1 < RING:
            attend(h + 1)
        weigh(h)
    copies = [pltpu.make_async_copy(grad_ref, grad_hbm, out_sems.at[RING])] + [
        pltpu.make_async_copy(weight_ref.at[h], weight_hbm.at[:, h], out_sems.at[h])
        for h in range(RING)
    ]
    for copy in copies:
        copy.start()
    for copy in copies:
        copy.wait()


def back_kernel(grad_ref, w_ref, normed_ref, out_ref, gain_ref):
    parts = [w_ref[:, h].reshape(PADDED, w_ref.shape[-1]) for h in range(RING)]
    grads = jnp.concatenate([grad_ref[h] for h in range(RING)], axis=1)
    total = dot(grads, jnp.concatenate(parts, axis=0), NN)
    out_ref[...] = total.astype(out_ref.dtype)
    gain_ref[...] = jnp.sum(total * normed_ref[...].astype(f32), axis=0, keepdims=True)


def turn_kernel(whole_ref, out_ref):
    whole = whole_ref[...].reshape(out_ref.shape[1], PADDED).astype(f32)
    out_ref[...] = whole.T[: 3 * HEAD]


def final_kernel(rows_ref, gain_ref, keep_ref, core_ref, pair_ref, out_ref):
    values = rows_ref[...].astype(f32)
    inverse = lax.rsqrt(jnp.mean(values * values, axis=-1, keepdims=True) + epsilon)
    scaled = values * inverse
    normed_grad = keep_ref[...] + core_ref[...].astype(f32) + pair_ref[...].astype(f32)
    grad_scaled = normed_grad * gain_ref[...]
    mixed = jnp.mean(grad_scaled * scaled, axis=-1, keepdims=True)
    out_ref[...] = (inverse * (grad_scaled - scaled * mixed)).astype(bf16)


def vmem():
    return pl.BlockSpec(memory_space=pltpu.VMEM)


def smem():
    return pl.BlockSpec(memory_space=pltpu.SMEM)


def params(limit=SMALL):
    return pltpu.CompilerParams(vmem_limit_bytes=limit)


def pack_call(rows):
    return pl.pallas_call(
        pack_kernel,
        out_shape=jax.ShapeDtypeStruct((HEADS, LINES, 128), bf16),
        in_specs=[vmem()],
        out_specs=vmem(),
        compiler_params=params(),
    )(rows)


def permute_call(place, source, received):
    return pl.pallas_call(
        permute_kernel,
        out_shape=jax.ShapeDtypeStruct((RING, SLOTS, LINES, 128), bf16),
        in_specs=[smem(), smem(), vmem()],
        out_specs=vmem(),
        scratch_shapes=[pltpu.VMEM((HEADS * CHUNK, 128), f32), pltpu.VMEM((CHUNK, 128), f32)],
        compiler_params=params(),
    )(place, source, received)


def norm_call(rows, gain):
    return pl.pallas_call(
        norm_kernel,
        out_shape=jax.ShapeDtypeStruct(rows.shape, bf16),
        in_specs=[vmem(), vmem()],
        out_specs=vmem(),
        compiler_params=params(),
    )(rows, gain)


def gather_call(half, core):
    rows, width = 2 * half.shape[0], half.shape[1]
    return pl.pallas_call(
        gather_kernel,
        out_shape=(
            jax.ShapeDtypeStruct((rows, width), bf16),
            jax.ShapeDtypeStruct((width, rows), bf16),
        ),
        in_specs=[vmem(), vmem()],
        out_specs=(vmem(), vmem()),
        compiler_params=params(BIG),
    )(half, core)


def hbm():
    return pl.BlockSpec(memory_space=pl.ANY)


def kept(rows):
    return (
        ((RING, rows, 128), bf16),
        ((RING, rows, 128), bf16),
        ((RING, rows, PADDED), bf16),
        ((RING, rows, SUPER), f32),
    )


def forward_call(place, normed, weights, windows):
    rows, width = normed.shape
    return pl.pallas_call(
        forward_kernel,
        out_shape=tuple(jax.ShapeDtypeStruct(*each) for each in kept(rows)),
        in_specs=[smem(), hbm(), hbm(), vmem()],
        out_specs=(hbm(),) * 4,
        scratch_shapes=[pltpu.VMEM(*each) for each in kept(rows)]
        + [
            pltpu.VMEM((RING, rows, 128), bf16),
            pltpu.VMEM((rows, SUPER), f32),
            pltpu.VMEM((rows, width), bf16),
            pltpu.VMEM((RING, 16, 16, width), bf16),
            pltpu.SemaphoreType.DMA((RING + 1,)),
            pltpu.SemaphoreType.DMA((4,)),
        ],
        compiler_params=params(BIG),
    )(place, normed, weights, windows)


def head_call(turned, upstream, forward):
    width, rows = turned.shape
    return pl.pallas_call(
        head_kernel,
        out_shape=(
            jax.ShapeDtypeStruct((RING, rows, PADDED), bf16),
            jax.ShapeDtypeStruct((16, RING, width // 16, PADDED), bf16),
        ),
        in_specs=[hbm(), vmem()] + [hbm()] * 4,
        out_specs=(hbm(),) * 2,
        scratch_shapes=[pltpu.VMEM(*each) for each in kept(rows)]
        + [
            pltpu.VMEM((RING, rows, 128), bf16),
            pltpu.VMEM((width, rows), bf16),
            pltpu.VMEM((RING, rows, PADDED), bf16),
            pltpu.VMEM((RING, 16, width // 16, PADDED), bf16),
            pltpu.SemaphoreType.DMA((5,)),
            pltpu.SemaphoreType.DMA((RING + 1,)),
        ],
        compiler_params=params(BIG),
    )(turned, upstream, *forward)


def back_call(grads, weights, normed, half, dtype):
    rows, width = 2 * CHUNK, weights.shape[-1]
    piece = 256
    return pl.pallas_call(
        back_kernel,
        grid=(width // piece,),
        out_shape=(
            jax.ShapeDtypeStruct((rows, width), dtype),
            jax.ShapeDtypeStruct((1, width), f32),
        ),
        in_specs=[
            pl.BlockSpec((RING, rows, PADDED), lambda n: (0, half, 0)),
            pl.BlockSpec((16, RING, 16, piece), lambda n: (0, 0, 0, n)),
            pl.BlockSpec((rows, piece), lambda n: (half, n)),
        ],
        out_specs=(
            pl.BlockSpec((rows, piece), lambda n: (0, n)),
            pl.BlockSpec((1, piece), lambda n: (0, n)),
        ),
        compiler_params=params(BIG),
    )(grads, weights, normed)


def final_call(rows, gain, keep, from_core, from_pair):
    part = pl.BlockSpec(rows.shape, lambda i: (0, 0))
    return pl.pallas_call(
        final_kernel,
        grid=(1,),
        out_shape=jax.ShapeDtypeStruct(rows.shape, bf16),
        in_specs=[part, pl.BlockSpec(gain.shape, lambda i: (0, 0)), part, part, part],
        out_specs=part,
        compiler_params=params(BIG),
    )(rows, gain, keep, from_core, from_pair)


def turn_call(whole):
    width = whole.shape[0] * whole.shape[1]
    return pl.pallas_call(
        turn_kernel,
        out_shape=jax.ShapeDtypeStruct((3 * HEAD, width), f32),
        in_specs=[vmem()],
        out_specs=vmem(),
        compiler_params=params(BIG),
    )(whole)


def swap(x, axis):
    return lax.ppermute(x, axis, [(0, 1), (1, 0)])


def on_device(layer_input, grad_packed, source_row, window_id, w_qkv, gain):
    width = layer_input.shape[1]
    dp = lax.axis_index("y") * 4 + lax.axis_index("x")
    ring = lax.axis_index("zq")
    slot = lax.axis_index("zp") * 2 + lax.axis_index("core")
    place = jnp.stack([ring, slot]).astype(jnp.int32)
    gain_row = gain.reshape(1, width)

    packed = pack_call(grad_packed)
    flipped = jnp.swapaxes(w_qkv, 1, 2).reshape(3 * HEAD, width)
    flipped = jnp.pad(flipped, ((0, PADDED - 3 * HEAD), (0, 0)))
    share = lax.dynamic_slice(flipped, (16 * dp, 0), (16, width))
    others = [lax.ppermute(share, "zq", [(i, (i + k) % RING) for i in range(RING)]) for k in (3, 2, 1)]
    own = norm_call(layer_input, gain_row)
    others, packed, own = lax.optimization_barrier((others, packed, own))
    circle = jnp.concatenate([share] + others + [share] + others, axis=0)
    ordered = lax.dynamic_slice(circle, (16 * ((RING - ring) % RING), 0), (16 * RING, width))
    weights = lax.all_gather(ordered, ("y", "x"), axis=0, tiled=True)
    weights = weights.reshape(16, RING, 16, width)

    by_head = lax.all_to_all(packed, ("zq", "zp", "core"), split_axis=0, concat_axis=0)
    permuted = permute_call(place, source_row.reshape(-1), by_head)
    upstream = lax.all_to_all(permuted, "zq", split_axis=0, concat_axis=0)

    half = jnp.concatenate([own, swap(own, "zp")], axis=0)
    normed, turned = gather_call(half, swap(half, "core"))
    windows = window_id.reshape(32, 128).astype(f32)
    forward = forward_call(place, normed, weights, windows)
    grads, weight_part = head_call(turned, upstream, forward)

    arrived = lax.all_to_all(weight_part, ("y", "x"), split_axis=0, concat_axis=0)
    summed = jnp.sum(arrived.astype(f32), axis=0).astype(bf16)
    send, gain_send = back_call(grads, weights, normed, 1, bf16)
    keep, gain_keep = back_call(grads, weights, normed, 0, f32)
    gain_part = gain_send + gain_keep
    from_core = swap(send, "core")
    pair = (keep[CHUNK:] + from_core[CHUNK:].astype(f32)).astype(bf16)
    gain_part = gain_part + swap(gain_part, "core")
    gain_part = gain_part + swap(gain_part, "zp")
    beside = gain_part.reshape(width // 16, 16).astype(bf16)
    beside = jnp.broadcast_to(beside[None], (RING, width // 16, 16))
    message = jnp.concatenate([summed[..., : 3 * HEAD], beside], axis=2)
    from_pair = swap(pair, "zp")
    message, from_pair = lax.optimization_barrier((message, from_pair))
    arrived = lax.all_to_all(message, "zq", split_axis=0, concat_axis=0)
    summed = jnp.sum(arrived.astype(f32), axis=0).astype(bf16)
    copies = jnp.broadcast_to(summed[None], (16,) + summed.shape)
    whole = lax.all_to_all(copies, ("y", "x"), split_axis=0, concat_axis=0)
    grad_gain = jnp.sum(whole[:, :, 3 * HEAD :].astype(f32), axis=0).reshape(width) / gain
    grad_weight = jnp.swapaxes(turn_call(whole).reshape(3, HEAD, width), 1, 2)
    grad_input = final_call(layer_input, gain_row, keep, from_core, from_pair)
    return (grad_input, grad_weight, grad_gain)


def solution(mesh):
    fine = Mesh(mesh.devices.reshape(4, 4, 4, 2, 2), ("y", "x", "zq", "zp", "core"))
    dp, group = ("y", "x"), ("zq", "zp", "core")
    rows = P(dp + group, None)
    return jax.shard_map(
        on_device,
        mesh=fine,
        in_specs=(rows, rows, P(dp, None), P(dp, None), P(None, None, group), P()),
        out_specs=(rows, P(None, None, group), P()),
        check_vma=False,
    )
```

```python
import functools

import jax
import jax.numpy as jnp
from jax import lax
from jax.experimental import pallas as pl
from jax.experimental.pallas import tpu as pltpu
from jax.sharding import Mesh, PartitionSpec as P

HEAD = 80
HEADS = 16
SUPER = 128
CHUNK = 256
SLOTS = 4
RING = 4
LINES = 160
PADDED = 256
XOR_ORDER = (0, 2, 1, 3)
epsilon = 1e-06
bf16 = jnp.bfloat16
f32 = jnp.float32
NT = (((1,), (1,)), ((), ()))
TN = (((0,), (0,)), ((), ()))
NN = (((1,), (0,)), ((), ()))
BIG = 58 * 1024 * 1024
SMALL = 20 * 1024 * 1024


def dot(a, b, dims):
    return lax.dot_general(a, b, dims, preferred_element_type=f32)


def lanes(shape):
    return lax.broadcasted_iota(jnp.int32, shape, len(shape) - 1)


def roll(x, shift):
    shift = shift % x.shape[-1]
    return x if shift == 0 else pltpu.roll(x, shift, x.ndim - 1)


def pack(rows):
    top = jnp.where(lanes((128, 128)) < 64, rows[:128], roll(rows[128:], 64))
    group = lanes((32, 128)) // 16
    low = roll(rows[:32], -64)
    for k in range(1, 8):
        low = jnp.where(group == k, roll(rows[32 * k : 32 * k + 32], 16 * k - 64), low)
    return top, low


def unpack(top, low, place):
    at = lanes((128, 128))
    upper = roll(top, place)
    lower = roll(top, place - 64)
    tail = [roll(low, place + 64 - 16 * k) for k in range(8)]
    first = jnp.concatenate(tail[:4], axis=0)
    second = jnp.concatenate(tail[4:], axis=0)
    wide = (at >= place) & (at < place + 64)
    rest = (at >= place + 64) & (at < place + HEAD)
    one = jnp.where(wide, upper, jnp.where(rest, first, 0.0))
    two = jnp.where(wide, lower, jnp.where(rest, second, 0.0))
    return one, two


def pack_kernel(rows_ref, out_ref):
    for g in range(HEADS):
        start = (HEAD * g) // 128 * 128
        shift = HEAD * g - start
        size = 128 if shift + HEAD <= 128 else 256
        window = rows_ref[:, start : start + size].astype(f32)
        window = roll(window, -shift)[:, :128]
        top, low = pack(window)
        out_ref[g, :128, :] = top.astype(bf16)
        out_ref[g, 128:, :] = low.astype(bf16)


def permute_kernel(place_ref, source_ref, in_ref, out_ref, table, picked):
    slot = place_ref[1]
    for src in range(HEADS):
        one, two = unpack(
            in_ref[src, :128, :].astype(f32), in_ref[src, 128:, :].astype(f32), 0
        )
        table[CHUNK * src : CHUNK * src + 128, :] = one
        table[CHUNK * src + 128 : CHUNK * src + 256, :] = two
    for q in range(RING):
        for o, off in enumerate(XOR_ORDER):
            base = q * SLOTS * CHUNK + (slot ^ off) * CHUNK

            def step(i, carry):
                at = i * 64
                for u in range(64):
                    row = source_ref[base + at + u]
                    picked[pl.ds(at + u, 1), :] = table[pl.ds(row, 1), :]
                return carry

            lax.fori_loop(0, CHUNK // 64, step, 0)
            top, low = pack(picked[...])
            out_ref[q, o, :128, :] = top.astype(bf16)
            out_ref[q, o, 128:, :] = low.astype(bf16)


def norm_kernel(rows_ref, gain_ref, out_ref):
    values = rows_ref[...].astype(f32)
    inverse = lax.rsqrt(jnp.mean(values * values, axis=-1, keepdims=True) + epsilon)
    out_ref[...] = (values * inverse * gain_ref[...]).astype(bf16)


def shifted(shape, move):
    row = lax.broadcasted_iota(jnp.int32, shape, 0)
    return jnp.where(move(row, lanes(shape)), 1.0, 0.0).astype(bf16)


def gather_kernel(half_ref, core_ref, out_ref, turned_ref):
    for c, part in enumerate((half_ref, core_ref)):
        rows = slice(2 * CHUNK * c, 2 * CHUNK * c + 2 * CHUNK)
        out_ref[rows, :] = part[...]
        turned_ref[:, rows] = part[...].T


def blocks_of(total_rows):
    return [slice(SUPER * b, SUPER * b + SUPER) for b in range(total_rows // SUPER)]


def forward_kernel(
    place_ref, normed_hbm, w_hbm, window_ref, second_hbm, key_hbm, query_hbm, probs_hbm,
    second, key_at, query_at, probs, first, same, normed_ref, w_ref, in_sems, out_sems,
):
    ring, slot = place_ref[0], place_ref[1]
    scaling = HEAD ** (-0.5)
    total_rows, width = normed_ref.shape
    blocks = blocks_of(total_rows)
    copies = [pltpu.make_async_copy(normed_hbm, normed_ref, in_sems.at[RING])] + [
        pltpu.make_async_copy(w_hbm.at[:, h], w_ref.at[h], in_sems.at[h]) for h in range(RING)
    ]
    for copy in copies:
        copy.start()
    for b, r in enumerate(blocks):
        line = ring * 8 + (slot ^ XOR_ORDER[b // 2]) * 2 + b % 2
        labels = jnp.broadcast_to(window_ref[pl.ds(line, 1), :], (SUPER, SUPER))
        same[r, :] = jnp.where(labels == labels.T, 0.0, -1e30)
    for copy in copies:
        copy.wait()

    def project(h):
        w = w_ref[h].reshape(PADDED, width)
        low = dot(normed_ref[...], w, NT).astype(bf16)
        first[h] = low[:, :128]
        second[h] = low[:, 128:]
        rounded = low.astype(f32)
        at = lanes((total_rows, PADDED))
        key_at[h] = jnp.where(at < HEAD, roll(rounded, -HEAD), 0.0)[:, :128].astype(bf16)
        query_at[h] = jnp.where(
            (at >= HEAD) & (at < 2 * HEAD), roll(rounded, HEAD), 0.0
        ).astype(bf16)

    def soften(h):
        scores = [dot(first[h, r, :], key_at[h, r, :], NT) for r in blocks]
        for b, r in enumerate(blocks):
            masked = scores[b] * scaling + same[r, :]
            powers = jnp.exp(masked - jnp.max(masked, axis=-1, keepdims=True))
            probs[h, r, :] = powers * (1.0 / jnp.sum(powers, axis=-1, keepdims=True))

    copies = [
        pltpu.make_async_copy(src, dst, out_sems.at[i])
        for i, (src, dst) in enumerate(
            ((second, second_hbm), (key_at, key_hbm), (query_at, query_hbm), (probs, probs_hbm))
        )
    ]
    project(0)
    for h in range(RING):
        if h + 1 < RING:
            project(h + 1)
        else:
            for copy in copies[:3]:
                copy.start()
        soften(h)
    copies[3].start()
    for copy in copies:
        copy.wait()


def head_kernel(
    turned_hbm, up_ref, second_hbm, key_hbm, query_hbm, probs_hbm, grad_hbm, weight_hbm,
    second, key_at, query_at, probs, upstream, turned_ref, grad_ref, weight_ref,
    in_sems, out_sems,
):
    scaling = HEAD ** (-0.5)
    width, total_rows = turned_ref.shape
    blocks = blocks_of(total_rows)
    copies = [
        pltpu.make_async_copy(src, dst, in_sems.at[i])
        for i, (src, dst) in enumerate(
            (
                (second_hbm, second), (probs_hbm, probs), (key_hbm, key_at),
                (query_hbm, query_at), (turned_hbm, turned_ref),
            )
        )
    ]
    for copy in copies:
        copy.start()
    to_wide = shifted(
        (128, 128), lambda r, c: (c >= 32) & (c < 96) & (r % 64 == c - 32)
    )
    to_rest = shifted(
        (128, 128), lambda r, c: (c >= 96) & (c < 112) & (r % 16 == c - 96)
    )
    row = lax.broadcasted_iota(jnp.int32, (CHUNK, 128), 0)
    keep_wide = row // 128 == lanes((CHUNK, 128)) // 64
    keep_rest = row // 32 == lanes((CHUNK, 128)) // 16

    def spread(h):
        for c in range(SLOTS):
            top, low = up_ref[h, c, :128, :], up_ref[h, c, 128:, :]
            wide = jnp.where(keep_wide, jnp.concatenate([top] * 2, axis=0), 0.0)
            rest = jnp.where(keep_rest, jnp.concatenate([low] * 8, axis=0), 0.0)
            both = dot(wide.astype(bf16), to_wide, NN) + dot(rest.astype(bf16), to_rest, NN)
            upstream[h, CHUNK * c : CHUNK * c + CHUNK, :] = both.astype(bf16)

    def attend(h):
        grad_probs = [dot(upstream[h, r, :], second[h, r, :], NT) for r in blocks]
        grad_scores, probs_low = [], []
        for b, r in enumerate(blocks):
            prob = probs[h, r, :]
            row_dot = jnp.sum(prob * grad_probs[b], axis=-1, keepdims=True)
            grad_scores.append((prob * (grad_probs[b] - row_dot)).astype(bf16))
            probs_low.append(prob.astype(bf16))
        for b, r in enumerate(blocks):
            grad_query = dot(grad_scores[b], key_at[h, r, :], NN)
            grad_key = dot(grad_scores[b], query_at[h, r, :], TN)
            grad_value = dot(probs_low[b], upstream[h, r, :], TN)
            grad_ref[h, r, :128] = ((grad_query + grad_key[:, :128]) * scaling).astype(bf16)
            grad_ref[h, r, 128:] = (grad_key[:, 128:] * scaling + grad_value).astype(bf16)

    def weigh(h):
        part = dot(turned_ref[...], grad_ref[h], NN).astype(bf16)
        weight_ref[h] = part.reshape(16, width // 16, PADDED)

    for h in range(RING):
        spread(h)
    for copy in copies[:4]:
        copy.wait()
    out_copies = [pltpu.make_async_copy(grad_ref, grad_hbm, out_sems.at[RING])] + [
        pltpu.make_async_copy(weight_ref.at[h], weight_hbm.at[:, h], out_sems.at[h])
        for h in range(RING)
    ]
    attend(0)
    copies[4].wait()
    for h in range(RING):
        if h + 1 < RING:
            attend(h + 1)
        else:
            for copy in out_copies[:RING]:
                copy.start()
        weigh(h)
    out_copies[RING].start()
    for copy in out_copies:
        copy.wait()


def back_kernel(grad_ref, w_ref, normed_ref, out_ref, gain_ref):
    parts = [w_ref[:, h].reshape(PADDED, w_ref.shape[-1]) for h in range(RING)]
    grads = jnp.concatenate([grad_ref[h] for h in range(RING)], axis=1)
    total = dot(grads, jnp.concatenate(parts, axis=0), NN)
    out_ref[...] = total.astype(out_ref.dtype)
    gain_ref[...] = jnp.sum(total * normed_ref[...].astype(f32), axis=0, keepdims=True)


def spread_kernel(in_ref, out_ref):
    total = in_ref[0].astype(f32)
    for q in range(1, RING):
        total += in_ref[q].astype(f32)
    out_ref[...] = jnp.broadcast_to(total.astype(bf16)[None], out_ref.shape)


def turn_kernel(whole_ref, out_ref):
    whole = whole_ref[...].reshape(out_ref.shape[1], PADDED).astype(f32)
    out_ref[...] = whole.T[: 3 * HEAD]


def final_kernel(rows_ref, gain_ref, keep_ref, core_ref, pair_ref, out_ref):
    values = rows_ref[...].astype(f32)
    inverse = lax.rsqrt(jnp.mean(values * values, axis=-1, keepdims=True) + epsilon)
    scaled = values * inverse
    normed_grad = keep_ref[...] + core_ref[...].astype(f32) + pair_ref[...].astype(f32)
    grad_scaled = normed_grad * gain_ref[...]
    mixed = jnp.mean(grad_scaled * scaled, axis=-1, keepdims=True)
    out_ref[...] = (inverse * (grad_scaled - scaled * mixed)).astype(bf16)


def vmem():
    return pl.BlockSpec(memory_space=pltpu.VMEM)


def smem():
    return pl.BlockSpec(memory_space=pltpu.SMEM)


def params(limit=SMALL):
    return pltpu.CompilerParams(vmem_limit_bytes=limit)


def pack_call(rows):
    return pl.pallas_call(
        pack_kernel,
        out_shape=jax.ShapeDtypeStruct((HEADS, LINES, 128), bf16),
        in_specs=[vmem()],
        out_specs=vmem(),
        compiler_params=params(),
    )(rows)


def permute_call(place, source, received):
    return pl.pallas_call(
        permute_kernel,
        out_shape=jax.ShapeDtypeStruct((RING, SLOTS, LINES, 128), bf16),
        in_specs=[smem(), smem(), vmem()],
        out_specs=vmem(),
        scratch_shapes=[pltpu.VMEM((HEADS * CHUNK, 128), f32), pltpu.VMEM((CHUNK, 128), f32)],
        compiler_params=params(),
    )(place, source, received)


def norm_call(rows, gain):
    return pl.pallas_call(
        norm_kernel,
        out_shape=jax.ShapeDtypeStruct(rows.shape, bf16),
        in_specs=[vmem(), vmem()],
        out_specs=vmem(),
        compiler_params=params(),
    )(rows, gain)


def gather_call(half, core):
    rows, width = 2 * half.shape[0], half.shape[1]
    return pl.pallas_call(
        gather_kernel,
        out_shape=(
            jax.ShapeDtypeStruct((rows, width), bf16),
            jax.ShapeDtypeStruct((width, rows), bf16),
        ),
        in_specs=[vmem(), vmem()],
        out_specs=(vmem(), vmem()),
        compiler_params=params(BIG),
    )(half, core)


def hbm():
    return pl.BlockSpec(memory_space=pl.ANY)


def kept(rows):
    return (
        ((RING, rows, 128), bf16),
        ((RING, rows, 128), bf16),
        ((RING, rows, PADDED), bf16),
        ((RING, rows, SUPER), f32),
    )


def forward_call(place, normed, weights, windows):
    rows, width = normed.shape
    return pl.pallas_call(
        forward_kernel,
        out_shape=tuple(jax.ShapeDtypeStruct(*each) for each in kept(rows)),
        in_specs=[smem(), hbm(), hbm(), vmem()],
        out_specs=(hbm(),) * 4,
        scratch_shapes=[pltpu.VMEM(*each) for each in kept(rows)]
        + [
            pltpu.VMEM((RING, rows, 128), bf16),
            pltpu.VMEM((rows, SUPER), f32),
            pltpu.VMEM((rows, width), bf16),
            pltpu.VMEM((RING, 16, 16, width), bf16),
            pltpu.SemaphoreType.DMA((RING + 1,)),
            pltpu.SemaphoreType.DMA((4,)),
        ],
        compiler_params=params(BIG),
    )(place, normed, weights, windows)


def head_call(turned, upstream, forward):
    width, rows = turned.shape
    return pl.pallas_call(
        head_kernel,
        out_shape=(
            jax.ShapeDtypeStruct((RING, rows, PADDED), bf16),
            jax.ShapeDtypeStruct((16, RING, width // 16, PADDED), bf16),
        ),
        in_specs=[hbm(), vmem()] + [hbm()] * 4,
        out_specs=(hbm(),) * 2,
        scratch_shapes=[pltpu.VMEM(*each) for each in kept(rows)]
        + [
            pltpu.VMEM((RING, rows, 128), bf16),
            pltpu.VMEM((width, rows), bf16),
            pltpu.VMEM((RING, rows, PADDED), bf16),
            pltpu.VMEM((RING, 16, width // 16, PADDED), bf16),
            pltpu.SemaphoreType.DMA((5,)),
            pltpu.SemaphoreType.DMA((RING + 1,)),
        ],
        compiler_params=params(BIG),
    )(turned, upstream, *forward)


def back_call(grads, weights, normed, half, dtype):
    rows, width = 2 * CHUNK, weights.shape[-1]
    piece = 256
    return pl.pallas_call(
        back_kernel,
        grid=(width // piece,),
        out_shape=(
            jax.ShapeDtypeStruct((rows, width), dtype),
            jax.ShapeDtypeStruct((1, width), f32),
        ),
        in_specs=[
            pl.BlockSpec((RING, rows, PADDED), lambda n: (0, half, 0)),
            pl.BlockSpec((16, RING, 16, piece), lambda n: (0, 0, 0, n)),
            pl.BlockSpec((rows, piece), lambda n: (half, n)),
        ],
        out_specs=(
            pl.BlockSpec((rows, piece), lambda n: (0, n)),
            pl.BlockSpec((1, piece), lambda n: (0, n)),
        ),
        compiler_params=params(BIG),
    )(grads, weights, normed)


def final_call(rows, gain, keep, from_core, from_pair):
    part = pl.BlockSpec(rows.shape, lambda i: (0, 0))
    return pl.pallas_call(
        final_kernel,
        grid=(1,),
        out_shape=jax.ShapeDtypeStruct(rows.shape, bf16),
        in_specs=[part, pl.BlockSpec(gain.shape, lambda i: (0, 0)), part, part, part],
        out_specs=part,
        compiler_params=params(BIG),
    )(rows, gain, keep, from_core, from_pair)


def spread_call(arrived):
    return pl.pallas_call(
        spread_kernel,
        out_shape=jax.ShapeDtypeStruct((16,) + arrived.shape[1:], bf16),
        in_specs=[vmem()],
        out_specs=vmem(),
        compiler_params=params(),
    )(arrived)


def turn_call(whole):
    width = whole.shape[0] * whole.shape[1]
    return pl.pallas_call(
        turn_kernel,
        out_shape=jax.ShapeDtypeStruct((3 * HEAD, width), f32),
        in_specs=[vmem()],
        out_specs=vmem(),
        compiler_params=params(BIG),
    )(whole)


def swap(x, axis):
    return lax.ppermute(x, axis, [(0, 1), (1, 0)])


def on_device(layer_input, grad_packed, source_row, window_id, w_qkv, gain):
    width = layer_input.shape[1]
    dp = lax.axis_index("y") * 4 + lax.axis_index("x")
    ring = lax.axis_index("zq")
    slot = lax.axis_index("zp") * 2 + lax.axis_index("core")
    place = jnp.stack([ring, slot]).astype(jnp.int32)
    gain_row = gain.reshape(1, width)

    own = norm_call(layer_input, gain_row)
    grad_rows, own = lax.optimization_barrier((grad_packed, own))
    packed = pack_call(grad_rows)
    flipped = jnp.swapaxes(w_qkv, 1, 2).reshape(3 * HEAD, width)
    flipped = jnp.pad(flipped, ((0, PADDED - 3 * HEAD), (0, 0)))
    share = lax.dynamic_slice(flipped, (16 * dp, 0), (16, width))
    others = [lax.ppermute(share, "zq", [(i, (i + k) % RING) for i in range(RING)]) for k in (3, 2, 1)]
    others, packed = lax.optimization_barrier((others, packed))
    circle = jnp.concatenate([share] + others + [share] + others, axis=0)
    ordered = lax.dynamic_slice(circle, (16 * ((RING - ring) % RING), 0), (16 * RING, width))
    weights = lax.all_gather(ordered, ("y", "x"), axis=0, tiled=True)
    weights = weights.reshape(16, RING, 16, width)

    by_head = lax.all_to_all(packed, ("zq", "zp", "core"), split_axis=0, concat_axis=0)
    permuted = permute_call(place, source_row.reshape(-1), by_head)
    upstream = lax.all_to_all(permuted, "zq", split_axis=0, concat_axis=0)

    half = jnp.concatenate([own, swap(own, "zp")], axis=0)
    normed, turned = gather_call(half, swap(half, "core"))
    windows = window_id.reshape(32, 128).astype(f32)
    forward = forward_call(place, normed, weights, windows)
    grads, weight_part = head_call(turned, upstream, forward)

    arrived = lax.all_to_all(weight_part, ("y", "x"), split_axis=0, concat_axis=0)
    summed = jnp.sum(arrived.astype(f32), axis=0).astype(bf16)
    send, gain_send = back_call(grads, weights, normed, 1, bf16)
    keep, gain_keep = back_call(grads, weights, normed, 0, f32)
    gain_part = gain_send + gain_keep
    from_core = swap(send, "core")
    pair = (keep[CHUNK:] + from_core[CHUNK:].astype(f32)).astype(bf16)
    gain_part = gain_part + swap(gain_part, "core")
    gain_part = gain_part + swap(gain_part, "zp")
    beside = gain_part.reshape(width // 16, 16).astype(bf16)
    beside = jnp.broadcast_to(beside[None], (RING, width // 16, 16))
    message = jnp.concatenate([summed[..., : 3 * HEAD], beside], axis=2)
    from_pair = swap(pair, "zp")
    message, from_pair = lax.optimization_barrier((message, from_pair))
    arrived = lax.all_to_all(message, "zq", split_axis=0, concat_axis=0)
    copies = spread_call(arrived)
    whole = lax.all_to_all(copies, ("y", "x"), split_axis=0, concat_axis=0)
    grad_gain = jnp.sum(whole[:, :, 3 * HEAD :].astype(f32), axis=0).reshape(width) / gain
    grad_weight = jnp.swapaxes(turn_call(whole).reshape(3, HEAD, width), 1, 2)
    grad_input = final_call(layer_input, gain_row, keep, from_core, from_pair)
    return (grad_input, grad_weight, grad_gain)


def solution(mesh):
    fine = Mesh(mesh.devices.reshape(4, 4, 4, 2, 2), ("y", "x", "zq", "zp", "core"))
    dp, group = ("y", "x"), ("zq", "zp", "core")
    rows = P(dp + group, None)
    return jax.shard_map(
        on_device,
        mesh=fine,
        in_specs=(rows, rows, P(dp, None), P(dp, None), P(None, None, group), P()),
        out_specs=(rows, P(None, None, group), P()),
        check_vma=False,
    )
```

```python
import functools

import jax
import jax.numpy as jnp
from jax import lax
from jax.experimental import pallas as pl
from jax.experimental.pallas import tpu as pltpu
from jax.sharding import Mesh, PartitionSpec as P

HEAD = 80
HEADS = 16
SUPER = 128
CHUNK = 256
SLOTS = 4
RING = 4
LINES = 160
PADDED = 256
XOR_ORDER = (0, 2, 1, 3)
epsilon = 1e-06
bf16 = jnp.bfloat16
f32 = jnp.float32
NT = (((1,), (1,)), ((), ()))
TN = (((0,), (0,)), ((), ()))
NN = (((1,), (0,)), ((), ()))
BIG = 58 * 1024 * 1024
SMALL = 20 * 1024 * 1024


def dot(a, b, dims):
    return lax.dot_general(a, b, dims, preferred_element_type=f32)


def lanes(shape):
    return lax.broadcasted_iota(jnp.int32, shape, len(shape) - 1)


def roll(x, shift):
    shift = shift % x.shape[-1]
    return x if shift == 0 else pltpu.roll(x, shift, x.ndim - 1)


def pack(rows):
    top = jnp.where(lanes((128, 128)) < 64, rows[:128], roll(rows[128:], 64))
    group = lanes((32, 128)) // 16
    low = roll(rows[:32], -64)
    for k in range(1, 8):
        low = jnp.where(group == k, roll(rows[32 * k : 32 * k + 32], 16 * k - 64), low)
    return top, low


def unpack(top, low, place):
    at = lanes((128, 128))
    upper = roll(top, place)
    lower = roll(top, place - 64)
    tail = [roll(low, place + 64 - 16 * k) for k in range(8)]
    first = jnp.concatenate(tail[:4], axis=0)
    second = jnp.concatenate(tail[4:], axis=0)
    wide = (at >= place) & (at < place + 64)
    rest = (at >= place + 64) & (at < place + HEAD)
    one = jnp.where(wide, upper, jnp.where(rest, first, 0.0))
    two = jnp.where(wide, lower, jnp.where(rest, second, 0.0))
    return one, two


def pack_kernel(rows_ref, out_ref):
    for g in range(HEADS):
        start = (HEAD * g) // 128 * 128
        shift = HEAD * g - start
        size = 128 if shift + HEAD <= 128 else 256
        window = rows_ref[:, start : start + size].astype(f32)
        window = roll(window, -shift)[:, :128]
        top, low = pack(window)
        out_ref[g, :128, :] = top.astype(bf16)
        out_ref[g, 128:, :] = low.astype(bf16)


def permute_kernel(place_ref, source_ref, in_ref, out_ref, table, picked):
    slot = place_ref[1]
    for src in range(HEADS):
        one, two = unpack(
            in_ref[src, :128, :].astype(f32), in_ref[src, 128:, :].astype(f32), 0
        )
        table[CHUNK * src : CHUNK * src + 128, :] = one
        table[CHUNK * src + 128 : CHUNK * src + 256, :] = two
    for q in range(RING):
        for o, off in enumerate(XOR_ORDER):
            base = q * SLOTS * CHUNK + (slot ^ off) * CHUNK

            def step(i, carry):
                at = i * 64
                for u in range(64):
                    row = source_ref[base + at + u]
                    picked[pl.ds(at + u, 1), :] = table[pl.ds(row, 1), :]
                return carry

            lax.fori_loop(0, CHUNK // 64, step, 0)
            top, low = pack(picked[...])
            out_ref[q, o, :128, :] = top.astype(bf16)
            out_ref[q, o, 128:, :] = low.astype(bf16)


def norm_kernel(rows_ref, gain_ref, out_ref):
    values = rows_ref[...].astype(f32)
    inverse = lax.rsqrt(jnp.mean(values * values, axis=-1, keepdims=True) + epsilon)
    out_ref[...] = (values * inverse * gain_ref[...]).astype(bf16)


def shifted(shape, move):
    row = lax.broadcasted_iota(jnp.int32, shape, 0)
    return jnp.where(move(row, lanes(shape)), 1.0, 0.0).astype(bf16)


def gather_kernel(half_ref, core_ref, out_ref, turned_ref):
    for c, part in enumerate((half_ref, core_ref)):
        rows = slice(2 * CHUNK * c, 2 * CHUNK * c + 2 * CHUNK)
        out_ref[rows, :] = part[...]
        turned_ref[:, rows] = part[...].T


def front(x):
    return jnp.where(lanes(x.shape) < HEAD, x, 0.0).astype(bf16)


def blocks_of(total_rows):
    return [slice(SUPER * b, SUPER * b + SUPER) for b in range(total_rows // SUPER)]


def forward_kernel(
    place_ref, normed_hbm, w_hbm, window_ref, first_hbm, second_hbm, probs_hbm,
    first, second, probs, same, normed_ref, w_ref, in_sems, out_sems,
):
    ring, slot = place_ref[0], place_ref[1]
    scaling = HEAD ** (-0.5)
    total_rows, width = normed_ref.shape
    blocks = blocks_of(total_rows)
    copies = [pltpu.make_async_copy(normed_hbm, normed_ref, in_sems.at[RING])] + [
        pltpu.make_async_copy(w_hbm.at[:, h], w_ref.at[h], in_sems.at[h]) for h in range(RING)
    ]
    for copy in copies:
        copy.start()
    for b, r in enumerate(blocks):
        line = ring * 8 + (slot ^ XOR_ORDER[b // 2]) * 2 + b % 2
        labels = jnp.broadcast_to(window_ref[pl.ds(line, 1), :], (SUPER, SUPER))
        same[r, :] = jnp.where(labels == labels.T, 0.0, -1e30)
    for copy in copies[:2]:
        copy.wait()
    late = copies[2:]

    def project(h):
        w = w_ref[h].reshape(PADDED, width)
        low = dot(normed_ref[...], w, NT).astype(bf16)
        first[h] = low[:, :128]
        second[h] = low[:, 128:]

    def soften(h):
        scores = [dot(front(first[h, r, :]), second[h, r, :], NT) for r in blocks]
        for b, r in enumerate(blocks):
            masked = scores[b] * scaling + same[r, :]
            powers = jnp.exp(masked - jnp.max(masked, axis=-1, keepdims=True))
            probs[h, r, :] = powers * (1.0 / jnp.sum(powers, axis=-1, keepdims=True))

    copies = [
        pltpu.make_async_copy(src, dst, out_sems.at[i])
        for i, (src, dst) in enumerate(
            ((first, first_hbm), (second, second_hbm), (probs, probs_hbm))
        )
    ]
    project(0)
    for copy in late:
        copy.wait()
    for h in range(RING):
        if h + 1 < RING:
            project(h + 1)
        else:
            for copy in copies[:2]:
                copy.start()
        soften(h)
    copies[2].start()
    for copy in copies:
        copy.wait()


def head_kernel(
    turned_hbm, up_ref, first_hbm, second_hbm, probs_hbm, grad_hbm, weight_hbm,
    first, second, probs, upstream, turned_ref, grad_ref, weight_ref,
    in_sems, out_sems,
):
    scaling = HEAD ** (-0.5)
    width, total_rows = turned_ref.shape
    blocks = blocks_of(total_rows)
    copies = [
        pltpu.make_async_copy(src, dst, in_sems.at[i])
        for i, (src, dst) in enumerate(
            (
                (first_hbm, first), (second_hbm, second), (probs_hbm, probs),
                (turned_hbm, turned_ref),
            )
        )
    ]
    for copy in copies:
        copy.start()
    to_wide = shifted(
        (128, PADDED),
        lambda r, c: ((c >= 80) & (c < 128) & (r % 64 == c - 80))
        | ((c >= 208) & (c < 224) & (r % 64 == c - 160)),
    )
    to_rest = shifted(
        (128, PADDED), lambda r, c: (c >= 224) & (c < 240) & (r % 16 == c - 224)
    )
    row = lax.broadcasted_iota(jnp.int32, (CHUNK, 128), 0)
    keep_wide = row // 128 == lanes((CHUNK, 128)) // 64
    keep_rest = row // 32 == lanes((CHUNK, 128)) // 16

    def spread(h):
        for c in range(SLOTS):
            top, low = up_ref[h, c, :128, :], up_ref[h, c, 128:, :]
            wide = jnp.where(keep_wide, jnp.concatenate([top] * 2, axis=0), 0.0)
            rest = jnp.where(keep_rest, jnp.concatenate([low] * 8, axis=0), 0.0)
            both = dot(wide.astype(bf16), to_wide, NN) + dot(rest.astype(bf16), to_rest, NN)
            upstream[h, CHUNK * c : CHUNK * c + CHUNK, :] = both.astype(bf16)

    def attend(h):
        grad_probs = [
            dot(upstream[h, r, :128], first[h, r, :], NT)
            + dot(upstream[h, r, 128:], second[h, r, :], NT)
            for r in blocks
        ]
        grad_scores, probs_low = [], []
        for b, r in enumerate(blocks):
            prob = probs[h, r, :]
            row_dot = jnp.sum(prob * grad_probs[b], axis=-1, keepdims=True)
            grad_scores.append((prob * (grad_probs[b] - row_dot)).astype(bf16))
            probs_low.append(prob.astype(bf16))
        for b, r in enumerate(blocks):
            grad_query = dot(grad_scores[b], front(second[h, r, :]), NN)
            grad_key = dot(grad_scores[b], front(first[h, r, :]), TN)
            grad_value = dot(probs_low[b], upstream[h, r, :], TN)
            grad_ref[h, r, :128] = (grad_query * scaling + grad_value[:, :128]).astype(bf16)
            grad_ref[h, r, 128:] = (grad_key * scaling + grad_value[:, 128:]).astype(bf16)

    def weigh(h):
        part = dot(turned_ref[...], grad_ref[h], NN).astype(bf16)
        weight_ref[h] = part.reshape(16, width // 16, PADDED)

    for h in range(RING):
        spread(h)
    for copy in copies[:3]:
        copy.wait()
    out_copies = [pltpu.make_async_copy(grad_ref, grad_hbm, out_sems.at[RING])] + [
        pltpu.make_async_copy(weight_ref.at[h], weight_hbm.at[:, h], out_sems.at[h])
        for h in range(RING)
    ]
    attend(0)
    copies[3].wait()
    for h in range(RING):
        if h + 1 < RING:
            attend(h + 1)
        else:
            for copy in out_copies[:RING]:
                copy.start()
        weigh(h)
    out_copies[RING].start()
    for copy in out_copies:
        copy.wait()


def back_kernel(grad_ref, w_ref, normed_ref, out_ref, gain_ref):
    parts = [w_ref[:, h].reshape(PADDED, w_ref.shape[-1]) for h in range(RING)]
    grads = jnp.concatenate([grad_ref[h] for h in range(RING)], axis=1)
    total = dot(grads, jnp.concatenate(parts, axis=0), NN)
    out_ref[...] = total.astype(out_ref.dtype)
    gain_ref[...] = jnp.sum(total * normed_ref[...].astype(f32), axis=0, keepdims=True)


def spread_kernel(in_ref, out_ref):
    total = in_ref[0].astype(f32)
    for q in range(1, RING):
        total += in_ref[q].astype(f32)
    out_ref[...] = jnp.broadcast_to(total.astype(bf16)[None], out_ref.shape)


def turn_kernel(whole_ref, out_ref):
    whole = whole_ref[...].reshape(out_ref.shape[1], PADDED).astype(f32)
    turned = whole.T
    out_ref[:HEAD] = turned[:HEAD]
    out_ref[HEAD : 2 * HEAD] = turned[128 : 128 + HEAD]
    out_ref[2 * HEAD : 2 * HEAD + 48] = turned[HEAD:128]
    out_ref[2 * HEAD + 48 :] = turned[128 + HEAD : 3 * HEAD]


def final_kernel(rows_ref, gain_ref, keep_ref, core_ref, pair_ref, out_ref):
    values = rows_ref[...].astype(f32)
    inverse = lax.rsqrt(jnp.mean(values * values, axis=-1, keepdims=True) + epsilon)
    scaled = values * inverse
    normed_grad = keep_ref[...] + core_ref[...].astype(f32) + pair_ref[...].astype(f32)
    grad_scaled = normed_grad * gain_ref[...]
    mixed = jnp.mean(grad_scaled * scaled, axis=-1, keepdims=True)
    out_ref[...] = (inverse * (grad_scaled - scaled * mixed)).astype(bf16)


def vmem():
    return pl.BlockSpec(memory_space=pltpu.VMEM)


def smem():
    return pl.BlockSpec(memory_space=pltpu.SMEM)


def params(limit=SMALL):
    return pltpu.CompilerParams(vmem_limit_bytes=limit)


def pack_call(rows):
    return pl.pallas_call(
        pack_kernel,
        out_shape=jax.ShapeDtypeStruct((HEADS, LINES, 128), bf16),
        in_specs=[vmem()],
        out_specs=vmem(),
        compiler_params=params(),
    )(rows)


def permute_call(place, source, received):
    return pl.pallas_call(
        permute_kernel,
        out_shape=jax.ShapeDtypeStruct((RING, SLOTS, LINES, 128), bf16),
        in_specs=[smem(), smem(), vmem()],
        out_specs=vmem(),
        scratch_shapes=[pltpu.VMEM((HEADS * CHUNK, 128), f32), pltpu.VMEM((CHUNK, 128), f32)],
        compiler_params=params(),
    )(place, source, received)


def norm_call(rows, gain):
    return pl.pallas_call(
        norm_kernel,
        out_shape=jax.ShapeDtypeStruct(rows.shape, bf16),
        in_specs=[vmem(), vmem()],
        out_specs=vmem(),
        compiler_params=params(),
    )(rows, gain)


def gather_call(half, core):
    rows, width = 2 * half.shape[0], half.shape[1]
    return pl.pallas_call(
        gather_kernel,
        out_shape=(
            jax.ShapeDtypeStruct((rows, width), bf16),
            jax.ShapeDtypeStruct((width, rows), bf16),
        ),
        in_specs=[vmem(), vmem()],
        out_specs=(vmem(), vmem()),
        compiler_params=params(BIG),
    )(half, core)


def hbm():
    return pl.BlockSpec(memory_space=pl.ANY)


def kept(rows):
    return (
        ((RING, rows, 128), bf16),
        ((RING, rows, 128), bf16),
        ((RING, rows, SUPER), f32),
    )


def forward_call(place, normed, weights, windows):
    rows, width = normed.shape
    return pl.pallas_call(
        forward_kernel,
        out_shape=tuple(jax.ShapeDtypeStruct(*each) for each in kept(rows)),
        in_specs=[smem(), hbm(), hbm(), vmem()],
        out_specs=(hbm(),) * 3,
        scratch_shapes=[pltpu.VMEM(*each) for each in kept(rows)]
        + [
            pltpu.VMEM((rows, SUPER), f32),
            pltpu.VMEM((rows, width), bf16),
            pltpu.VMEM((RING, 16, 16, width), bf16),
            pltpu.SemaphoreType.DMA((RING + 1,)),
            pltpu.SemaphoreType.DMA((3,)),
        ],
        compiler_params=params(BIG),
    )(place, normed, weights, windows)


def head_call(turned, upstream, forward):
    width, rows = turned.shape
    return pl.pallas_call(
        head_kernel,
        out_shape=(
            jax.ShapeDtypeStruct((RING, rows, PADDED), bf16),
            jax.ShapeDtypeStruct((16, RING, width // 16, PADDED), bf16),
        ),
        in_specs=[hbm(), vmem()] + [hbm()] * 3,
        out_specs=(hbm(),) * 2,
        scratch_shapes=[pltpu.VMEM(*each) for each in kept(rows)]
        + [
            pltpu.VMEM((RING, rows, PADDED), bf16),
            pltpu.VMEM((width, rows), bf16),
            pltpu.VMEM((RING, rows, PADDED), bf16),
            pltpu.VMEM((RING, 16, width // 16, PADDED), bf16),
            pltpu.SemaphoreType.DMA((4,)),
            pltpu.SemaphoreType.DMA((RING + 1,)),
        ],
        compiler_params=params(BIG),
    )(turned, upstream, *forward)


def back_call(grads, weights, normed, half, dtype):
    rows, width = 2 * CHUNK, weights.shape[-1]
    piece = 256
    return pl.pallas_call(
        back_kernel,
        grid=(width // piece,),
        out_shape=(
            jax.ShapeDtypeStruct((rows, width), dtype),
            jax.ShapeDtypeStruct((1, width), f32),
        ),
        in_specs=[
            pl.BlockSpec((RING, rows, PADDED), lambda n: (0, half, 0)),
            pl.BlockSpec((16, RING, 16, piece), lambda n: (0, 0, 0, n)),
            pl.BlockSpec((rows, piece), lambda n: (half, n)),
        ],
        out_specs=(
            pl.BlockSpec((rows, piece), lambda n: (0, n)),
            pl.BlockSpec((1, piece), lambda n: (0, n)),
        ),
        compiler_params=params(BIG),
    )(grads, weights, normed)


def final_call(rows, gain, keep, from_core, from_pair):
    part = pl.BlockSpec(rows.shape, lambda i: (0, 0))
    return pl.pallas_call(
        final_kernel,
        grid=(1,),
        out_shape=jax.ShapeDtypeStruct(rows.shape, bf16),
        in_specs=[part, pl.BlockSpec(gain.shape, lambda i: (0, 0)), part, part, part],
        out_specs=part,
        compiler_params=params(BIG),
    )(rows, gain, keep, from_core, from_pair)


def spread_call(arrived):
    return pl.pallas_call(
        spread_kernel,
        out_shape=jax.ShapeDtypeStruct((16,) + arrived.shape[1:], bf16),
        in_specs=[vmem()],
        out_specs=vmem(),
        compiler_params=params(),
    )(arrived)


def turn_call(whole):
    width = whole.shape[0] * whole.shape[1]
    return pl.pallas_call(
        turn_kernel,
        grid=(2,),
        out_shape=jax.ShapeDtypeStruct((3 * HEAD, width), f32),
        in_specs=[pl.BlockSpec((8, width // 16, PADDED), lambda i: (i, 0, 0))],
        out_specs=pl.BlockSpec((3 * HEAD, width // 2), lambda i: (0, i)),
        compiler_params=params(BIG),
    )(whole)


def swap(x, axis):
    return lax.ppermute(x, axis, [(0, 1), (1, 0)])


def on_device(layer_input, grad_packed, source_row, window_id, w_qkv, gain):
    width = layer_input.shape[1]
    dp = lax.axis_index("y") * 4 + lax.axis_index("x")
    ring = lax.axis_index("zq")
    slot = lax.axis_index("zp") * 2 + lax.axis_index("core")
    place = jnp.stack([ring, slot]).astype(jnp.int32)
    gain_row = gain.reshape(1, width)

    own = norm_call(layer_input, gain_row)
    grad_rows, own = lax.optimization_barrier((grad_packed, own))
    packed = pack_call(grad_rows)
    flipped = jnp.swapaxes(w_qkv, 1, 2).reshape(3 * HEAD, width)
    query, key, value = (flipped[HEAD * j : HEAD * j + HEAD] for j in range(3))
    spare = jnp.zeros((PADDED - 3 * HEAD, width), bf16)
    flipped = jnp.concatenate([query, value[:48], key, value[48:], spare], axis=0)
    share = lax.dynamic_slice(flipped, (16 * dp, 0), (16, width))
    others = [lax.ppermute(share, "zq", [(i, (i + k) % RING) for i in range(RING)]) for k in (3, 2, 1)]
    others, packed = lax.optimization_barrier((others, packed))
    circle = jnp.concatenate([share] + others + [share] + others, axis=0)
    ordered = lax.dynamic_slice(circle, (16 * ((RING - ring) % RING), 0), (16 * RING, width))
    weights = lax.all_gather(ordered, ("y", "x"), axis=0, tiled=True)
    weights = weights.reshape(16, RING, 16, width)

    by_head = lax.all_to_all(packed, ("zq", "zp", "core"), split_axis=0, concat_axis=0)
    permuted = permute_call(place, source_row.reshape(-1), by_head)
    upstream = lax.all_to_all(permuted, "zq", split_axis=0, concat_axis=0)

    half = jnp.concatenate([own, swap(own, "zp")], axis=0)
    normed, turned = gather_call(half, swap(half, "core"))
    windows = window_id.reshape(32, 128).astype(f32)
    forward = forward_call(place, normed, weights, windows)
    grads, weight_part = head_call(turned, upstream, forward)

    arrived = lax.all_to_all(weight_part, ("y", "x"), split_axis=0, concat_axis=0)
    summed = jnp.sum(arrived.astype(f32), axis=0).astype(bf16)
    send, gain_send = back_call(grads, weights, normed, 1, bf16)
    keep, gain_keep = back_call(grads, weights, normed, 0, f32)
    gain_part = gain_send + gain_keep
    from_core = swap(send, "core")
    pair = (keep[CHUNK:] + from_core[CHUNK:].astype(f32)).astype(bf16)
    gain_part = gain_part + swap(gain_part, "core")
    gain_part = gain_part + swap(gain_part, "zp")
    beside = gain_part.reshape(width // 16, 16).astype(bf16)
    beside = jnp.broadcast_to(beside[None], (RING, width // 16, 16))
    message = jnp.concatenate([summed[..., : 3 * HEAD], beside], axis=2)
    from_pair = swap(pair, "zp")
    message, from_pair = lax.optimization_barrier((message, from_pair))
    arrived = lax.all_to_all(message, "zq", split_axis=0, concat_axis=0)
    copies = spread_call(arrived)
    whole = lax.all_to_all(copies, ("y", "x"), split_axis=0, concat_axis=0)
    grad_gain = jnp.sum(whole[:, :, 3 * HEAD :].astype(f32), axis=0).reshape(width) / gain
    grad_weight = jnp.swapaxes(turn_call(whole).reshape(3, HEAD, width), 1, 2)
    grad_input = final_call(layer_input, gain_row, keep, from_core, from_pair)
    return (grad_input, grad_weight, grad_gain)


def solution(mesh):
    fine = Mesh(mesh.devices.reshape(4, 4, 4, 2, 2), ("y", "x", "zq", "zp", "core"))
    dp, group = ("y", "x"), ("zq", "zp", "core")
    rows = P(dp + group, None)
    return jax.shard_map(
        on_device,
        mesh=fine,
        in_specs=(rows, rows, P(dp, None), P(dp, None), P(None, None, group), P()),
        out_specs=(rows, P(None, None, group), P()),
        check_vma=False,
    )
```

```python
import functools

import jax
import jax.numpy as jnp
from jax import lax
from jax.experimental import pallas as pl
from jax.experimental.pallas import tpu as pltpu
from jax.sharding import Mesh, PartitionSpec as P

HEAD = 80
HEADS = 16
SUPER = 128
CHUNK = 256
SLOTS = 4
RING = 4
LINES = 160
PADDED = 256
XOR_ORDER = (0, 2, 1, 3)
epsilon = 1e-06
bf16 = jnp.bfloat16
f32 = jnp.float32
NT = (((1,), (1,)), ((), ()))
TN = (((0,), (0,)), ((), ()))
NN = (((1,), (0,)), ((), ()))
BIG = 58 * 1024 * 1024
SMALL = 20 * 1024 * 1024


def dot(a, b, dims):
    return lax.dot_general(a, b, dims, preferred_element_type=f32)


def lanes(shape):
    return lax.broadcasted_iota(jnp.int32, shape, len(shape) - 1)


def roll(x, shift):
    shift = shift % x.shape[-1]
    return x if shift == 0 else pltpu.roll(x, shift, x.ndim - 1)


def pack(rows):
    top = jnp.where(lanes((128, 128)) < 64, rows[:128], roll(rows[128:], 64))
    group = lanes((32, 128)) // 16
    low = roll(rows[:32], -64)
    for k in range(1, 8):
        low = jnp.where(group == k, roll(rows[32 * k : 32 * k + 32], 16 * k - 64), low)
    return top, low


def unpack(top, low, place):
    at = lanes((128, 128))
    upper = roll(top, place)
    lower = roll(top, place - 64)
    tail = [roll(low, place + 64 - 16 * k) for k in range(8)]
    first = jnp.concatenate(tail[:4], axis=0)
    second = jnp.concatenate(tail[4:], axis=0)
    wide = (at >= place) & (at < place + 64)
    rest = (at >= place + 64) & (at < place + HEAD)
    one = jnp.where(wide, upper, jnp.where(rest, first, 0.0))
    two = jnp.where(wide, lower, jnp.where(rest, second, 0.0))
    return one, two


def pack_kernel(rows_ref, out_ref):
    for g in range(HEADS):
        start = (HEAD * g) // 128 * 128
        shift = HEAD * g - start
        size = 128 if shift + HEAD <= 128 else 256
        window = rows_ref[:, start : start + size].astype(f32)
        window = roll(window, -shift)[:, :128]
        top, low = pack(window)
        out_ref[g, :128, :] = top.astype(bf16)
        out_ref[g, 128:, :] = low.astype(bf16)


def permute_kernel(place_ref, source_ref, in_ref, out_ref, table, picked):
    slot = place_ref[1]
    for src in range(HEADS):
        one, two = unpack(
            in_ref[src, :128, :].astype(f32), in_ref[src, 128:, :].astype(f32), 0
        )
        table[CHUNK * src : CHUNK * src + 128, :] = one
        table[CHUNK * src + 128 : CHUNK * src + 256, :] = two
    for q in range(RING):
        for o, off in enumerate(XOR_ORDER):
            base = q * SLOTS * CHUNK + (slot ^ off) * CHUNK

            def step(i, carry):
                at = i * 64
                for u in range(64):
                    row = source_ref[base + at + u]
                    picked[pl.ds(at + u, 1), :] = table[pl.ds(row, 1), :]
                return carry

            lax.fori_loop(0, CHUNK // 64, step, 0)
            top, low = pack(picked[...])
            out_ref[q, o, :128, :] = top.astype(bf16)
            out_ref[q, o, 128:, :] = low.astype(bf16)


def norm_kernel(rows_ref, gain_ref, out_ref):
    values = rows_ref[...].astype(f32)
    inverse = lax.rsqrt(jnp.mean(values * values, axis=-1, keepdims=True) + epsilon)
    out_ref[...] = (values * inverse * gain_ref[...]).astype(bf16)


def shifted(shape, move):
    row = lax.broadcasted_iota(jnp.int32, shape, 0)
    return jnp.where(move(row, lanes(shape)), 1.0, 0.0).astype(bf16)


def gather_kernel(half_ref, core_ref, out_ref, turned_ref):
    for c, part in enumerate((half_ref, core_ref)):
        rows = slice(2 * CHUNK * c, 2 * CHUNK * c + 2 * CHUNK)
        out_ref[rows, :] = part[...]
        turned_ref[:, rows] = part[...].T


def front(x):
    return jnp.where(lanes(x.shape) < HEAD, x, 0.0).astype(bf16)


def blocks_of(total_rows):
    return [slice(SUPER * b, SUPER * b + SUPER) for b in range(total_rows // SUPER)]


def forward_kernel(
    place_ref, normed_hbm, w_hbm, window_ref, first_hbm, second_hbm, probs_hbm,
    first, second, probs, same, normed_ref, w_ref, in_sems, out_sems,
):
    ring, slot = place_ref[0], place_ref[1]
    scaling = HEAD ** (-0.5)
    total_rows, width = normed_ref.shape
    blocks = blocks_of(total_rows)
    copies = [pltpu.make_async_copy(normed_hbm, normed_ref, in_sems.at[RING])] + [
        pltpu.make_async_copy(w_hbm.at[:, h], w_ref.at[h], in_sems.at[h]) for h in range(RING)
    ]
    for copy in copies:
        copy.start()
    for b, r in enumerate(blocks):
        line = ring * 8 + (slot ^ XOR_ORDER[b // 2]) * 2 + b % 2
        labels = jnp.broadcast_to(window_ref[pl.ds(line, 1), :], (SUPER, SUPER))
        same[r, :] = jnp.where(labels == labels.T, 0.0, -1e30)
    for copy in copies[:2]:
        copy.wait()
    late = copies[2:]

    def project(h):
        w = w_ref[h].reshape(PADDED, width)
        low = dot(normed_ref[...], w, NT).astype(bf16)
        first[h] = low[:, :128]
        second[h] = low[:, 128:]

    def soften(h):
        scores = [dot(front(first[h, r, :]), second[h, r, :], NT) for r in blocks]
        for b, r in enumerate(blocks):
            masked = scores[b] * scaling + same[r, :]
            powers = jnp.exp(masked - jnp.max(masked, axis=-1, keepdims=True))
            probs[h, r, :] = powers * (1.0 / jnp.sum(powers, axis=-1, keepdims=True))

    copies = [
        pltpu.make_async_copy(src, dst, out_sems.at[i])
        for i, (src, dst) in enumerate(
            ((first, first_hbm), (second, second_hbm), (probs, probs_hbm))
        )
    ]
    project(0)
    for copy in late:
        copy.wait()
    for h in range(RING):
        if h + 1 < RING:
            project(h + 1)
        else:
            for copy in copies[:2]:
                copy.start()
        soften(h)
    copies[2].start()
    for copy in copies:
        copy.wait()


def head_kernel(
    turned_hbm, up_ref, first_hbm, second_hbm, probs_hbm, grad_hbm, weight_hbm,
    first, second, probs, upstream, turned_ref, grad_ref, weight_ref,
    in_sems, out_sems,
):
    scaling = HEAD ** (-0.5)
    width, total_rows = turned_ref.shape
    blocks = blocks_of(total_rows)
    copies = [
        pltpu.make_async_copy(src, dst, in_sems.at[i])
        for i, (src, dst) in enumerate(
            (
                (first_hbm, first), (second_hbm, second), (probs_hbm, probs),
                (turned_hbm, turned_ref),
            )
        )
    ]
    for copy in copies:
        copy.start()
    to_wide = shifted(
        (128, PADDED),
        lambda r, c: ((c >= 80) & (c < 128) & (r % 64 == c - 80))
        | ((c >= 208) & (c < 224) & (r % 64 == c - 160)),
    )
    to_rest = shifted(
        (128, PADDED), lambda r, c: (c >= 224) & (c < 240) & (r % 16 == c - 224)
    )
    row = lax.broadcasted_iota(jnp.int32, (CHUNK, 128), 0)
    keep_wide = row // 128 == lanes((CHUNK, 128)) // 64
    keep_rest = row // 32 == lanes((CHUNK, 128)) // 16

    def spread(h):
        for c in range(SLOTS):
            top, low = up_ref[h, c, :128, :], up_ref[h, c, 128:, :]
            wide = jnp.where(keep_wide, jnp.concatenate([top] * 2, axis=0), 0.0)
            rest = jnp.where(keep_rest, jnp.concatenate([low] * 8, axis=0), 0.0)
            both = dot(wide.astype(bf16), to_wide, NN) + dot(rest.astype(bf16), to_rest, NN)
            upstream[h, CHUNK * c : CHUNK * c + CHUNK, :] = both.astype(bf16)

    def attend(h):
        grad_probs = [
            dot(upstream[h, r, :128], first[h, r, :], NT)
            + dot(upstream[h, r, 128:], second[h, r, :], NT)
            for r in blocks
        ]
        grad_scores, probs_low = [], []
        for b, r in enumerate(blocks):
            prob = probs[h, r, :]
            row_dot = jnp.sum(prob * grad_probs[b], axis=-1, keepdims=True)
            grad_scores.append((prob * (grad_probs[b] - row_dot)).astype(bf16))
            probs_low.append(prob.astype(bf16))
        for b, r in enumerate(blocks):
            grad_query = dot(grad_scores[b], front(second[h, r, :]), NN)
            grad_key = dot(grad_scores[b], front(first[h, r, :]), TN)
            grad_value = dot(probs_low[b], upstream[h, r, :], TN)
            grad_ref[h, r, :128] = (grad_query * scaling + grad_value[:, :128]).astype(bf16)
            grad_ref[h, r, 128:] = (grad_key * scaling + grad_value[:, 128:]).astype(bf16)

    def weigh(h):
        part = dot(turned_ref[...], grad_ref[h], NN).astype(bf16)
        weight_ref[h] = part.reshape(16, width // 16, PADDED)

    for h in range(RING):
        spread(h)
    for copy in copies[:3]:
        copy.wait()
    out_copies = [pltpu.make_async_copy(grad_ref, grad_hbm, out_sems.at[RING])] + [
        pltpu.make_async_copy(weight_ref.at[h], weight_hbm.at[:, h], out_sems.at[h])
        for h in range(RING)
    ]
    attend(0)
    copies[3].wait()
    for h in range(RING):
        if h + 1 < RING:
            attend(h + 1)
        else:
            for copy in out_copies[:RING]:
                copy.start()
        weigh(h)
    out_copies[RING].start()
    for copy in out_copies:
        copy.wait()


def back_kernel(grad_ref, w_ref, normed_ref, out_ref, gain_ref):
    parts = [w_ref[:, h].reshape(PADDED, w_ref.shape[-1]) for h in range(RING)]
    grads = jnp.concatenate([grad_ref[h] for h in range(RING)], axis=1)
    total = dot(grads, jnp.concatenate(parts, axis=0), NN)
    out_ref[...] = total.astype(out_ref.dtype)
    gain_ref[...] = jnp.sum(total * normed_ref[...].astype(f32), axis=0, keepdims=True)


def spread_kernel(in_ref, out_ref):
    total = in_ref[0].astype(f32)
    for q in range(1, RING):
        total += in_ref[q].astype(f32)
    out_ref[...] = jnp.broadcast_to(total.astype(bf16)[None], out_ref.shape)


def turn_kernel(whole_ref, out_ref):
    whole = whole_ref[...].reshape(out_ref.shape[1], PADDED).astype(f32)
    turned = whole.T
    out_ref[:HEAD] = turned[:HEAD]
    out_ref[HEAD : 2 * HEAD] = turned[128 : 128 + HEAD]
    out_ref[2 * HEAD : 2 * HEAD + 48] = turned[HEAD:128]
    out_ref[2 * HEAD + 48 :] = turned[128 + HEAD : 3 * HEAD]


def final_kernel(rows_ref, gain_ref, keep_ref, core_ref, pair_ref, out_ref):
    values = rows_ref[...].astype(f32)
    inverse = lax.rsqrt(jnp.mean(values * values, axis=-1, keepdims=True) + epsilon)
    scaled = values * inverse
    normed_grad = keep_ref[...] + core_ref[...].astype(f32) + pair_ref[...].astype(f32)
    grad_scaled = normed_grad * gain_ref[...]
    mixed = jnp.mean(grad_scaled * scaled, axis=-1, keepdims=True)
    out_ref[...] = (inverse * (grad_scaled - scaled * mixed)).astype(bf16)


def vmem():
    return pl.BlockSpec(memory_space=pltpu.VMEM)


def smem():
    return pl.BlockSpec(memory_space=pltpu.SMEM)


def params(limit=SMALL):
    return pltpu.CompilerParams(vmem_limit_bytes=limit)


def pack_call(rows):
    return pl.pallas_call(
        pack_kernel,
        out_shape=jax.ShapeDtypeStruct((HEADS, LINES, 128), bf16),
        in_specs=[vmem()],
        out_specs=vmem(),
        compiler_params=params(),
    )(rows)


def permute_call(place, source, received):
    return pl.pallas_call(
        permute_kernel,
        out_shape=jax.ShapeDtypeStruct((RING, SLOTS, LINES, 128), bf16),
        in_specs=[smem(), smem(), vmem()],
        out_specs=vmem(),
        scratch_shapes=[pltpu.VMEM((HEADS * CHUNK, 128), f32), pltpu.VMEM((CHUNK, 128), f32)],
        compiler_params=params(),
    )(place, source, received)


def norm_call(rows, gain):
    return pl.pallas_call(
        norm_kernel,
        out_shape=jax.ShapeDtypeStruct(rows.shape, bf16),
        in_specs=[vmem(), vmem()],
        out_specs=vmem(),
        compiler_params=params(),
    )(rows, gain)


def gather_call(half, core):
    rows, width = 2 * half.shape[0], half.shape[1]
    piece = 256
    part = pl.BlockSpec((half.shape[0], piece), lambda n: (0, n))
    return pl.pallas_call(
        gather_kernel,
        grid=(width // piece,),
        out_shape=(
            jax.ShapeDtypeStruct((rows, width), bf16),
            jax.ShapeDtypeStruct((width, rows), bf16),
        ),
        in_specs=[part, part],
        out_specs=(
            pl.BlockSpec((rows, piece), lambda n: (0, n)),
            pl.BlockSpec((piece, rows), lambda n: (n, 0)),
        ),
        compiler_params=params(BIG),
    )(half, core)


def hbm():
    return pl.BlockSpec(memory_space=pl.ANY)


def kept(rows):
    return (
        ((RING, rows, 128), bf16),
        ((RING, rows, 128), bf16),
        ((RING, rows, SUPER), f32),
    )


def forward_call(place, normed, weights, windows):
    rows, width = normed.shape
    return pl.pallas_call(
        forward_kernel,
        out_shape=tuple(jax.ShapeDtypeStruct(*each) for each in kept(rows)),
        in_specs=[smem(), hbm(), hbm(), vmem()],
        out_specs=(hbm(),) * 3,
        scratch_shapes=[pltpu.VMEM(*each) for each in kept(rows)]
        + [
            pltpu.VMEM((rows, SUPER), f32),
            pltpu.VMEM((rows, width), bf16),
            pltpu.VMEM((RING, 16, 16, width), bf16),
            pltpu.SemaphoreType.DMA((RING + 1,)),
            pltpu.SemaphoreType.DMA((3,)),
        ],
        compiler_params=params(BIG),
    )(place, normed, weights, windows)


def head_call(turned, upstream, forward):
    width, rows = turned.shape
    return pl.pallas_call(
        head_kernel,
        out_shape=(
            jax.ShapeDtypeStruct((RING, rows, PADDED), bf16),
            jax.ShapeDtypeStruct((16, RING, width // 16, PADDED), bf16),
        ),
        in_specs=[hbm(), vmem()] + [hbm()] * 3,
        out_specs=(hbm(),) * 2,
        scratch_shapes=[pltpu.VMEM(*each) for each in kept(rows)]
        + [
            pltpu.VMEM((RING, rows, PADDED), bf16),
            pltpu.VMEM((width, rows), bf16),
            pltpu.VMEM((RING, rows, PADDED), bf16),
            pltpu.VMEM((RING, 16, width // 16, PADDED), bf16),
            pltpu.SemaphoreType.DMA((4,)),
            pltpu.SemaphoreType.DMA((RING + 1,)),
        ],
        compiler_params=params(BIG),
    )(turned, upstream, *forward)


def back_call(grads, weights, normed, half, dtype):
    rows, width = 2 * CHUNK, weights.shape[-1]
    piece = 256
    return pl.pallas_call(
        back_kernel,
        grid=(width // piece,),
        out_shape=(
            jax.ShapeDtypeStruct((rows, width), dtype),
            jax.ShapeDtypeStruct((1, width), f32),
        ),
        in_specs=[
            pl.BlockSpec((RING, rows, PADDED), lambda n: (0, half, 0)),
            pl.BlockSpec((16, RING, 16, piece), lambda n: (0, 0, 0, n)),
            pl.BlockSpec((rows, piece), lambda n: (half, n)),
        ],
        out_specs=(
            pl.BlockSpec((rows, piece), lambda n: (0, n)),
            pl.BlockSpec((1, piece), lambda n: (0, n)),
        ),
        compiler_params=params(BIG),
    )(grads, weights, normed)


def final_call(rows, gain, keep, from_core, from_pair):
    part = pl.BlockSpec(rows.shape, lambda i: (0, 0))
    return pl.pallas_call(
        final_kernel,
        grid=(1,),
        out_shape=jax.ShapeDtypeStruct(rows.shape, bf16),
        in_specs=[part, pl.BlockSpec(gain.shape, lambda i: (0, 0)), part, part, part],
        out_specs=part,
        compiler_params=params(BIG),
    )(rows, gain, keep, from_core, from_pair)


def spread_call(arrived):
    return pl.pallas_call(
        spread_kernel,
        out_shape=jax.ShapeDtypeStruct((16,) + arrived.shape[1:], bf16),
        in_specs=[vmem()],
        out_specs=vmem(),
        compiler_params=params(),
    )(arrived)


def turn_call(whole):
    width = whole.shape[0] * whole.shape[1]
    return pl.pallas_call(
        turn_kernel,
        grid=(2,),
        out_shape=jax.ShapeDtypeStruct((3 * HEAD, width), f32),
        in_specs=[pl.BlockSpec((8, width // 16, PADDED), lambda i: (i, 0, 0))],
        out_specs=pl.BlockSpec((3 * HEAD, width // 2), lambda i: (0, i)),
        compiler_params=params(BIG),
    )(whole)


def swap(x, axis):
    return lax.ppermute(x, axis, [(0, 1), (1, 0)])


def on_device(layer_input, grad_packed, source_row, window_id, w_qkv, gain):
    width = layer_input.shape[1]
    dp = lax.axis_index("y") * 4 + lax.axis_index("x")
    ring = lax.axis_index("zq")
    slot = lax.axis_index("zp") * 2 + lax.axis_index("core")
    place = jnp.stack([ring, slot]).astype(jnp.int32)
    gain_row = gain.reshape(1, width)

    own = norm_call(layer_input, gain_row)
    grad_rows, own = lax.optimization_barrier((grad_packed, own))
    packed = pack_call(grad_rows)
    flipped = jnp.swapaxes(w_qkv, 1, 2).reshape(3 * HEAD, width)
    block = jnp.where(dp < 5, dp, jnp.where(dp < 8, dp + 5, jnp.where(dp < 13, dp - 3, dp)))
    share = lax.dynamic_slice(flipped, (16 * jnp.minimum(block, 14), 0), (16, width))
    share = jnp.where(dp < 15, share, jnp.zeros_like(share))
    others = [lax.ppermute(share, "zq", [(i, (i + k) % RING) for i in range(RING)]) for k in (3, 2, 1)]
    others, packed = lax.optimization_barrier((others, packed))
    circle = jnp.concatenate([share] + others + [share] + others, axis=0)
    ordered = lax.dynamic_slice(circle, (16 * ((RING - ring) % RING), 0), (16 * RING, width))
    weights = lax.all_gather(ordered, ("y", "x"), axis=0, tiled=True)
    weights = weights.reshape(16, RING, 16, width)

    by_head = lax.all_to_all(packed, ("zq", "zp", "core"), split_axis=0, concat_axis=0)
    permuted = permute_call(place, source_row.reshape(-1), by_head)
    upstream = lax.all_to_all(permuted, "zq", split_axis=0, concat_axis=0)

    half = jnp.concatenate([own, swap(own, "zp")], axis=0)
    normed, turned = gather_call(half, swap(half, "core"))
    windows = window_id.reshape(32, 128).astype(f32)
    forward = forward_call(place, normed, weights, windows)
    grads, weight_part = head_call(turned, upstream, forward)

    arrived = lax.all_to_all(weight_part, ("y", "x"), split_axis=0, concat_axis=0)
    summed = jnp.sum(arrived.astype(f32), axis=0).astype(bf16)
    send, gain_send = back_call(grads, weights, normed, 1, bf16)
    keep, gain_keep = back_call(grads, weights, normed, 0, f32)
    gain_part = gain_send + gain_keep
    from_core = swap(send, "core")
    pair = (keep[CHUNK:] + from_core[CHUNK:].astype(f32)).astype(bf16)
    gain_part = gain_part + swap(gain_part, "core")
    gain_part = gain_part + swap(gain_part, "zp")
    beside = gain_part.reshape(width // 16, 16).astype(bf16)
    beside = jnp.broadcast_to(beside[None], (RING, width // 16, 16))
    message = jnp.concatenate([summed[..., : 3 * HEAD], beside], axis=2)
    from_pair = swap(pair, "zp")
    message, from_pair = lax.optimization_barrier((message, from_pair))
    arrived = lax.all_to_all(message, "zq", split_axis=0, concat_axis=0)
    copies = spread_call(arrived)
    whole = lax.all_to_all(copies, ("y", "x"), split_axis=0, concat_axis=0)
    grad_gain = jnp.sum(whole[:, :, 3 * HEAD :].astype(f32), axis=0).reshape(width) / gain
    grad_weight = jnp.swapaxes(turn_call(whole).reshape(3, HEAD, width), 1, 2)
    grad_input = final_call(layer_input, gain_row, keep, from_core, from_pair)
    return (grad_input, grad_weight, grad_gain)


def solution(mesh):
    fine = Mesh(mesh.devices.reshape(4, 4, 4, 2, 2), ("y", "x", "zq", "zp", "core"))
    dp, group = ("y", "x"), ("zq", "zp", "core")
    rows = P(dp + group, None)
    return jax.shard_map(
        on_device,
        mesh=fine,
        in_specs=(rows, rows, P(dp, None), P(dp, None), P(None, None, group), P()),
        out_specs=(rows, P(None, None, group), P()),
        check_vma=False,
    )
```

```python
import functools

import jax
import jax.numpy as jnp
from jax import lax
from jax.experimental import pallas as pl
from jax.experimental.pallas import tpu as pltpu
from jax.sharding import Mesh, PartitionSpec as P

HEAD = 80
HEADS = 16
SUPER = 128
CHUNK = 256
SLOTS = 4
RING = 4
LINES = 160
PADDED = 256
XOR_ORDER = (0, 2, 1, 3)
epsilon = 1e-06
bf16 = jnp.bfloat16
f32 = jnp.float32
NT = (((1,), (1,)), ((), ()))
TN = (((0,), (0,)), ((), ()))
NN = (((1,), (0,)), ((), ()))
BIG = 58 * 1024 * 1024
SMALL = 20 * 1024 * 1024


def dot(a, b, dims):
    return lax.dot_general(a, b, dims, preferred_element_type=f32)


def lanes(shape):
    return lax.broadcasted_iota(jnp.int32, shape, len(shape) - 1)


def roll(x, shift):
    shift = shift % x.shape[-1]
    return x if shift == 0 else pltpu.roll(x, shift, x.ndim - 1)


def pack(rows):
    top = jnp.where(lanes((128, 128)) < 64, rows[:128], roll(rows[128:], 64))
    group = lanes((32, 128)) // 16
    low = roll(rows[:32], -64)
    for k in range(1, 8):
        low = jnp.where(group == k, roll(rows[32 * k : 32 * k + 32], 16 * k - 64), low)
    return top, low


def unpack(top, low, place):
    at = lanes((128, 128))
    upper = roll(top, place)
    lower = roll(top, place - 64)
    tail = [roll(low, place + 64 - 16 * k) for k in range(8)]
    first = jnp.concatenate(tail[:4], axis=0)
    second = jnp.concatenate(tail[4:], axis=0)
    wide = (at >= place) & (at < place + 64)
    rest = (at >= place + 64) & (at < place + HEAD)
    one = jnp.where(wide, upper, jnp.where(rest, first, 0.0))
    two = jnp.where(wide, lower, jnp.where(rest, second, 0.0))
    return one, two


def pack_kernel(rows_ref, out_ref):
    for g in range(HEADS):
        start = (HEAD * g) // 128 * 128
        shift = HEAD * g - start
        size = 128 if shift + HEAD <= 128 else 256
        window = rows_ref[:, start : start + size].astype(f32)
        window = roll(window, -shift)[:, :128]
        top, low = pack(window)
        out_ref[g, :128, :] = top.astype(bf16)
        out_ref[g, 128:, :] = low.astype(bf16)


def permute_kernel(place_ref, source_ref, in_ref, out_ref, table, picked):
    slot = place_ref[1]
    for src in range(HEADS):
        one, two = unpack(
            in_ref[src, :128, :].astype(f32), in_ref[src, 128:, :].astype(f32), 0
        )
        table[CHUNK * src : CHUNK * src + 128, :] = one
        table[CHUNK * src + 128 : CHUNK * src + 256, :] = two
    for q in range(RING):
        for o, off in enumerate(XOR_ORDER):
            base = q * SLOTS * CHUNK + (slot ^ off) * CHUNK

            def step(i, carry):
                at = i * 128
                for u in range(128):
                    row = source_ref[base + at + u]
                    picked[pl.ds(at + u, 1), :] = table[pl.ds(row, 1), :]
                return carry

            lax.fori_loop(0, CHUNK // 128, step, 0)
            top, low = pack(picked[...])
            out_ref[q, o, :128, :] = top.astype(bf16)
            out_ref[q, o, 128:, :] = low.astype(bf16)


def norm_kernel(rows_ref, gain_ref, out_ref):
    values = rows_ref[...].astype(f32)
    inverse = lax.rsqrt(jnp.mean(values * values, axis=-1, keepdims=True) + epsilon)
    out_ref[...] = (values * inverse * gain_ref[...]).astype(bf16)


def shifted(shape, move):
    row = lax.broadcasted_iota(jnp.int32, shape, 0)
    return jnp.where(move(row, lanes(shape)), 1.0, 0.0).astype(bf16)


def gather_kernel(half_ref, core_ref, out_ref, turned_ref):
    for c, part in enumerate((half_ref, core_ref)):
        rows = slice(2 * CHUNK * c, 2 * CHUNK * c + 2 * CHUNK)
        out_ref[rows, :] = part[...]
        turned_ref[:, rows] = part[...].T


def front(x):
    return jnp.where(lanes(x.shape) < HEAD, x, 0.0).astype(bf16)


def blocks_of(total_rows):
    return [slice(SUPER * b, SUPER * b + SUPER) for b in range(total_rows // SUPER)]


def forward_kernel(
    place_ref, normed_hbm, w_hbm, window_ref, first_hbm, second_hbm, probs_hbm,
    first, second, probs, same, normed_ref, w_ref, in_sems, out_sems,
):
    ring, slot = place_ref[0], place_ref[1]
    scaling = HEAD ** (-0.5)
    total_rows, width = normed_ref.shape
    blocks = blocks_of(total_rows)
    copies = [pltpu.make_async_copy(normed_hbm, normed_ref, in_sems.at[RING])] + [
        pltpu.make_async_copy(w_hbm.at[:, h], w_ref.at[h], in_sems.at[h]) for h in range(RING)
    ]
    for copy in copies:
        copy.start()
    for b, r in enumerate(blocks):
        line = ring * 8 + (slot ^ XOR_ORDER[b // 2]) * 2 + b % 2
        labels = jnp.broadcast_to(window_ref[pl.ds(line, 1), :], (SUPER, SUPER))
        same[r, :] = jnp.where(labels == labels.T, 0.0, -1e30)
    for copy in copies[:2]:
        copy.wait()
    late = copies[2:]

    def project(h):
        w = w_ref[h].reshape(PADDED, width)
        low = dot(normed_ref[...], w, NT).astype(bf16)
        first[h] = low[:, :128]
        second[h] = low[:, 128:]

    def soften(h):
        scores = [dot(front(first[h, r, :]), second[h, r, :], NT) for r in blocks]
        for b, r in enumerate(blocks):
            masked = scores[b] * scaling + same[r, :]
            powers = jnp.exp(masked - jnp.max(masked, axis=-1, keepdims=True))
            probs[h, r, :] = powers * (1.0 / jnp.sum(powers, axis=-1, keepdims=True))

    copies = [
        pltpu.make_async_copy(src, dst, out_sems.at[i])
        for i, (src, dst) in enumerate(
            ((first, first_hbm), (second, second_hbm), (probs, probs_hbm))
        )
    ]
    project(0)
    for copy in late:
        copy.wait()
    for h in range(RING):
        if h + 1 < RING:
            project(h + 1)
        else:
            for copy in copies[:2]:
                copy.start()
        soften(h)
    copies[2].start()
    for copy in copies:
        copy.wait()


def head_kernel(
    turned_hbm, up_ref, first_hbm, second_hbm, probs_hbm, grad_hbm, weight_hbm,
    first, second, probs, upstream, turned_ref, grad_ref, weight_ref,
    in_sems, out_sems,
):
    scaling = HEAD ** (-0.5)
    width, total_rows = turned_ref.shape
    blocks = blocks_of(total_rows)
    copies = [
        pltpu.make_async_copy(src, dst, in_sems.at[i])
        for i, (src, dst) in enumerate(
            (
                (first_hbm, first), (second_hbm, second), (probs_hbm, probs),
                (turned_hbm, turned_ref),
            )
        )
    ]
    for copy in copies:
        copy.start()
    to_wide = shifted(
        (128, PADDED),
        lambda r, c: ((c >= 80) & (c < 128) & (r % 64 == c - 80))
        | ((c >= 208) & (c < 224) & (r % 64 == c - 160)),
    )
    to_rest = shifted(
        (128, PADDED), lambda r, c: (c >= 224) & (c < 240) & (r % 16 == c - 224)
    )
    row = lax.broadcasted_iota(jnp.int32, (CHUNK, 128), 0)
    keep_wide = row // 128 == lanes((CHUNK, 128)) // 64
    keep_rest = row // 32 == lanes((CHUNK, 128)) // 16

    def spread(h):
        for c in range(SLOTS):
            top, low = up_ref[h, c, :128, :], up_ref[h, c, 128:, :]
            wide = jnp.where(keep_wide, jnp.concatenate([top] * 2, axis=0), 0.0)
            rest = jnp.where(keep_rest, jnp.concatenate([low] * 8, axis=0), 0.0)
            both = dot(wide.astype(bf16), to_wide, NN) + dot(rest.astype(bf16), to_rest, NN)
            upstream[h, CHUNK * c : CHUNK * c + CHUNK, :] = both.astype(bf16)

    def attend(h):
        grad_probs = [
            dot(upstream[h, r, :128], first[h, r, :], NT)
            + dot(upstream[h, r, 128:], second[h, r, :], NT)
            for r in blocks
        ]
        grad_scores, probs_low = [], []
        for b, r in enumerate(blocks):
            prob = probs[h, r, :]
            row_dot = jnp.sum(prob * grad_probs[b], axis=-1, keepdims=True)
            grad_scores.append((prob * (grad_probs[b] - row_dot)).astype(bf16))
            probs_low.append(prob.astype(bf16))
        for b, r in enumerate(blocks):
            grad_query = dot(grad_scores[b], front(second[h, r, :]), NN)
            grad_key = dot(grad_scores[b], front(first[h, r, :]), TN)
            grad_value = dot(probs_low[b], upstream[h, r, :], TN)
            grad_ref[h, r, :128] = (grad_query * scaling + grad_value[:, :128]).astype(bf16)
            grad_ref[h, r, 128:] = (grad_key * scaling + grad_value[:, 128:]).astype(bf16)

    def weigh(h):
        part = dot(turned_ref[...], grad_ref[h], NN).astype(bf16)
        weight_ref[h] = part.reshape(16, width // 16, PADDED)

    for h in range(RING):
        spread(h)
    for copy in copies[:3]:
        copy.wait()
    out_copies = [pltpu.make_async_copy(grad_ref, grad_hbm, out_sems.at[RING])] + [
        pltpu.make_async_copy(weight_ref.at[h], weight_hbm.at[:, h], out_sems.at[h])
        for h in range(RING)
    ]
    attend(0)
    copies[3].wait()
    for h in range(RING):
        if h + 1 < RING:
            attend(h + 1)
        else:
            for copy in out_copies[:RING]:
                copy.start()
        weigh(h)
    out_copies[RING].start()
    for copy in out_copies:
        copy.wait()


def back_kernel(grad_ref, w_ref, normed_ref, out_ref, gain_ref):
    parts = [w_ref[:, h].reshape(PADDED, w_ref.shape[-1]) for h in range(RING)]
    grads = jnp.concatenate([grad_ref[h] for h in range(RING)], axis=1)
    total = dot(grads, jnp.concatenate(parts, axis=0), NN)
    out_ref[...] = total.astype(out_ref.dtype)
    gain_ref[...] = jnp.sum(total * normed_ref[...].astype(f32), axis=0, keepdims=True)


def spread_kernel(in_ref, out_ref):
    total = in_ref[0].astype(f32)
    for q in range(1, RING):
        total += in_ref[q].astype(f32)
    out_ref[...] = jnp.broadcast_to(total.astype(bf16)[None], out_ref.shape)


def turn_kernel(whole_ref, out_ref):
    whole = whole_ref[...].reshape(out_ref.shape[1], PADDED).astype(f32)
    turned = whole.T
    out_ref[:HEAD] = turned[:HEAD]
    out_ref[HEAD : 2 * HEAD] = turned[128 : 128 + HEAD]
    out_ref[2 * HEAD : 2 * HEAD + 48] = turned[HEAD:128]
    out_ref[2 * HEAD + 48 :] = turned[128 + HEAD : 3 * HEAD]


def final_kernel(rows_ref, gain_ref, keep_ref, core_ref, pair_ref, out_ref):
    values = rows_ref[...].astype(f32)
    inverse = lax.rsqrt(jnp.mean(values * values, axis=-1, keepdims=True) + epsilon)
    scaled = values * inverse
    normed_grad = keep_ref[...] + core_ref[...].astype(f32) + pair_ref[...].astype(f32)
    grad_scaled = normed_grad * gain_ref[...]
    mixed = jnp.mean(grad_scaled * scaled, axis=-1, keepdims=True)
    out_ref[...] = (inverse * (grad_scaled - scaled * mixed)).astype(bf16)


def vmem():
    return pl.BlockSpec(memory_space=pltpu.VMEM)


def smem():
    return pl.BlockSpec(memory_space=pltpu.SMEM)


def params(limit=SMALL):
    return pltpu.CompilerParams(vmem_limit_bytes=limit)


def pack_call(rows):
    return pl.pallas_call(
        pack_kernel,
        out_shape=jax.ShapeDtypeStruct((HEADS, LINES, 128), bf16),
        in_specs=[vmem()],
        out_specs=vmem(),
        compiler_params=params(),
    )(rows)


def permute_call(place, source, received):
    return pl.pallas_call(
        permute_kernel,
        out_shape=jax.ShapeDtypeStruct((RING, SLOTS, LINES, 128), bf16),
        in_specs=[smem(), smem(), vmem()],
        out_specs=vmem(),
        scratch_shapes=[pltpu.VMEM((HEADS * CHUNK, 128), f32), pltpu.VMEM((CHUNK, 128), f32)],
        compiler_params=params(),
    )(place, source, received)


def norm_call(rows, gain):
    return pl.pallas_call(
        norm_kernel,
        out_shape=jax.ShapeDtypeStruct(rows.shape, bf16),
        in_specs=[vmem(), vmem()],
        out_specs=vmem(),
        compiler_params=params(),
    )(rows, gain)


def gather_call(half, core):
    rows, width = 2 * half.shape[0], half.shape[1]
    return pl.pallas_call(
        gather_kernel,
        out_shape=(
            jax.ShapeDtypeStruct((rows, width), bf16),
            jax.ShapeDtypeStruct((width, rows), bf16),
        ),
        in_specs=[vmem(), vmem()],
        out_specs=(vmem(), vmem()),
        compiler_params=params(BIG),
    )(half, core)


def hbm():
    return pl.BlockSpec(memory_space=pl.ANY)


def kept(rows):
    return (
        ((RING, rows, 128), bf16),
        ((RING, rows, 128), bf16),
        ((RING, rows, SUPER), f32),
    )


def forward_call(place, normed, weights, windows):
    rows, width = normed.shape
    return pl.pallas_call(
        forward_kernel,
        out_shape=tuple(jax.ShapeDtypeStruct(*each) for each in kept(rows)),
        in_specs=[smem(), hbm(), hbm(), vmem()],
        out_specs=(hbm(),) * 3,
        scratch_shapes=[pltpu.VMEM(*each) for each in kept(rows)]
        + [
            pltpu.VMEM((rows, SUPER), f32),
            pltpu.VMEM((rows, width), bf16),
            pltpu.VMEM((RING, 16, 16, width), bf16),
            pltpu.SemaphoreType.DMA((RING + 1,)),
            pltpu.SemaphoreType.DMA((3,)),
        ],
        compiler_params=params(BIG),
    )(place, normed, weights, windows)


def head_call(turned, upstream, forward):
    width, rows = turned.shape
    return pl.pallas_call(
        head_kernel,
        out_shape=(
            jax.ShapeDtypeStruct((RING, rows, PADDED), bf16),
            jax.ShapeDtypeStruct((16, RING, width // 16, PADDED), bf16),
        ),
        in_specs=[hbm(), vmem()] + [hbm()] * 3,
        out_specs=(hbm(),) * 2,
        scratch_shapes=[pltpu.VMEM(*each) for each in kept(rows)]
        + [
            pltpu.VMEM((RING, rows, PADDED), bf16),
            pltpu.VMEM((width, rows), bf16),
            pltpu.VMEM((RING, rows, PADDED), bf16),
            pltpu.VMEM((RING, 16, width // 16, PADDED), bf16),
            pltpu.SemaphoreType.DMA((4,)),
            pltpu.SemaphoreType.DMA((RING + 1,)),
        ],
        compiler_params=params(BIG),
    )(turned, upstream, *forward)


def back_call(grads, weights, normed, half, dtype):
    rows, width = 2 * CHUNK, weights.shape[-1]
    piece = 256
    return pl.pallas_call(
        back_kernel,
        grid=(width // piece,),
        out_shape=(
            jax.ShapeDtypeStruct((rows, width), dtype),
            jax.ShapeDtypeStruct((1, width), f32),
        ),
        in_specs=[
            pl.BlockSpec((RING, rows, PADDED), lambda n: (0, half, 0)),
            pl.BlockSpec((16, RING, 16, piece), lambda n: (0, 0, 0, n)),
            pl.BlockSpec((rows, piece), lambda n: (half, n)),
        ],
        out_specs=(
            pl.BlockSpec((rows, piece), lambda n: (0, n)),
            pl.BlockSpec((1, piece), lambda n: (0, n)),
        ),
        compiler_params=params(BIG),
    )(grads, weights, normed)


def final_call(rows, gain, keep, from_core, from_pair):
    part = pl.BlockSpec(rows.shape, lambda i: (0, 0))
    return pl.pallas_call(
        final_kernel,
        grid=(1,),
        out_shape=jax.ShapeDtypeStruct(rows.shape, bf16),
        in_specs=[part, pl.BlockSpec(gain.shape, lambda i: (0, 0)), part, part, part],
        out_specs=part,
        compiler_params=params(BIG),
    )(rows, gain, keep, from_core, from_pair)


def spread_call(arrived):
    return pl.pallas_call(
        spread_kernel,
        out_shape=jax.ShapeDtypeStruct((16,) + arrived.shape[1:], bf16),
        in_specs=[vmem()],
        out_specs=vmem(),
        compiler_params=params(),
    )(arrived)


def turn_call(whole):
    width = whole.shape[0] * whole.shape[1]
    return pl.pallas_call(
        turn_kernel,
        grid=(2,),
        out_shape=jax.ShapeDtypeStruct((3 * HEAD, width), f32),
        in_specs=[pl.BlockSpec((8, width // 16, PADDED), lambda i: (i, 0, 0))],
        out_specs=pl.BlockSpec((3 * HEAD, width // 2), lambda i: (0, i)),
        compiler_params=params(BIG),
    )(whole)


def swap(x, axis):
    return lax.ppermute(x, axis, [(0, 1), (1, 0)])


def on_device(layer_input, grad_packed, source_row, window_id, w_qkv, gain):
    width = layer_input.shape[1]
    dp = lax.axis_index("y") * 4 + lax.axis_index("x")
    ring = lax.axis_index("zq")
    slot = lax.axis_index("zp") * 2 + lax.axis_index("core")
    place = jnp.stack([ring, slot]).astype(jnp.int32)
    gain_row = gain.reshape(1, width)

    own = norm_call(layer_input, gain_row)
    grad_rows, own = lax.optimization_barrier((grad_packed, own))
    packed = pack_call(grad_rows)
    flipped = jnp.swapaxes(w_qkv, 1, 2).reshape(3 * HEAD, width)
    block = jnp.where(dp < 5, dp, jnp.where(dp < 8, dp + 5, jnp.where(dp < 13, dp - 3, dp)))
    share = lax.dynamic_slice(flipped, (16 * jnp.minimum(block, 14), 0), (16, width))
    share = jnp.where(dp < 15, share, jnp.zeros_like(share))
    others = [lax.ppermute(share, "zq", [(i, (i + k) % RING) for i in range(RING)]) for k in (3, 2, 1)]
    others, packed = lax.optimization_barrier((others, packed))
    circle = jnp.concatenate([share] + others + [share] + others, axis=0)
    ordered = lax.dynamic_slice(circle, (16 * ((RING - ring) % RING), 0), (16 * RING, width))
    weights = lax.all_gather(ordered, ("y", "x"), axis=0, tiled=True)
    weights = weights.reshape(16, RING, 16, width)

    by_head = lax.all_to_all(packed, ("zq", "zp", "core"), split_axis=0, concat_axis=0)
    permuted = permute_call(place, source_row.reshape(-1), by_head)
    upstream = lax.all_to_all(permuted, "zq", split_axis=0, concat_axis=0)

    half = jnp.concatenate([own, swap(own, "zp")], axis=0)
    normed, turned = gather_call(half, swap(half, "core"))
    windows = window_id.reshape(32, 128).astype(f32)
    forward = forward_call(place, normed, weights, windows)
    grads, weight_part = head_call(turned, upstream, forward)

    arrived = lax.all_to_all(weight_part, ("y", "x"), split_axis=0, concat_axis=0)
    summed = jnp.sum(arrived.astype(f32), axis=0).astype(bf16)
    send, gain_send = back_call(grads, weights, normed, 1, bf16)
    keep, gain_keep = back_call(grads, weights, normed, 0, f32)
    gain_part = gain_send + gain_keep
    from_core = swap(send, "core")
    pair = (keep[CHUNK:] + from_core[CHUNK:].astype(f32)).astype(bf16)
    gain_part = gain_part + swap(gain_part, "core")
    gain_part = gain_part + swap(gain_part, "zp")
    beside = gain_part.reshape(width // 16, 16).astype(bf16)
    beside = jnp.broadcast_to(beside[None], (RING, width // 16, 16))
    message = jnp.concatenate([summed[..., : 3 * HEAD], beside], axis=2)
    from_pair = swap(pair, "zp")
    message, from_pair = lax.optimization_barrier((message, from_pair))
    arrived = lax.all_to_all(message, "zq", split_axis=0, concat_axis=0)
    copies = spread_call(arrived)
    whole = lax.all_to_all(copies, ("y", "x"), split_axis=0, concat_axis=0)
    grad_gain = jnp.sum(whole[:, :, 3 * HEAD :].astype(f32), axis=0).reshape(width) / gain
    grad_weight = jnp.swapaxes(turn_call(whole).reshape(3, HEAD, width), 1, 2)
    grad_input = final_call(layer_input, gain_row, keep, from_core, from_pair)
    return (grad_input, grad_weight, grad_gain)


def solution(mesh):
    fine = Mesh(mesh.devices.reshape(4, 4, 4, 2, 2), ("y", "x", "zq", "zp", "core"))
    dp, group = ("y", "x"), ("zq", "zp", "core")
    rows = P(dp + group, None)
    return jax.shard_map(
        on_device,
        mesh=fine,
        in_specs=(rows, rows, P(dp, None), P(dp, None), P(None, None, group), P()),
        out_specs=(rows, P(None, None, group), P()),
        check_vma=False,
    )
```
